128 devices in a mesh: dp: 8 (over z, core), seq: 16 (over y, x).
Axes of the slice: x: 4, y: 4, z: 4, core: 2. Of those that a mesh axis runs over, the one named last changes fastest.
Arguments:
- inputs: bfloat16 [16384, 768], P(('dp', 'seq')), may hold values from -24 to 24
- gain_attn: bfloat16 [768], P(('dp', 'seq')), may hold values from 0.5 to 1.5
- w_query: bfloat16 [768, 768], P(('dp', 'seq')), may hold values from -0.21875 to 0.21875
- w_key: bfloat16 [768, 768], P(('dp', 'seq')), may hold values from -0.21875 to 0.21875
- w_value: bfloat16 [768, 768], P(('dp', 'seq')), may hold values from -0.21875 to 0.21875
- w_output: bfloat16 [768, 768], P(('dp', 'seq')), may hold values from -6 to 6
- gain_ffn: bfloat16 [768], P(('dp', 'seq')), may hold values from 0.5 to 1.5
- router: bfloat16 [768, 32], P(('dp', 'seq')), may hold values from -0.109375 to 0.109375
- expert_in: bfloat16 [32, 768, 3072], P('seq', None, 'dp'), may hold values from -0.21875 to 0.21875
- expert_out: bfloat16 [32, 3072, 768], P('seq', 'dp'), may hold values from -6 to 6
- expert_index: int32 [16384], P(('dp', 'seq')), may hold values from 0 to 31, as said below
- slot_index: int32 [16384], P(('dp', 'seq')), may hold values from 0 to 4, as said below
- segment_ids: int32 [16384], P(('dp', 'seq')), may hold values from 0 to 2, as said below
- cotangent: bfloat16 [16384, 768], P(('dp', 'seq')), may hold values from -6 to 6
Outputs:
- outputs: bfloat16 [16384, 768], P(('dp', 'seq'))
- d_inputs: float32 [16384, 768], P(('dp', 'seq'))
- d_gain_attn: float32 [768], P(('dp', 'seq'))
- d_w_query: float32 [768, 768], P(('dp', 'seq'))
- d_w_key: float32 [768, 768], P(('dp', 'seq'))
- d_w_value: float32 [768, 768], P(('dp', 'seq'))
- d_w_output: float32 [768, 768], P(('dp', 'seq'))
- d_gain_ffn: float32 [768], P(('dp', 'seq'))
- d_router: float32 [768, 32], P(('dp', 'seq'))
- d_expert_in: float32 [32, 768, 3072], P('seq', None, 'dp')
- d_expert_out: float32 [32, 3072, 768], P('seq', 'dp')
The draws below stay inside these ranges and needn't reach their ends.
Inputs may be any that keep to these rules, and one draw needn't show every extreme that they name: `expert_index`: among the tokens of one device no expert is named by more than 5 tokens, and in every draw one expert is named by exactly 5 tokens of every device. `slot_index`: tokens of one device that name the same expert have different slot numbers. `segment_ids`: each sequence of 2048 tokens holds three contiguous documents numbered 0, 1, 2 in order, each of 192 tokens or more; one of the three, at a place that varies from sequence to sequence, holds 1152 tokens or more. Document edges fall at any token, independently of device boundaries.
All inputs are finite; a program needn't handle non-finite values.
Results may differ from the reference program's by a relative error of at most 0.025.
Values may be sent and summed in bfloat16 or wider, within the bound.
No kernel may reach another device: no remote copies, remote signals or barrier semaphores. Data moves between devices by JAX's collectives and lax.ppermute only.
A program may use at most 128 MiB of HBM per device.

```python
import math
import jax
import jax.numpy as jnp
from jax import lax

D = 768
HEADS = 12
FF = 3072
TOK_DEV = 128
DOC_MIN = 192
HEAD_DIM = 64
EXPERTS = 32
CAP = 5
LENGTH = 2048
SEQS = 8
TOKENS = 16384


def routing(key):
    blocks = TOKENS // TOK_DEV
    slots_all = EXPERTS * CAP
    full_expert = jax.random.randint(jax.random.fold_in(key, 101), (), 0, EXPERTS)

    def one_block(block_key):
        ordering = jax.random.permutation(block_key, slots_all)
        others = (ordering // CAP != full_expert).astype(jnp.int32)
        ordering = ordering[jnp.argsort(others, stable=True)]
        picked = ordering[:TOK_DEV]
        return picked[jax.random.permutation(jax.random.fold_in(block_key, 7), TOK_DEV)]
    picked = jax.vmap(one_block)(jax.random.split(jax.random.fold_in(key, 102), blocks))
    return picked.reshape(TOKENS).astype(jnp.int32)


def draw_expert_index(key, part):
    return (routing(key) // CAP).astype(jnp.int32)


def draw_slot_index(key, part):
    return (routing(key) % CAP).astype(jnp.int32)


def draw_segment_ids(key, part):
    key = jax.random.fold_in(key, 3)
    long_key, short_key, place_key = jax.random.split(key, 3)
    long_len = jax.random.randint(long_key, (SEQS,), LENGTH // 2 + TOK_DEV, LENGTH - 2 * DOC_MIN + 1).astype(jnp.int32)
    remainder = (LENGTH - long_len).astype(jnp.int32)
    first_short = jax.random.randint(short_key, (SEQS,), DOC_MIN, remainder - DOC_MIN + 1).astype(jnp.int32)
    second_short = remainder - first_short
    long_place = jax.random.randint(place_key, (SEQS,), 0, 3).astype(jnp.int32)
    first_len = jnp.where(long_place == 0, long_len, first_short)
    second_len = jnp.where(long_place == 1, long_len, jnp.where(long_place == 0, first_short, second_short))
    edge_one = first_len[:, None]
    edge_two = (first_len + second_len)[:, None]
    positions = jnp.arange(LENGTH, dtype=jnp.int32)[None, :]
    labels = (positions >= edge_one).astype(jnp.int32) + (positions >= edge_two).astype(jnp.int32)
    return labels.reshape(TOKENS).astype(jnp.int32)


def raised(values, rng, source, target, shards_of, factor):
    def block_of(position):
        return (jnp.arange(values.shape[position]) // (values.shape[position] // shards_of)).reshape((-1,) + (1,) * (values.ndim - 1 - position))

    first = jax.random.permutation(rng, shards_of)[block_of(target)]
    other_side = (block_of(target) + shards_of // 2) % shards_of
    return jnp.where((block_of(source) == first) | (block_of(source) == other_side), factor * values, values)


def steps_of(rng, extent, shards, least, top_value):
    def one(position, shards_of):
        steps = jax.random.uniform(jax.random.fold_in(jax.random.fold_in(rng, 6), position), (shards_of,), jnp.float32, least / len(shards), top_value / len(shards))
        return jnp.repeat(jnp.exp(steps), extent[position] // shards_of).reshape((-1,) + (1,) * (len(extent) - position - 1))

    factor_of = one(*shards[0])
    for cut in shards[1:]:
        factor_of = factor_of * one(*cut)
    return factor_of


def scatter_about(own_key, extent, spread, bound, cuts=(), held_as=jnp.bfloat16):
    values = jax.random.normal(own_key, extent, jnp.float32) * spread
    if len(cuts) > 0:
        values = steps_of(own_key, extent, cuts, -0.22, 0.18) * values
    return jnp.clip(values, min=-bound, max=bound).astype(held_as)


def gaussian_with(own_key, shape, spread, limit, cuts, heavy, kind=jnp.bfloat16):
    values = spread * jax.random.normal(own_key, shape, jnp.float32)
    if cuts:
        values = values * steps_of(own_key, shape, cuts, -0.22, 0.18)
    return jnp.clip(raised(values, jax.random.fold_in(own_key, 3), *heavy), -limit, limit).astype(kind)


def setup_inputs(seed: int = 0) -> dict:
    splits = jax.random.split(jax.random.key(seed), 15)
    inputs = gaussian_with(splits[0], (TOKENS, D), 1.0, 24.0, ((0, 128),), (0, 1, 128, 5.5))
    gain_attn = jnp.clip(1.0 + 0.1 * jax.random.normal(splits[1], (D,), jnp.float32), 0.5, 1.5).astype(jnp.bfloat16)
    w_query = scatter_about(splits[2], (D, D), D ** -0.5, 0.21875, ((0, 128),))
    w_key = scatter_about(splits[3], (D, D), D ** -0.5, 0.21875, ((0, 128),))
    w_value = scatter_about(splits[4], (D, D), D ** -0.5, 0.21875, ((0, 128),))
    w_output = scatter_about(splits[5], (D, D), (max(1, 4 * D // LENGTH)) ** -0.5, 6.0, ((0, 128),))
    gain_ffn = jnp.clip(1.0 + 0.1 * jax.random.normal(splits[6], (D,), jnp.float32), 0.5, 1.5).astype(jnp.bfloat16)
    router = scatter_about(splits[7], (D, EXPERTS), (4 * D) ** -0.5, 0.109375, ((0, 128),))
    expert_in = scatter_about(splits[8], (EXPERTS, D, FF), D ** -0.5, 0.21875, ((0, 16), (2, 8)))
    expert_out = scatter_about(splits[9], (EXPERTS, FF, D), (max(1, FF // (4 * EXPERTS * EXPERTS))) ** -0.5, 6.0, ((0, 16), (1, 8)))
    expert_index = draw_expert_index(jax.random.fold_in(splits[14], 71), 0)
    slot_index = draw_slot_index(jax.random.fold_in(splits[14], 71), 0)
    segment_ids = draw_segment_ids(jax.random.fold_in(splits[14], 71), 0)
    cotangent = scatter_about(splits[13], (TOKENS, D), 1.0, 6.0, ((0, 128),))
    return dict(inputs=inputs, gain_attn=gain_attn, w_query=w_query, w_key=w_key, w_value=w_value, w_output=w_output, gain_ffn=gain_ffn, router=router, expert_in=expert_in, expert_out=expert_out, expert_index=expert_index, slot_index=slot_index, segment_ids=segment_ids, cotangent=cotangent)


EPSILON = 1e-06

@jax.custom_vjp
def low(v):
    return lax.optimization_barrier(v.astype(jnp.bfloat16)).astype(jnp.float32)

@jax.custom_vjp
def low_back(v):
    return v

def low_keep(v):
    return (low(v), None)

def low_pass(kept, grad):
    return (grad,)

def back_keep(v):
    return (v, None)

def back_low(kept, grad):
    return (low(grad),)
low.defvjp(low_keep, low_pass)
low_back.defvjp(back_keep, back_low)

def normalize(values, gain_vec):
    return values * lax.rsqrt(lax.optimization_barrier(jnp.mean(values * values, axis=-1, keepdims=True)) + EPSILON) * gain_vec

def attend(pieces):
    queries, keys_all, values_all, segments = pieces
    factor = HEAD_DIM ** (-0.5)
    span = math.gcd(LENGTH, 512)

    def one_block(block_pieces):
        query_part, seg_part = block_pieces
        scores = low_back(jnp.einsum('qhd,khd->hqk', query_part, keys_all, precision=lax.Precision.HIGHEST) * factor)
        allowed = seg_part[:, None] == segments[None, :]
        weights_low = low(jax.nn.softmax(jnp.where(allowed[None], scores, -1e+30), axis=-1))
        return jnp.einsum('hqk,khd->qhd', weights_low, values_all, precision=lax.Precision.HIGHEST)
    result = lax.map(jax.checkpoint(one_block), (queries.reshape(LENGTH // span, span, HEADS, HEAD_DIM), segments.reshape(LENGTH // span, span)))
    return result.reshape(LENGTH, D)

def expert_apply(pieces):
    rows_in, weight_in, weight_out = pieces
    before_act = low_back(jnp.dot(rows_in, weight_in, precision=lax.Precision.HIGHEST))
    activated = low(jax.nn.gelu(before_act))
    return low_back(low(jnp.dot(activated, weight_out, precision=lax.Precision.HIGHEST)))

def forward(inputs, gain_attn, w_query, w_key, w_value, w_output, gain_ffn, router, expert_in, expert_out, expert_index, slot_index, segment_ids):
    highest = lax.Precision.HIGHEST
    normed_one = low(normalize(inputs, gain_attn))
    queries = low_back(low(jnp.dot(normed_one, w_query, precision=highest)))
    keys_all = low_back(low(jnp.dot(normed_one, w_key, precision=highest)))
    values_all = low_back(low(jnp.dot(normed_one, w_value, precision=highest)))
    head_shape = (SEQS, LENGTH, HEADS, HEAD_DIM)
    attended = lax.map(jax.checkpoint(attend), (queries.reshape(head_shape), keys_all.reshape(head_shape), values_all.reshape(head_shape), segment_ids.reshape(SEQS, LENGTH)))
    mixed = low_back(low(attended.reshape(TOKENS, D)))
    hidden_one = inputs + low_back(jnp.dot(mixed, w_output, precision=highest))
    normed_two = low(normalize(hidden_one, gain_ffn))
    logits = low_back(jnp.dot(normed_two, router, precision=highest))
    router_probs = jax.nn.softmax(logits, axis=-1)
    chosen = (expert_index[:, None] == jnp.arange(EXPERTS).astype(jnp.int32)[None, :]).astype(router_probs.dtype)
    gate_value = lax.optimization_barrier(jnp.sum(router_probs * chosen, axis=-1))
    devices_all = TOKENS // TOK_DEV
    source = (jnp.arange(TOKENS) // TOK_DEV).astype(jnp.int32)
    slot_place = expert_index * (devices_all * CAP) + source * CAP + slot_index
    buffer = jnp.zeros((EXPERTS * devices_all * CAP, D), normed_two.dtype).at[slot_place].set(normed_two)
    buffer = low_back(buffer).reshape(EXPERTS, devices_all * CAP, D)
    returned = lax.map(jax.checkpoint(expert_apply), (buffer, expert_in, expert_out)).reshape(EXPERTS * devices_all * CAP, D)
    return hidden_one + gate_value[:, None] * returned[slot_place]

def reference(inputs, gain_attn, w_query, w_key, w_value, w_output, gain_ffn, router, expert_in, expert_out, expert_index, slot_index, segment_ids, cotangent):
    floats = tuple((array.astype(jnp.float32) for array in (inputs, gain_attn, w_query, w_key, w_value, w_output, gain_ffn, router, expert_in, expert_out)))

    def closed(*params):
        return forward(*params, expert_index, slot_index, segment_ids)
    result, pullback = jax.vjp(closed, *floats)
    grads = pullback(cotangent.astype(jnp.float32))
    return (result.astype(jnp.bfloat16), grads[0], grads[1], grads[2], grads[3], grads[4], grads[5], grads[6], grads[7], grads[8], grads[9])
```

```python
import jax
import jax.numpy as jnp
import numpy as np
from jax import lax
from jax.sharding import Mesh
from jax.sharding import PartitionSpec as P

HEADS = 12
GROUPS = 4
CAPACITY = 5
EPSILON = 1e-06
ALL = ("z", "core", "y", "x")
SIZES = (4, 2, 4, 4)

f32 = jnp.float32
bf16 = jnp.bfloat16

PLACES = np.arange(128).reshape(SIZES)
HEAD_GROUPS = [[int(i) for i in PLACES[z, 0, k, :]] for z in range(4) for k in range(4)] + [
    [int(i) for i in PLACES[z, 1, :, k]] for z in range(4) for k in range(4)
]
QUERY_GROUPS = [[int(i) for i in PLACES[z, 0, :, k]] for z in range(4) for k in range(4)] + [
    [int(i) for i in PLACES[z, 1, k, :]] for z in range(4) for k in range(4)
]


def shifted(values, groups, step):
    pairs = [(g[i], g[(i + step) % len(g)]) for g in groups for i in range(len(g))]
    return lax.ppermute(values, ALL, pairs)


def swap_rows(values, groups=None):
    return lax.all_to_all(
        values, ALL, split_axis=0, concat_axis=0, tiled=True, axis_index_groups=groups
    )


def matmul(a, b):
    return jnp.dot(a, b, preferred_element_type=f32)


def matmul_t(a, b):
    return lax.dot_general(a, b, (((1,), (1,)), ((), ())), preferred_element_type=f32)


def matmul_tn(a, b):
    return lax.dot_general(a, b, (((0,), (0,)), ((), ())), preferred_element_type=f32)


def inverse_rms(values):
    return lax.rsqrt(jnp.mean(values * values, axis=-1, keepdims=True) + EPSILON)


def norm_back(values, scale, grad, gain_vec):
    u = grad * gain_vec
    return scale * u - values * (scale * scale * scale) * jnp.mean(
        u * values, axis=-1, keepdims=True
    )


def body(
    inputs,
    gain_attn,
    w_query,
    w_key,
    w_value,
    w_output,
    gain_ffn,
    router,
    expert_in,
    expert_out,
    expert_index,
    slot_index,
    segment_ids,
    cotangent,
):
    tok_rows, width = inputs.shape
    head_dim = width // HEADS
    factor = head_dim ** (-0.5)
    cols = width // GROUPS
    heads_here = HEADS // GROUPS
    experts_all = router.shape[1]
    rows_held = w_query.shape[0]
    local_experts = expert_in.shape[0]
    hidden = expert_in.shape[2]
    block_rows = GROUPS * tok_rows

    core = lax.axis_index("core")
    y_place = lax.axis_index("y")
    x_place = lax.axis_index("x")
    dp_place = lax.axis_index("z") * 2 + core
    head_place = jnp.where(core == 0, x_place, y_place)
    query_place = jnp.where(core == 0, y_place, x_place)
    ring = jnp.arange(GROUPS, dtype=jnp.int32)

    input_parts = jnp.stack(
        [inputs] + [shifted(inputs, HEAD_GROUPS, step) for step in range(1, GROUPS)]
    )
    output_mat = lax.all_gather(w_output, ALL, axis=0, tiled=True)

    three = jnp.stack((w_query, w_key, w_value), axis=1).reshape(rows_held, 3, GROUPS, cols)
    three = jnp.transpose(three, (2, 0, 1, 3)).reshape(GROUPS, rows_held, 3 * cols)
    extra = jnp.concatenate((gain_attn[:, None], gain_ffn[:, None], router), axis=1)
    padding = 64 - extra.shape[1]
    extra = jnp.pad(extra, ((0, 0), (0, padding)))
    packed = jnp.concatenate(
        (three, jnp.broadcast_to(extra[None], (GROUPS,) + extra.shape)), axis=2
    )
    seg_row = jnp.pad(segment_ids.astype(bf16), (0, packed.shape[2] - tok_rows))
    seg_rows = jnp.stack((seg_row, jnp.zeros_like(seg_row)))
    packed = jnp.concatenate(
        (packed, jnp.broadcast_to(seg_rows[None], (GROUPS,) + seg_rows.shape)), axis=1
    )
    row_count = packed.shape[1]
    by_core = jnp.stack(
        (
            jnp.broadcast_to(packed[None, :], (GROUPS,) + packed.shape),
            jnp.broadcast_to(packed[:, None], (GROUPS,) + packed.shape),
        )
    )
    send = jnp.broadcast_to(by_core[None], (SIZES[0],) + by_core.shape)
    held = swap_rows(send.reshape(128, row_count, packed.shape[2]))
    weights = held[:, :rows_held, :].reshape(width, packed.shape[2])
    qkv_mat = weights[:, : 3 * cols]
    gain_one = weights[:, 3 * cols].astype(f32)
    gain_two = weights[:, 3 * cols + 1].astype(f32)
    router_mat = weights[:, 3 * cols + 2 : 3 * cols + 2 + experts_all]
    segs = lax.dynamic_slice_in_dim(held[:, rows_held, :tok_rows], dp_place * 16, 16, axis=0)
    segs = segs.reshape(GROUPS, GROUPS, tok_rows)
    segs = jnp.where(core == 0, segs, jnp.transpose(segs, (1, 0, 2)))
    key_segs = jnp.take(segs, (query_place - ring) % GROUPS, axis=0)
    query_seg = key_segs[0].reshape(block_rows)
    key_segs = key_segs.reshape(GROUPS * block_rows)

    block_inputs = jnp.take(input_parts, (head_place - ring) % GROUPS, axis=0)
    block_inputs = block_inputs.reshape(block_rows, width).astype(f32)
    scale_one = inverse_rms(block_inputs)
    normal_one = block_inputs * scale_one
    normed_one = (normal_one * gain_one).astype(bf16)
    qkv = matmul(normed_one, qkv_mat).astype(bf16)
    queries = qkv[:, :cols]
    kv_own = qkv[:, cols:]
    kv_all = jnp.concatenate(
        [kv_own] + [shifted(kv_own, QUERY_GROUPS, step) for step in range(1, GROUPS)]
    )
    kv_heads = kv_all.reshape(GROUPS * block_rows, 2, heads_here, head_dim)
    keys_h = jnp.transpose(kv_heads[:, 0], (1, 0, 2))
    values_h = jnp.transpose(kv_heads[:, 1], (1, 0, 2))
    queries_h = jnp.transpose(queries.reshape(block_rows, heads_here, head_dim), (1, 0, 2))
    allowed = query_seg[:, None] == key_segs[None, :]

    def scores_of(queries_h, keys_h):
        scores = jnp.einsum("htd,hkd->htk", queries_h, keys_h, preferred_element_type=f32) * factor
        return jnp.where(allowed[None], scores, -1e30)

    scores = scores_of(queries_h, keys_h)
    top = jnp.max(scores, axis=-1, keepdims=True)
    weights_f = jnp.exp(scores - top)
    total = jnp.sum(weights_f, axis=-1, keepdims=True)
    log_total = top + jnp.log(total)
    probs_low = (weights_f / total).astype(bf16)
    attended = jnp.einsum("htk,hkd->htd", probs_low, values_h, preferred_element_type=f32)

    att_rows = jnp.transpose(attended.astype(bf16), (1, 0, 2)).reshape(GROUPS, tok_rows, cols)
    mixed_parts = swap_rows(att_rows, HEAD_GROUPS)
    mixed = jnp.transpose(mixed_parts, (1, 0, 2)).reshape(tok_rows, width)
    mixed_block = jnp.stack(
        [mixed] + [shifted(mixed, HEAD_GROUPS, step) for step in range(1, GROUPS)]
    )
    mixed_block = jnp.take(mixed_block, (head_place - ring) % GROUPS, axis=0).reshape(
        block_rows, width
    )
    inputs_f = inputs.astype(f32)
    hidden_one = inputs_f + matmul(mixed, output_mat)
    scale_two = inverse_rms(hidden_one)
    normal_two = hidden_one * scale_two
    normed_two = (normal_two * gain_two).astype(bf16)
    router_probs = jax.nn.softmax(matmul(normed_two, router_mat), axis=-1)
    chosen = (expert_index[:, None] == jnp.arange(experts_all, dtype=jnp.int32)[None, :]).astype(
        f32
    )
    gate_value = jnp.sum(router_probs * chosen, axis=-1, keepdims=True)
    grad_out = cotangent.astype(f32)
    grad_expert = (gate_value * grad_out).astype(bf16)

    slots = experts_all * CAPACITY
    slot_place = expert_index * CAPACITY + slot_index
    place_mat = (slot_place[:, None] == jnp.arange(slots, dtype=jnp.int32)[None, :]).astype(bf16)
    both = jnp.concatenate((normed_two, grad_expert), axis=1)
    sent = matmul_tn(place_mat, both).astype(bf16).reshape(16, slots // 16, 2 * width)
    arrived = lax.all_to_all(sent, ("y", "x"), split_axis=0, concat_axis=0, tiled=True)
    dev_rows = 16 * CAPACITY
    arrived = jnp.transpose(
        arrived.reshape(16, local_experts, CAPACITY, 2 * width), (1, 0, 2, 3)
    ).reshape(local_experts, dev_rows, 2 * width)

    def z_shift(values, step):
        return lax.ppermute(values, "z", [(i, (i + step) % 4) for i in range(4)])

    def core_swap(values):
        return lax.ppermute(values, "core", [(0, 1), (1, 0)])

    z_rows = jnp.stack([arrived] + [z_shift(arrived, step) for step in range(1, 4)])
    rows_all = jnp.concatenate((z_rows, core_swap(z_rows)))
    rows_all = jnp.transpose(rows_all, (1, 0, 2, 3)).reshape(
        local_experts, 8 * dev_rows, 2 * width
    )
    token_rows = rows_all[:, :, :width]
    grad_rows = rows_all[:, :, width:]
    before_act = jnp.einsum("jrd,jdf->jrf", token_rows, expert_in, preferred_element_type=f32)
    activated_f, gelu_back = jax.vjp(jax.nn.gelu, before_act)
    activated = activated_f.astype(bf16)
    part_out = jnp.einsum("jrf,jfd->jrd", activated, expert_out, preferred_element_type=f32)
    grad_act = jnp.einsum("jrd,jfd->jrf", grad_rows, expert_out, preferred_element_type=f32)
    grad_pre = gelu_back(grad_act)[0].astype(bf16)
    part_back = jnp.einsum("jrf,jdf->jrd", grad_pre, expert_in, preferred_element_type=f32)
    d_expert_out = jnp.einsum("jrf,jrd->jfd", activated, grad_rows, preferred_element_type=f32)
    d_expert_in = jnp.einsum("jrd,jrf->jdf", token_rows, grad_pre, preferred_element_type=f32)

    parts = jnp.concatenate((part_out, part_back), axis=2).astype(bf16)
    parts = parts.reshape(local_experts, 2, 4, dev_rows, 2 * width)
    chip_sum = (parts[:, 0].astype(f32) + core_swap(parts[:, 1]).astype(f32)).astype(bf16)
    home = chip_sum[:, 0].astype(f32)
    for step in range(1, 4):
        home = home + z_shift(chip_sum[:, step], 4 - step).astype(f32)
    home = jnp.transpose(
        home.astype(bf16).reshape(local_experts, 16, CAPACITY, 2 * width), (1, 0, 2, 3)
    ).reshape(16, slots // 16, 2 * width)
    returned = lax.all_to_all(home, ("y", "x"), split_axis=0, concat_axis=0, tiled=True)
    returned = matmul(place_mat, returned.reshape(slots, 2 * width))
    expert_tok = returned[:, :width]
    grad_routed = returned[:, width:]

    outputs = hidden_one + gate_value * expert_tok
    grad_gate = jnp.sum(grad_out * expert_tok, axis=-1, keepdims=True)
    grad_logits = (router_probs * (chosen - gate_value) * grad_gate).astype(bf16)
    d_router = matmul_tn(normed_two, grad_logits)
    grad_normed_two = grad_routed + matmul_t(grad_logits, router_mat)
    d_gain_ffn = jnp.sum(grad_normed_two * normal_two, axis=0)
    grad_hidden = grad_out + norm_back(hidden_one, scale_two, grad_normed_two, gain_two)
    grad_branch = grad_hidden.astype(bf16)
    grad_mixed = matmul_t(grad_branch, output_mat).astype(bf16)

    pair = jnp.stack(
        (grad_mixed.reshape(tok_rows, GROUPS, cols), grad_branch.reshape(tok_rows, GROUPS, cols)),
        axis=2,
    )
    pair = jnp.transpose(pair, (1, 0, 2, 3)).reshape(GROUPS, tok_rows, 2 * cols)
    pair = swap_rows(pair, HEAD_GROUPS).reshape(block_rows, 2 * cols)
    grad_heads = jnp.transpose(
        pair[:, :cols].reshape(block_rows, heads_here, head_dim), (1, 0, 2)
    )
    d_w_out = matmul_tn(mixed_block, pair[:, cols:])

    delta = jnp.sum(grad_heads.astype(f32) * attended, axis=-1, keepdims=True)
    probs = jnp.exp(scores_of(queries_h, keys_h) - log_total)
    grad_probs = jnp.einsum("htd,hkd->htk", grad_heads, values_h, preferred_element_type=f32)
    grad_scores = (probs * (grad_probs - delta)).astype(bf16)
    grad_q = jnp.einsum("htk,hkd->thd", grad_scores, keys_h, preferred_element_type=f32) * factor
    grad_k = jnp.einsum("htk,htd->khd", grad_scores, queries_h, preferred_element_type=f32) * factor
    grad_v = jnp.einsum(
        "htk,htd->khd", probs.astype(bf16), grad_heads, preferred_element_type=f32
    )
    kv_parts = jnp.concatenate(
        (
            grad_k.reshape(GROUPS, block_rows, cols),
            grad_v.reshape(GROUPS, block_rows, cols),
        ),
        axis=2,
    ).astype(bf16)
    kv_grad = kv_parts[0].astype(f32)
    for step in range(1, GROUPS):
        kv_grad = kv_grad + shifted(kv_parts[step], QUERY_GROUPS, GROUPS - step).astype(f32)
    grad_qkv = jnp.concatenate((grad_q.reshape(block_rows, cols).astype(bf16), kv_grad.astype(bf16)), axis=1)

    d_qkv = matmul_tn(normed_one, grad_qkv)
    normed_part = matmul_t(grad_qkv, qkv_mat)
    d_gain_attn = jnp.sum(normed_part * normal_one, axis=0)
    grad_normed_one = jnp.sum(
        swap_rows(normed_part.astype(bf16).reshape(GROUPS, tok_rows, width), HEAD_GROUPS).astype(
            f32
        ),
        axis=0,
    )

    sums = jnp.concatenate(
        (
            d_qkv,
            d_w_out,
            d_router,
            d_gain_attn[:, None],
            d_gain_ffn[:, None],
            jnp.zeros((width, 128 - experts_all - 2), f32),
        ),
        axis=1,
    ).astype(bf16)
    sum_cols = sums.shape[1]
    sums = swap_rows(sums.reshape(128, rows_held, sum_cols)).astype(f32)
    sums = jnp.sum(sums.reshape(SIZES[:1] + (2, 4, 4, rows_held, sum_cols)), axis=0)
    by_head = jnp.sum(sums[0], axis=0) + jnp.sum(sums[1], axis=1)
    rest = jnp.sum(by_head[..., 4 * cols :], axis=0)
    mats = jnp.transpose(
        by_head[..., : 4 * cols].reshape(GROUPS, rows_held, 4, cols), (2, 1, 0, 3)
    ).reshape(4, rows_held, width)

    scale_in = inverse_rms(inputs_f)
    d_inputs = grad_hidden + norm_back(inputs_f, scale_in, grad_normed_one, gain_one)
    return (
        outputs.astype(bf16),
        d_inputs,
        rest[:, experts_all],
        mats[0],
        mats[1],
        mats[2],
        mats[3],
        rest[:, experts_all + 1],
        rest[:, :experts_all],
        d_expert_in,
        d_expert_out,
    )


def solution(mesh):
    mesh = Mesh(mesh.devices.reshape(SIZES), ALL)
    dp = ("z", "core")
    seq = ("y", "x")
    rows = P(ALL, None)
    in_specs = (
        rows,
        P(ALL),
        rows,
        rows,
        rows,
        rows,
        P(ALL),
        rows,
        P(seq, None, dp),
        P(seq, dp, None),
        P(ALL),
        P(ALL),
        P(ALL),
        rows,
    )
    out_specs = (
        rows,
        rows,
        P(ALL),
        rows,
        rows,
        rows,
        rows,
        P(ALL),
        rows,
        P(seq, None, dp),
        P(seq, dp, None),
    )
    return jax.shard_map(body, mesh=mesh, in_specs=in_specs, out_specs=out_specs, check_vma=False)
```

```python
import functools

import jax
import jax.numpy as jnp
import numpy as np
from jax import lax
from jax.experimental import pallas as pl
from jax.experimental.pallas import tpu as pltpu
from jax.sharding import Mesh
from jax.sharding import PartitionSpec as P

HEADS = 12
GROUPS = 4
CAPACITY = 5
EPSILON = 1e-06
ALL = ("z", "core", "y", "x")
SIZES = (4, 2, 4, 4)

f32 = jnp.float32
bf16 = jnp.bfloat16

PLACES = np.arange(128).reshape(SIZES)
HEAD_GROUPS = [[int(i) for i in PLACES[z, 0, k, :]] for z in range(4) for k in range(4)] + [
    [int(i) for i in PLACES[z, 1, :, k]] for z in range(4) for k in range(4)
]
QUERY_GROUPS = [[int(i) for i in PLACES[z, 0, :, k]] for z in range(4) for k in range(4)] + [
    [int(i) for i in PLACES[z, 1, k, :]] for z in range(4) for k in range(4)
]

CORE_GROUPS = [[int(i) for i in PLACES[:, core].reshape(-1)] for core in range(2)]


def shifted(values, groups, step):
    pairs = [(g[i], g[(i + step) % len(g)]) for g in groups for i in range(len(g))]
    return lax.ppermute(values, ALL, pairs)


def swap_rows(values, groups=None):
    return lax.all_to_all(
        values, ALL, split_axis=0, concat_axis=0, tiled=True, axis_index_groups=groups
    )


def matmul(a, b):
    return jnp.dot(a, b, preferred_element_type=f32)


def matmul_t(a, b):
    return lax.dot_general(a, b, (((1,), (1,)), ((), ())), preferred_element_type=f32)


def matmul_tn(a, b):
    return lax.dot_general(a, b, (((0,), (0,)), ((), ())), preferred_element_type=f32)


def inverse_rms(values):
    return lax.rsqrt(jnp.mean(values * values, axis=-1, keepdims=True) + EPSILON)


def norm_back(values, scale, grad, gain_vec):
    u = grad * gain_vec
    return scale * u - values * (scale * scale * scale) * jnp.mean(
        u * values, axis=-1, keepdims=True
    )

MASKED = -1e30
VMEM_LIMIT = 48 * 1024 * 1024


def call_kernel(kernel, out_shapes, flops, *operands, scalars=None):
    moved = sum(v.size * v.dtype.itemsize for v in operands)
    moved += sum(v.size * v.dtype.itemsize for v in out_shapes)
    in_specs = [pl.BlockSpec(memory_space=pltpu.VMEM)] * len(operands)
    if scalars is not None:
        in_specs = [pl.BlockSpec(memory_space=pltpu.SMEM)] + in_specs
        operands = (scalars,) + operands
    return pl.pallas_call(
        kernel,
        out_shape=out_shapes,
        in_specs=in_specs,
        out_specs=[pl.BlockSpec(memory_space=pltpu.VMEM)] * len(out_shapes),
        compiler_params=pltpu.CompilerParams(vmem_limit_bytes=VMEM_LIMIT),
        cost_estimate=pl.CostEstimate(flops=flops, bytes_accessed=moved, transcendentals=0),
    )(*operands)


def shape(rows, columns, dtype=f32):
    return jax.ShapeDtypeStruct((rows, columns), dtype)


def transposed_scores(k_ref, kmask_ref, q_ref, qmask_ref, lanes, factor):
    key_side = jnp.concatenate((k_ref[:, lanes], kmask_ref[...]), axis=1)
    query_side = jnp.concatenate((q_ref[:, lanes] * factor, qmask_ref[...]), axis=1)
    return matmul_t(key_side, query_side)


def attend_kernel(first, last, blocks, heads, head_dim, factor, *refs):
    q_ref, qmask_ref = refs[:2]
    kv_refs = refs[2 : 2 + blocks]
    mask_refs = refs[2 + blocks : 2 + 2 * blocks]
    rest = refs[2 + 2 * blocks :]
    if not first:
        old_sum, old_top, old_total = rest[:3]
        rest = rest[3:]
    cols = heads * head_dim
    for head in range(heads):
        lanes = slice(head * head_dim, (head + 1) * head_dim)
        value_lanes = slice(cols + head * head_dim, cols + (head + 1) * head_dim)
        if first:
            top = total = accum = None
        else:
            top = old_top[head : head + 1, :]
            total = old_total[head : head + 1, :]
            accum = old_sum[lanes, :]
        for kv_ref, mask_ref in zip(kv_refs, mask_refs):
            scores = transposed_scores(kv_ref, mask_ref, q_ref, qmask_ref, lanes, factor)
            newest = jnp.max(scores, axis=0, keepdims=True)
            if top is not None:
                newest = jnp.maximum(top, newest)
            terms = jnp.exp(scores - newest)
            term_sum = jnp.sum(terms, axis=0, keepdims=True)
            product = matmul_tn(kv_ref[:, value_lanes], terms.astype(bf16))
            if top is None:
                total, accum = term_sum, product
            else:
                shrink = jnp.exp(top - newest)
                total = total * shrink + term_sum
                accum = accum * shrink + product
            top = newest
        if last:
            att_ref, low_ref, log_ref = rest
            accum = accum / total
            att_ref[lanes, :] = accum
            low_ref[:, :, lanes] = accum.T.astype(bf16).reshape(low_ref.shape[:2] + (head_dim,))
            log_ref[head : head + 1, :] = top + jnp.log(total)
        else:
            sum_ref, top_ref, total_ref = rest
            sum_ref[lanes, :] = accum
            top_ref[head : head + 1, :] = top
            total_ref[head : head + 1, :] = total


def attend_back_kernel(blocks, heads, head_dim, factor, *refs):
    q_ref, qmask_ref, grad_ref, att_ref, log_ref = refs[:5]
    kv_refs = refs[5 : 5 + blocks]
    mask_refs = refs[5 + blocks : 5 + 2 * blocks]
    dq_ref = refs[5 + 2 * blocks]
    out_refs = refs[6 + 2 * blocks :]
    cols = heads * head_dim
    for head in range(heads):
        lanes = slice(head * head_dim, (head + 1) * head_dim)
        value_lanes = slice(cols + head * head_dim, cols + (head + 1) * head_dim)
        grad = grad_ref[:, :, lanes].reshape(-1, head_dim)
        query = q_ref[:, lanes] * factor
        delta = jnp.sum(grad.astype(f32).T * att_ref[lanes, :], axis=0, keepdims=True)
        log_total = log_ref[head : head + 1, :]
        dq = None
        for kv_ref, mask_ref, out_ref in zip(kv_refs, mask_refs, out_refs):
            scores = transposed_scores(kv_ref, mask_ref, q_ref, qmask_ref, lanes, factor)
            probs = jnp.exp(scores - log_total)
            grad_probs = matmul_t(kv_ref[:, value_lanes], grad)
            grad_scores = (probs * (grad_probs - delta)).astype(bf16)
            out_ref[:, value_lanes] = matmul(probs.astype(bf16), grad).astype(out_ref.dtype)
            out_ref[:, lanes] = matmul(grad_scores, query).astype(out_ref.dtype)
            product = matmul_tn(kv_ref[:, lanes], grad_scores)
            dq = product if dq is None else dq + product
        dq_ref[:, lanes] = dq.T * factor


def front_kernel(
    cols, pick_ref, held_ref, rows_ref, mat_ref, out_ref, extra_ref, gain_ref, normed_ref, q_ref, kv_ref
):
    held = held_ref[...].reshape(-1, held_ref.shape[2])
    weights = matmul(pick_ref[...], held).astype(bf16)
    mat = weights[:, : 3 * cols]
    mat_ref[...] = mat
    out_ref[...] = weights[:, 3 * cols + 64 : 4 * cols + 64]
    extra = weights[:, 4 * cols + 64 :]
    extra_ref[...] = extra
    gains = extra.astype(f32).T[:8]
    gain_ref[...] = gains
    rows = rows_ref[...].reshape(-1, rows_ref.shape[2]).astype(f32)
    normed = (rows * inverse_rms(rows) * gains[0:1]).astype(bf16)
    normed_ref[...] = normed
    qkv = matmul(normed, mat).astype(bf16)
    q_ref[...] = qkv[:, :cols]
    kv_ref[...] = qkv[:, cols:]


def chosen_lane(expert_ref, lanes):
    lane = lax.broadcasted_iota(jnp.int32, (expert_ref.shape[0], lanes), 1)
    return (lane == expert_ref[...] + 2).astype(f32)


def slot_matrix(keys_ref, parity):
    slot = lax.broadcasted_iota(jnp.int32, (128, keys_ref.shape[1]), 0)
    return (slot == keys_ref[parity : parity + 1, :]).astype(bf16)


def route_kernel(
    experts,
    place_ref,
    att_ref,
    w0_ref,
    w1_ref,
    w2_ref,
    w3_ref,
    in_ref,
    cot_ref,
    gain_ref,
    extra_ref,
    expert_ref,
    keys_ref,
    sent0_ref,
    sent1_ref,
    hidden_ref,
    normed_ref,
    probs_ref,
):
    query_place = place_ref[1]
    mixed = jnp.concatenate([att_ref[i] for i in range(GROUPS)], axis=1)
    pieces = [matmul(mixed, ref[...]) for ref in (w0_ref, w1_ref, w2_ref, w3_ref)]
    columns = []
    for spot in range(GROUPS):
        value = pieces[0]
        for step in range(1, GROUPS):
            value = jnp.where((query_place + GROUPS - step) % GROUPS == spot, pieces[step], value)
        columns.append(value)
    hidden = in_ref[...].astype(f32) + jnp.concatenate(columns, axis=1)
    hidden_ref[...] = hidden
    normed = (hidden * inverse_rms(hidden) * gain_ref[1:2]).astype(bf16)
    normed_ref[...] = normed
    logits = matmul(normed, extra_ref[...])
    lane = lax.broadcasted_iota(jnp.int32, logits.shape, 1)
    logits = jnp.where((lane >= 2) & (lane < 2 + experts), logits, MASKED)
    terms = jnp.exp(logits - jnp.max(logits, axis=1, keepdims=True))
    probs = terms / jnp.sum(terms, axis=1, keepdims=True)
    probs_ref[...] = probs
    gate = jnp.sum(probs * chosen_lane(expert_ref, probs.shape[1]), axis=1, keepdims=True)
    grad_expert = (gate * cot_ref[...].astype(f32)).astype(bf16)
    width = normed.shape[1]
    for parity, sent_ref in enumerate((sent0_ref, sent1_ref)):
        slots = slot_matrix(keys_ref, parity)
        sent_ref[:, :width] = matmul(slots, normed).astype(bf16)
        sent_ref[:, width:] = matmul(slots, grad_expert).astype(bf16)


def return_kernel(
    experts,
    place_ref,
    back0_ref,
    back1_ref,
    w0_ref,
    w1_ref,
    w2_ref,
    w3_ref,
    hidden_ref,
    cot_ref,
    probs_ref,
    gain_ref,
    extra_ref,
    expert_ref,
    keys_ref,
    outputs_ref,
    grad_ref,
    pair_ref,
    logits_ref,
    gain_sum_ref,
):
    query_place = place_ref[1]
    width = hidden_ref.shape[1]
    cols = width // GROUPS
    back = None
    for parity, back_ref in enumerate((back0_ref, back1_ref)):
        product = matmul_tn(slot_matrix(keys_ref, parity), back_ref[...])
        back = product if back is None else back + product
    expert_tok, grad_routed = back[:, :width], back[:, width:]
    hidden = hidden_ref[...]
    grad_out = cot_ref[...].astype(f32)
    probs = probs_ref[...]
    chosen = chosen_lane(expert_ref, probs.shape[1])
    gate = jnp.sum(probs * chosen, axis=1, keepdims=True)
    outputs_ref[...] = (hidden + gate * expert_tok).astype(bf16)
    grad_gate = jnp.sum(grad_out * expert_tok, axis=1, keepdims=True)
    grad_logits = (probs * (chosen - gate) * grad_gate).astype(bf16)
    logits_ref[...] = grad_logits
    grad_normed = grad_routed + matmul_t(grad_logits, extra_ref[...])
    scale = inverse_rms(hidden)
    gain_sum_ref[...] = jnp.sum(grad_normed * hidden * scale, axis=0, keepdims=True)
    grad_hidden = grad_out + norm_back(hidden, scale, grad_normed, gain_ref[1:2])
    grad_ref[...] = grad_hidden
    branch = grad_hidden.astype(bf16)
    grad_mixed = None
    for step, ref in enumerate((w0_ref, w1_ref, w2_ref, w3_ref)):
        block = branch[:, :cols]
        for spot in range(1, GROUPS):
            block = jnp.where(
                (query_place + GROUPS - step) % GROUPS == spot,
                branch[:, spot * cols : (spot + 1) * cols],
                block,
            )
        product = matmul_t(block, ref[...])
        grad_mixed = product if grad_mixed is None else grad_mixed + product
    for spot in range(GROUPS):
        lanes = slice(spot * cols, (spot + 1) * cols)
        pair_ref[spot, :, :cols] = grad_mixed[:, lanes].astype(bf16)
        pair_ref[spot, :, cols:] = branch[:, lanes]


def expert_kernel(expert, blocks, part, width, *refs):
    row_refs = refs[:blocks]
    in_ref, out_ref = refs[blocks : blocks + 2]
    part_refs = refs[blocks + 2 : 2 * blocks + 2]
    rows_ref, act_ref, pre_ref = refs[2 * blocks + 2 :]
    for place, row_ref in enumerate(row_refs):
        rows_ref[pl.ds(place * part, part), :] = row_ref[...]
    before_act = matmul(rows_ref[:, :width], in_ref[expert])
    grad_act = matmul_t(rows_ref[:, width:], out_ref[expert])
    square = before_act * before_act
    inner = jnp.tanh(0.7978845608028654 * (before_act + 0.044715 * square * before_act))
    half = 0.5 * (1.0 + inner)
    act_ref[...] = (before_act * half).astype(bf16)
    slope = half + (0.5 * 0.7978845608028654) * before_act * (1.0 - inner * inner) * (
        1.0 + (3 * 0.044715) * square
    )
    pre_ref[...] = (grad_act * slope).astype(bf16)
    part_out = matmul(act_ref[...], out_ref[expert])
    part_back = matmul_t(pre_ref[...], in_ref[expert])
    for place, part_ref in enumerate(part_refs):
        rows = slice(place * part, (place + 1) * part)
        part_ref[:, :width] = part_out[rows].astype(bf16)
        part_ref[:, width:] = part_back[rows].astype(bf16)


def expert_grad_kernel(experts, width, *refs):
    in_ref, out_ref = refs[3 * experts :]
    for expert in range(experts):
        rows_ref, act_ref, pre_ref = refs[3 * expert : 3 * expert + 3]
        out_ref[expert] = matmul_tn(act_ref[...], rows_ref[:, width:])
        in_ref[expert] = matmul_tn(rows_ref[:, :width], pre_ref[...])


def tail_kernel(
    dq_far_ref,
    dq_own_ref,
    kv0_ref,
    kv1_ref,
    kv2_ref,
    kv3_ref,
    mat_ref,
    rows_ref,
    one_ref,
    spread_ref,
    turned_ref,
    att0_ref,
    att1_ref,
    att2_ref,
    att3_ref,
    pair_ref,
    two_ref,
    logits_ref,
    gain_two_ref,
    own_ref,
    away_ref,
    part_ref,
):
    cols = dq_far_ref.shape[1]
    grad_q = (dq_far_ref[...] + dq_own_ref[...]).astype(bf16)
    grad_kv = kv0_ref[...]
    for ref in (kv1_ref, kv2_ref, kv3_ref):
        grad_kv = grad_kv + ref[...].astype(f32)
    grad_qkv = jnp.concatenate((grad_q, grad_kv.astype(bf16)), axis=1)
    part = matmul_t(grad_qkv, mat_ref[...])
    part_ref[...] = part.astype(bf16).reshape(part_ref.shape)
    rows = rows_ref[...].reshape(part.shape).astype(f32)
    gain_one = jnp.sum(part * rows * inverse_rms(rows), axis=0, keepdims=True)
    branch = pair_ref[:, :, cols:].reshape(-1, cols)
    products = [
        matmul_tn(ref[...].reshape(-1, cols), branch).astype(bf16)
        for ref in (att0_ref, att1_ref, att2_ref, att3_ref)
    ]
    products = jnp.concatenate(products, axis=0)
    half = own_ref.shape[0]
    for place, sums_ref in enumerate((own_ref, away_ref)):
        spot = slice(place * half, (place + 1) * half)
        sums_ref[:, : 3 * cols] = matmul(one_ref[spot], grad_qkv).astype(bf16)
        sums_ref[:, 3 * cols : 4 * cols] = matmul(turned_ref[spot], products).astype(bf16)
        rest = matmul(two_ref[spot], logits_ref[...])
        lane = lax.broadcasted_iota(jnp.int32, rest.shape, 1)
        spread = spread_ref[spot].astype(f32)
        for index, gain in ((0, gain_one), (1, gain_two_ref[...])):
            gain = jnp.sum(spread * gain, axis=1, keepdims=True)
            rest = jnp.where(lane == index, gain, rest)
        rest = jnp.concatenate((rest, jnp.zeros_like(rest)), axis=1)
        sums_ref[:, 4 * cols :] = rest.astype(bf16)


def sum_kernel(groups, sums_ref, mats_ref, rest_ref):
    rows = rest_ref.shape[0]
    cols = mats_ref.shape[2] // groups
    terms = [[None] * groups, [None] * groups]
    for z in range(4):
        for y in range(groups):
            for x in range(groups):
                both = sums_ref[(z * groups + y) * groups + x].astype(f32)
                for core, head in ((0, x), (1, y)):
                    term = both[core * 8 : core * 8 + 8]
                    old = terms[core][head]
                    terms[core][head] = term if old is None else old + term
    rest = None
    for head in range(groups):
        total = (terms[0][head] + terms[1][head])[:rows]
        for mat in range(4):
            mats_ref[mat, :, head * cols : (head + 1) * cols] = total[
                :, mat * cols : (mat + 1) * cols
            ]
        extra = total[:, 4 * cols :]
        rest = extra if rest is None else rest + extra
    rest_ref[...] = rest


def body(
    inputs,
    gain_attn,
    w_query,
    w_key,
    w_value,
    w_output,
    gain_ffn,
    router,
    expert_in,
    expert_out,
    expert_index,
    slot_index,
    segment_ids,
    cotangent,
):
    tok_rows, width = inputs.shape
    head_dim = width // HEADS
    factor = head_dim ** (-0.5)
    cols = width // GROUPS
    heads_here = HEADS // GROUPS
    experts_all = router.shape[1]
    rows_held = w_query.shape[0]
    local_experts = expert_in.shape[0]
    hidden = expert_in.shape[2]
    block_rows = GROUPS * tok_rows

    core = lax.axis_index("core")
    y_place = lax.axis_index("y")
    x_place = lax.axis_index("x")
    head_place = jnp.where(core == 0, x_place, y_place)
    query_place = jnp.where(core == 0, y_place, x_place)
    ring = jnp.arange(GROUPS, dtype=jnp.int32)

    input_parts = jnp.stack(
        [inputs] + [shifted(inputs, HEAD_GROUPS, step) for step in range(1, GROUPS)]
    )

    def core_swap(values):
        return lax.ppermute(values, "core", [(0, 1), (1, 0)])

    def by_chip(values, other):
        return jnp.where(core == 0, values, other), jnp.where(core == 0, other, values)

    extra = jnp.concatenate((gain_attn[:, None], gain_ffn[:, None], router), axis=1)
    extra = jnp.pad(extra, ((0, 0), (0, 64 - extra.shape[1])))
    mine = jnp.concatenate((w_query, w_key, w_value, w_output, extra), axis=1)
    chip = jnp.concatenate(by_chip(mine, core_swap(mine)))
    chip_rows = chip.shape[0]
    mats = chip[:, : 4 * width].reshape(chip_rows, 4, GROUPS, cols)
    mats = jnp.transpose(mats, (2, 0, 1, 3))
    three = mats[:, :, :3].reshape(GROUPS, chip_rows, 3 * cols)
    three = jnp.pad(three, ((0, 0), (0, 0), (0, 64)))
    square = (GROUPS, GROUPS, chip_rows)
    packed = jnp.concatenate(
        (
            jnp.broadcast_to(three[None], square + (3 * cols + 64,)),
            jnp.broadcast_to(mats[:, None, :, 3], square + (cols,)),
            jnp.broadcast_to(chip[None, None, :, 4 * width :], square + (64,)),
        ),
        axis=3,
    )
    wide = packed.shape[3]
    packed = jnp.where(core == 0, packed, jnp.transpose(packed, (1, 0, 2, 3)))
    seg_row = jnp.pad(segment_ids.astype(bf16), (0, wide - tok_rows))
    seg_rows = jnp.broadcast_to(
        jnp.pad(seg_row[None], ((0, 15 - chip_rows), (0, 0)))[None, None],
        (GROUPS, GROUPS, 16 - chip_rows, wide),
    )
    packed = jnp.concatenate((packed, seg_rows), axis=2)
    packed = jnp.broadcast_to(packed[None], (SIZES[0],) + packed.shape)
    held = swap_rows(packed.reshape(64, 16, wide), CORE_GROUPS)
    feature = jnp.arange(width, dtype=jnp.int32)
    owner, row = feature // rows_held, feature % rows_held
    owner_core = owner // 16 % 2
    chip_index = owner // 32 * 16 + owner % 16
    pick = (
        (chip_index * 16 + owner_core * rows_held + row)[:, None]
        == jnp.arange(1024, dtype=jnp.int32)[None, :]
    ).astype(bf16)
    spread_row = jnp.where(owner_core == core, 0, 512) + chip_index * 8 + row
    spread = (jnp.arange(1024, dtype=jnp.int32)[:, None] == spread_row[None, :]).astype(bf16)
    segs = held.reshape(SIZES[0], 16, 16, wide)[:, :, chip_rows, :tok_rows]
    segs = lax.dynamic_index_in_dim(segs, lax.axis_index("z"), axis=0, keepdims=False)
    segs = segs.reshape(GROUPS, GROUPS, tok_rows)
    segs = jnp.where(core == 0, segs, jnp.transpose(segs, (1, 0, 2)))
    key_segs = jnp.take(segs, (query_place - ring) % GROUPS, axis=0)
    query_seg = key_segs[0].reshape(block_rows)
    key_segs = key_segs.reshape(GROUPS * block_rows)

    block_inputs = jnp.take(input_parts, (head_place - ring) % GROUPS, axis=0)
    qkv_mat, out_cols, extra, gains, normed_one, queries, kv_own = call_kernel(
        functools.partial(front_kernel, cols),
        (
            shape(width, 3 * cols, bf16),
            shape(width, cols, bf16),
            shape(width, 64, bf16),
            shape(8, width),
            shape(block_rows, width, bf16),
            shape(block_rows, cols, bf16),
            shape(block_rows, 2 * cols, bf16),
        ),
        2 * width * (1024 * wide + 3 * cols * block_rows),
        pick,
        held,
        block_inputs,
    )
    kv_far = [shifted(kv_own, QUERY_GROUPS, step) for step in range(1, GROUPS)]
    out_parts = [out_cols] + [shifted(out_cols, QUERY_GROUPS, step) for step in range(1, GROUPS)]
    documents = jnp.arange(head_dim, dtype=bf16)[None, :]
    query_mask = (query_seg[:, None] == documents).astype(bf16)
    key_masks = jnp.where((key_segs[:, None] == documents) | (documents > 2), 0.0, MASKED)
    key_masks = key_masks.astype(bf16).reshape(GROUPS, block_rows, head_dim)
    key_masks = [key_masks[i] for i in range(GROUPS)]
    sizes = (heads_here, head_dim, factor)
    pairs = 2 * block_rows * block_rows * cols
    state = call_kernel(
        functools.partial(attend_kernel, True, False, 1, *sizes),
        (shape(cols, block_rows), shape(8, block_rows), shape(8, block_rows)),
        2 * pairs,
        queries,
        query_mask,
        kv_own,
        key_masks[0],
    )
    attended, att_low, log_total = call_kernel(
        functools.partial(attend_kernel, False, True, GROUPS - 1, *sizes),
        (
            shape(cols, block_rows),
            jax.ShapeDtypeStruct((GROUPS, tok_rows, cols), bf16),
            shape(8, block_rows),
        ),
        6 * pairs,
        queries,
        query_mask,
        *kv_far,
        *key_masks[1:],
        *state,
    )
    mixed_parts = swap_rows(att_low, HEAD_GROUPS)
    att_parts = [att_low] + [shifted(att_low, HEAD_GROUPS, step) for step in range(1, GROUPS)]
    places = jnp.stack((head_place, query_place)).astype(jnp.int32)
    expert_col = expert_index[:, None]
    slot_row = expert_index // local_experts * 8 + slot_index
    keys = jnp.stack(
        [
            jnp.where(expert_index % local_experts == parity, slot_row, -1)
            for parity in range(local_experts)
        ]
    )
    sent_shape = shape(128, 2 * width, bf16)
    sent0, sent1, hidden_one, normed_two, router_probs = call_kernel(
        functools.partial(route_kernel, experts_all),
        (
            sent_shape,
            sent_shape,
            shape(tok_rows, width),
            shape(tok_rows, width, bf16),
            shape(tok_rows, 64),
        ),
        2 * tok_rows * width * (width + 512),
        mixed_parts,
        *out_parts,
        inputs,
        cotangent,
        gains,
        extra,
        expert_col,
        keys,
        scalars=places,
    )

    dev_rows = 16 * CAPACITY
    dense = jnp.arange(dev_rows, dtype=jnp.int32)
    squeeze = (
        (dense // CAPACITY * 8 + dense % CAPACITY)[:, None]
        == jnp.arange(128, dtype=jnp.int32)[None, :]
    ).astype(bf16)

    def seq_swap(values):
        values = values.reshape(16, 8, 2 * width)
        values = lax.all_to_all(values, ("y", "x"), split_axis=0, concat_axis=0, tiled=True)
        return values.reshape(128, 2 * width)

    def z_shift(values, step):
        return lax.ppermute(values, "z", [(i, (i + step) % 4) for i in range(4)])

    block = shape(dev_rows, 2 * width, bf16)
    all_rows = 8 * dev_rows
    act_shape = shape(all_rows, hidden, bf16)
    arrived = [matmul(squeeze, seq_swap(sent)).astype(bf16) for sent in (sent0, sent1)]
    kept, backs = [], []
    for expert in range(local_experts):
        z_rows = [arrived[expert]] + [z_shift(arrived[expert], step) for step in range(1, 4)]
        row_blocks = z_rows + [core_swap(rows) for rows in z_rows]
        *parts, rows_all, activated, grad_pre = call_kernel(
            functools.partial(expert_kernel, expert, 8, dev_rows, width),
            (block,) * 8 + (shape(all_rows, 2 * width, bf16), act_shape, act_shape),
            8 * all_rows * width * hidden,
            *row_blocks,
            expert_in,
            expert_out,
        )
        kept += [rows_all, activated, grad_pre]
        chip_sums = [
            parts[place].astype(f32) + core_swap(parts[4 + place]).astype(f32)
            for place in range(4)
        ]
        home = chip_sums[0]
        for step in range(1, 4):
            home = home + z_shift(chip_sums[step].astype(bf16), 4 - step).astype(f32)
        home = matmul_tn(squeeze, home.astype(bf16)).astype(bf16)
        backs.append(seq_swap(home))
    d_expert_in, d_expert_out = call_kernel(
        functools.partial(expert_grad_kernel, local_experts, width),
        (
            jax.ShapeDtypeStruct(expert_in.shape, f32),
            jax.ShapeDtypeStruct(expert_out.shape, f32),
        ),
        4 * local_experts * all_rows * width * hidden,
        *kept,
    )

    outputs, grad_hidden, pair, grad_logits, d_gain_ffn = call_kernel(
        functools.partial(return_kernel, experts_all),
        (
            shape(tok_rows, width, bf16),
            shape(tok_rows, width),
            jax.ShapeDtypeStruct((GROUPS, tok_rows, 2 * cols), bf16),
            shape(tok_rows, 64, bf16),
            shape(1, width),
        ),
        2 * tok_rows * width * (width + 512),
        *backs,
        *out_parts,
        hidden_one,
        cotangent,
        router_probs,
        gains,
        extra,
        expert_col,
        keys,
        scalars=places,
    )

    pair = swap_rows(pair, HEAD_GROUPS)
    kv_block = shape(block_rows, 2 * cols, bf16)
    dq_far, *kv_parts = call_kernel(
        functools.partial(attend_back_kernel, GROUPS - 1, *sizes),
        (shape(block_rows, cols),) + (kv_block,) * (GROUPS - 1),
        15 * pairs,
        queries,
        query_mask,
        pair,
        attended,
        log_total,
        *kv_far,
        *key_masks[1:],
    )
    dq_own, kv_grad = call_kernel(
        functools.partial(attend_back_kernel, 1, *sizes),
        (shape(block_rows, cols), shape(block_rows, 2 * cols)),
        5 * pairs,
        queries,
        query_mask,
        pair,
        attended,
        log_total,
        kv_own,
        key_masks[0],
    )
    kv_back = [
        shifted(kv_parts[step - 1], QUERY_GROUPS, GROUPS - step) for step in range(1, GROUPS)
    ]

    turned_feature = (head_place - feature // cols) % GROUPS * cols + feature % cols
    turned = (
        jnp.arange(1024, dtype=jnp.int32)[:, None] == jnp.take(spread_row, turned_feature)[None, :]
    ).astype(bf16)
    sums_shape = shape(512, 896, bf16)
    own_sums, away_sums, normed_parts = call_kernel(
        tail_kernel,
        (sums_shape, sums_shape, jax.ShapeDtypeStruct((GROUPS, tok_rows, width), bf16)),
        2 * 1024 * block_rows * 4 * cols,
        dq_far,
        dq_own,
        kv_grad,
        *kv_back,
        qkv_mat,
        block_inputs,
        matmul_t(spread, normed_one).astype(bf16),
        spread,
        turned,
        *att_parts,
        pair,
        matmul_t(spread, normed_two).astype(bf16),
        grad_logits,
        d_gain_ffn,
    )

    def part_of(step):
        return lax.dynamic_index_in_dim(
            normed_parts, (head_place + step) % GROUPS, axis=0, keepdims=False
        )

    grad_normed_one = part_of(0).astype(f32)
    for step in range(1, GROUPS):
        grad_normed_one = grad_normed_one + shifted(part_of(step), HEAD_GROUPS, step).astype(f32)
    by_core = by_chip(own_sums, core_swap(away_sums))
    sums = jnp.stack([v.reshape(64, 8, 896) for v in by_core], axis=1).reshape(64, 16, 896)
    sums = swap_rows(sums, CORE_GROUPS)
    mats, rest = call_kernel(
        functools.partial(sum_kernel, GROUPS),
        (
            jax.ShapeDtypeStruct((4, rows_held, width), f32),
            shape(rows_held, 896 - 4 * cols),
        ),
        sums.size,
        sums,
    )

    inputs_f = inputs.astype(f32)
    d_inputs = grad_hidden + norm_back(
        inputs_f, inverse_rms(inputs_f), grad_normed_one, gains[0:1]
    )
    return (
        outputs,
        d_inputs,
        rest[:, 0],
        mats[0],
        mats[1],
        mats[2],
        mats[3],
        rest[:, 1],
        rest[:, 2 : 2 + experts_all],
        d_expert_in,
        d_expert_out,
    )


def solution(mesh):
    mesh = Mesh(mesh.devices.reshape(SIZES), ALL)
    dp = ("z", "core")
    seq = ("y", "x")
    rows = P(ALL, None)
    in_specs = (
        rows,
        P(ALL),
        rows,
        rows,
        rows,
        rows,
        P(ALL),
        rows,
        P(seq, None, dp),
        P(seq, dp, None),
        P(ALL),
        P(ALL),
        P(ALL),
        rows,
    )
    out_specs = (
        rows,
        rows,
        P(ALL),
        rows,
        rows,
        rows,
        rows,
        P(ALL),
        rows,
        P(seq, None, dp),
        P(seq, dp, None),
    )
    return jax.shard_map(body, mesh=mesh, in_specs=in_specs, out_specs=out_specs, check_vma=False)
```

```python
import functools

import jax
import jax.numpy as jnp
from jax import lax
from jax.experimental import pallas as pl
from jax.experimental.pallas import tpu as pltpu
from jax.sharding import Mesh
from jax.sharding import PartitionSpec as P

HEADS = 12
GROUPS = 4
CAPACITY = 5
EPSILON = 1e-06
ALL = ("z", "core", "y", "x")
SIZES = (4, 2, 4, 4)

f32 = jnp.float32
bf16 = jnp.bfloat16


def shifted(values, axis, step):
    return lax.ppermute(values, axis, [(i, (i + step) % 4) for i in range(4)])


def swap_rows(values, axes):
    return lax.all_to_all(values, axes, split_axis=0, concat_axis=0, tiled=True)


def matmul(a, b):
    return jnp.dot(a, b, preferred_element_type=f32)


def matmul_t(a, b):
    return lax.dot_general(a, b, (((1,), (1,)), ((), ())), preferred_element_type=f32)


def matmul_tn(a, b):
    return lax.dot_general(a, b, (((0,), (0,)), ((), ())), preferred_element_type=f32)


def inverse_rms(values):
    return lax.rsqrt(jnp.mean(values * values, axis=-1, keepdims=True) + EPSILON)


def norm_back(values, scale, grad, gain_vec):
    u = grad * gain_vec
    return scale * u - values * (scale * scale * scale) * jnp.mean(
        u * values, axis=-1, keepdims=True
    )

MASKED = -1e30
MIB = 1024 * 1024


def call_kernel(kernel, out_shapes, micros, scratch_mib, *operands, scalars=None, scratch=()):
    moved = sum(v.size * v.dtype.itemsize for v in operands)
    moved += sum(v.size * v.dtype.itemsize for v in out_shapes)
    in_specs = [pl.BlockSpec(memory_space=pltpu.VMEM)] * len(operands)
    if scalars is not None:
        in_specs = [pl.BlockSpec(memory_space=pltpu.SMEM)] + in_specs
        operands = (scalars,) + operands
    return pl.pallas_call(
        kernel,
        out_shape=out_shapes,
        in_specs=in_specs,
        out_specs=[pl.BlockSpec(memory_space=pltpu.VMEM)] * len(out_shapes),
        scratch_shapes=scratch,
        compiler_params=pltpu.CompilerParams(
            vmem_limit_bytes=(moved * 4 // 3 // MIB + 2 + scratch_mib) * MIB
        ),
        cost_estimate=pl.CostEstimate(
            flops=int(micros * 1.1e9), bytes_accessed=moved, transcendentals=0
        ),
    )(*operands)


def shape(rows, columns, dtype=f32):
    return jax.ShapeDtypeStruct((rows, columns), dtype)


def transposed_scores(k_ref, kmask_ref, q_ref, qmask_ref, lanes, factor):
    key_side = jnp.concatenate((k_ref[:, lanes], kmask_ref[...]), axis=1)
    query_side = jnp.concatenate((q_ref[:, lanes] * factor, qmask_ref[...]), axis=1)
    return matmul_t(key_side, query_side)


def attend_kernel(first, last, blocks, heads, head_dim, factor, *refs):
    q_ref, qmask_ref = refs[:2]
    kv_refs = refs[2 : 2 + blocks]
    mask_refs = refs[2 + blocks : 2 + 2 * blocks]
    rest = refs[2 + 2 * blocks :]
    if not first:
        old_sum, old_top, old_total = rest[:3]
        rest = rest[3:]
    cols = heads * head_dim
    for head in range(heads):
        lanes = slice(head * head_dim, (head + 1) * head_dim)
        value_lanes = slice(cols + head * head_dim, cols + (head + 1) * head_dim)
        if first:
            top = total = accum = None
        else:
            top = old_top[head : head + 1, :]
            total = old_total[head : head + 1, :]
            accum = old_sum[lanes, :]
        for kv_ref, mask_ref in zip(kv_refs, mask_refs):
            scores = transposed_scores(kv_ref, mask_ref, q_ref, qmask_ref, lanes, factor)
            newest = jnp.max(scores, axis=0, keepdims=True)
            if top is not None:
                newest = jnp.maximum(top, newest)
            terms = jnp.exp(scores - newest)
            term_sum = jnp.sum(terms, axis=0, keepdims=True)
            product = matmul_tn(kv_ref[:, value_lanes], terms.astype(bf16))
            if top is None:
                total, accum = term_sum, product
            else:
                shrink = jnp.exp(top - newest)
                total = total * shrink + term_sum
                accum = accum * shrink + product
            top = newest
        if last:
            att_ref, low_ref, log_ref = rest
            accum = accum / total
            att_ref[lanes, :] = accum
            low_ref[:, :, lanes] = accum.T.astype(bf16).reshape(low_ref.shape[:2] + (head_dim,))
            log_ref[head : head + 1, :] = top + jnp.log(total)
        else:
            sum_ref, top_ref, total_ref = rest
            sum_ref[lanes, :] = accum
            top_ref[head : head + 1, :] = top
            total_ref[head : head + 1, :] = total


def attend_back_kernel(blocks, heads, head_dim, factor, *refs):
    q_ref, qmask_ref, grad_ref, att_ref, log_ref = refs[:5]
    kv_refs = refs[5 : 5 + blocks]
    mask_refs = refs[5 + blocks : 5 + 2 * blocks]
    dq_ref = refs[5 + 2 * blocks]
    out_refs = refs[6 + 2 * blocks :]
    cols = heads * head_dim
    for head in range(heads):
        lanes = slice(head * head_dim, (head + 1) * head_dim)
        value_lanes = slice(cols + head * head_dim, cols + (head + 1) * head_dim)
        grad = grad_ref[:, :, lanes].reshape(-1, head_dim)
        query = q_ref[:, lanes] * factor
        delta = jnp.sum(grad.astype(f32).T * att_ref[lanes, :], axis=0, keepdims=True)
        log_total = log_ref[head : head + 1, :]
        dq = None
        for kv_ref, mask_ref, out_ref in zip(kv_refs, mask_refs, out_refs):
            scores = transposed_scores(kv_ref, mask_ref, q_ref, qmask_ref, lanes, factor)
            probs = jnp.exp(scores - log_total)
            grad_probs = matmul_t(kv_ref[:, value_lanes], grad)
            grad_scores = (probs * (grad_probs - delta)).astype(bf16)
            out_ref[:, value_lanes] = matmul(probs.astype(bf16), grad).astype(out_ref.dtype)
            out_ref[:, lanes] = matmul(grad_scores, query).astype(out_ref.dtype)
            product = matmul_tn(kv_ref[:, lanes], grad_scores)
            dq = product if dq is None else dq + product
        dq_ref[:, lanes] = dq.T * factor


def pack_kernel(
    groups,
    query_ref,
    key_ref,
    value_ref,
    output_ref,
    gain_one_ref,
    gain_two_ref,
    router_ref,
    seg_ref,
    packed_ref,
):
    rows = query_ref.shape[0]
    cols = query_ref.shape[1] // groups
    wide = packed_ref.shape[2]
    across = lax.broadcasted_iota(jnp.int32, (rows, rows), 1)
    same = across == lax.broadcasted_iota(jnp.int32, (rows, rows), 0)

    def column(ref):
        return jnp.sum(jnp.where(same, ref[...].astype(f32), 0.0), axis=1, keepdims=True)

    extra = (column(gain_one_ref), column(gain_two_ref), router_ref[...].astype(f32))
    used = 4 * cols + 2 + router_ref.shape[1]
    numbers = seg_ref[...].astype(f32)
    numbers = jnp.concatenate((numbers, jnp.zeros((1, wide - numbers.shape[1]), f32)), axis=1)
    for head in range(groups):
        lanes = slice(head * cols, (head + 1) * cols)
        mats = tuple(
            ref[:, lanes].astype(f32) for ref in (query_ref, key_ref, value_ref, output_ref)
        )
        block = jnp.concatenate(mats + extra + (jnp.zeros((rows, wide - used), f32),), axis=1)
        block = jnp.concatenate((block, numbers, jnp.zeros((7 - rows, wide), f32)), axis=0)
        block = block.astype(bf16)
        for place in range(head, packed_ref.shape[0], groups):
            packed_ref[place] = block


def front_kernel(
    cols,
    place_ref,
    pick_ref,
    held_ref,
    other_ref,
    r0_ref,
    r1_ref,
    r2_ref,
    r3_ref,
    mat_ref,
    out_ref,
    extra_ref,
    gain_ref,
    rows_ref,
    normed_ref,
    q_ref,
    kv_ref,
):
    head_place = place_ref[0]
    held = jnp.concatenate((held_ref[...], other_ref[...]), axis=0)
    weights = matmul(pick_ref[...], held.reshape(-1, held.shape[2])).astype(bf16)
    mat = weights[:, : 3 * cols]
    mat_ref[...] = mat
    out_ref[...] = weights[:, 3 * cols : 4 * cols]
    extra = weights[:, 4 * cols : 4 * cols + 64]
    extra_ref[...] = extra
    gains = extra.astype(f32).T[:8]
    gain_ref[...] = gains
    part = r0_ref.shape[0]
    for step, ref in enumerate((r0_ref, r1_ref, r2_ref, r3_ref)):
        start = (head_place + GROUPS - step) % GROUPS * part
        rows_ref[pl.ds(pl.multiple_of(start, part), part), :] = ref[...]
    rows = rows_ref[...].astype(f32)
    normed = (rows * inverse_rms(rows) * gains[0:1]).astype(bf16)
    normed_ref[...] = normed
    qkv = matmul(normed, mat).astype(bf16)
    q_ref[...] = qkv[:, :cols]
    kv_ref[...] = qkv[:, cols:]


def chosen_lane(expert_ref, lanes):
    lane = lax.broadcasted_iota(jnp.int32, (expert_ref.shape[0], lanes), 1)
    return (lane == expert_ref[...] + 2).astype(f32)


def slot_matrix(keys_ref, slots):
    slot = lax.broadcasted_iota(jnp.int32, (slots, keys_ref.shape[1]), 0)
    return (slot == keys_ref[...]).astype(bf16)


def route_kernel(
    experts,
    place_ref,
    att_ref,
    w0_ref,
    w1_ref,
    w2_ref,
    w3_ref,
    in_ref,
    cot_ref,
    gain_ref,
    extra_ref,
    expert_ref,
    keys_ref,
    sent_ref,
    hidden_ref,
    normed_ref,
    probs_ref,
):
    head_place = place_ref[0]
    mixed = jnp.concatenate([att_ref[i] for i in range(GROUPS)], axis=1)
    pieces = [matmul(mixed, ref[...]) for ref in (w0_ref, w1_ref, w2_ref, w3_ref)]
    columns = []
    for spot in range(GROUPS):
        value = pieces[0]
        for step in range(1, GROUPS):
            value = jnp.where((head_place + GROUPS - step) % GROUPS == spot, pieces[step], value)
        columns.append(value)
    hidden = in_ref[...].astype(f32) + jnp.concatenate(columns, axis=1)
    hidden_ref[...] = hidden
    normed = (hidden * inverse_rms(hidden) * gain_ref[1:2]).astype(bf16)
    normed_ref[...] = normed
    logits = matmul(normed, extra_ref[...])
    lane = lax.broadcasted_iota(jnp.int32, logits.shape, 1)
    logits = jnp.where((lane >= 2) & (lane < 2 + experts), logits, MASKED)
    terms = jnp.exp(logits - jnp.max(logits, axis=1, keepdims=True))
    probs = terms / jnp.sum(terms, axis=1, keepdims=True)
    probs_ref[...] = probs
    gate = jnp.sum(probs * chosen_lane(expert_ref, probs.shape[1]), axis=1, keepdims=True)
    grad_expert = (gate * cot_ref[...].astype(f32)).astype(bf16)
    width = normed.shape[1]
    slots = slot_matrix(keys_ref, sent_ref.shape[0])
    sent_ref[:, :width] = matmul(slots, normed).astype(bf16)
    sent_ref[:, width:] = matmul(slots, grad_expert).astype(bf16)


def return_kernel(
    experts,
    place_ref,
    back_ref,
    w0_ref,
    w1_ref,
    w2_ref,
    w3_ref,
    hidden_ref,
    cot_ref,
    probs_ref,
    gain_ref,
    extra_ref,
    expert_ref,
    keys_ref,
    outputs_ref,
    grad_ref,
    pair_ref,
    logits_ref,
    gain_sum_ref,
):
    head_place = place_ref[0]
    width = hidden_ref.shape[1]
    cols = width // GROUPS
    back = matmul_tn(slot_matrix(keys_ref, back_ref.shape[0]), back_ref[...])
    expert_tok, grad_routed = back[:, :width], back[:, width:]
    hidden = hidden_ref[...]
    grad_out = cot_ref[...].astype(f32)
    probs = probs_ref[...]
    chosen = chosen_lane(expert_ref, probs.shape[1])
    gate = jnp.sum(probs * chosen, axis=1, keepdims=True)
    outputs_ref[...] = (hidden + gate * expert_tok).astype(bf16)
    grad_gate = jnp.sum(grad_out * expert_tok, axis=1, keepdims=True)
    grad_logits = (probs * (chosen - gate) * grad_gate).astype(bf16)
    logits_ref[...] = grad_logits
    grad_normed = grad_routed + matmul_t(grad_logits, extra_ref[...])
    scale = inverse_rms(hidden)
    gain_sum_ref[...] = jnp.sum(grad_normed * hidden * scale, axis=0, keepdims=True)
    grad_hidden = grad_out + norm_back(hidden, scale, grad_normed, gain_ref[1:2])
    grad_ref[...] = grad_hidden
    branch = grad_hidden.astype(bf16)
    grad_mixed = None
    for step, ref in enumerate((w0_ref, w1_ref, w2_ref, w3_ref)):
        block = branch[:, :cols]
        for spot in range(1, GROUPS):
            block = jnp.where(
                (head_place + GROUPS - step) % GROUPS == spot,
                branch[:, spot * cols : (spot + 1) * cols],
                block,
            )
        product = matmul_t(block, ref[...])
        grad_mixed = product if grad_mixed is None else grad_mixed + product
    for spot in range(GROUPS):
        lanes = slice(spot * cols, (spot + 1) * cols)
        pair_ref[spot, :, :cols] = grad_mixed[:, lanes].astype(bf16)
        pair_ref[spot, :, cols:] = branch[:, lanes]


def expert_kernel(expert, blocks, part, width, *refs):
    row_refs = refs[:blocks]
    in_ref, out_ref = refs[blocks : blocks + 2]
    own_ref, away_ref, rows_ref, act_ref, pre_ref = refs[blocks + 2 :]
    for place, row_ref in enumerate(row_refs):
        rows_ref[pl.ds(place * part, part), :] = row_ref[...]
    before_act = matmul(rows_ref[:, :width], in_ref[expert])
    grad_act = matmul_t(rows_ref[:, width:], out_ref[expert])
    square = before_act * before_act
    inner = jnp.tanh(0.7978845608028654 * (before_act + 0.044715 * square * before_act))
    half = 0.5 * (1.0 + inner)
    act_ref[...] = (before_act * half).astype(bf16)
    slope = half + (0.5 * 0.7978845608028654) * before_act * (1.0 - inner * inner) * (
        1.0 + (3 * 0.044715) * square
    )
    pre_ref[...] = (grad_act * slope).astype(bf16)
    part_out = matmul(act_ref[...], out_ref[expert])
    part_back = matmul_t(pre_ref[...], in_ref[expert])
    half = own_ref.shape[0]
    for rows, part_ref in ((slice(half, None), away_ref), (slice(0, half), own_ref)):
        part_ref[:, :width] = part_out[rows].astype(bf16)
        part_ref[:, width:] = part_back[rows].astype(bf16)


def expert_grad_kernel(experts, width, *refs):
    in_ref, out_ref = refs[3 * experts :]
    for expert in range(experts):
        rows_ref, act_ref, pre_ref = refs[3 * expert : 3 * expert + 3]
        out_ref[expert] = matmul_tn(act_ref[...], rows_ref[:, width:])
        in_ref[expert] = matmul_tn(rows_ref[:, :width], pre_ref[...])


def weight_sums(sums_ref, three, one_ref, turned_ref, two_ref, spread_ref, logits_ref, *given):
    grad_qkv, products, gain_one, gain_two = given
    four = three + products.shape[1]
    sums_ref[:, :three] = matmul(one_ref[...], grad_qkv).astype(bf16)
    sums_ref[:, three:four] = matmul(turned_ref[...], products).astype(bf16)
    rest = matmul(two_ref[...], logits_ref[...])
    lane = lax.broadcasted_iota(jnp.int32, rest.shape, 1)
    spread = spread_ref[...].astype(f32)
    for index, gain in ((0, gain_one), (1, gain_two)):
        gain = jnp.sum(spread * gain, axis=1, keepdims=True)
        rest = jnp.where(lane == index, gain, rest)
    rest = jnp.concatenate((rest, jnp.zeros_like(rest)), axis=1)
    sums_ref[:, four:] = rest.astype(bf16)


def tail_kernel(blocks, place_ref, *refs):
    dq_refs, kv_refs = refs[:blocks], refs[blocks : 2 * blocks]
    att_refs = refs[2 * blocks : 3 * blocks]
    mat_ref, rows_ref, pair_ref, gain_two_ref, logits_ref = refs[3 * blocks : 3 * blocks + 5]
    own_mats, away_mats = refs[3 * blocks + 5 : 3 * blocks + 9], refs[3 * blocks + 9 : 3 * blocks + 13]
    away_ref, own_ref = refs[3 * blocks + 13 : 3 * blocks + 15]
    part_refs = refs[3 * blocks + 15 :]
    head_place = place_ref[0]
    cols = dq_refs[0].shape[1]
    grad_q = dq_refs[0][...]
    for ref in dq_refs[1:]:
        grad_q = grad_q + ref[...]
    grad_kv = kv_refs[0][...]
    for ref in kv_refs[1:]:
        grad_kv = grad_kv + ref[...].astype(f32)
    grad_qkv = jnp.concatenate((grad_q.astype(bf16), grad_kv.astype(bf16)), axis=1)
    part = matmul_t(grad_qkv, mat_ref[...])
    rows = rows_ref[...].astype(f32)
    gain_one = jnp.sum(part * rows * inverse_rms(rows), axis=0, keepdims=True)
    part = part.astype(bf16).astype(f32).reshape(blocks, -1, part.shape[1])
    for step, part_ref in enumerate(part_refs):
        value = part[0]
        for spot in range(1, blocks):
            value = jnp.where((head_place + step) % blocks == spot, part[spot], value)
        part_ref[...] = value.astype(part_ref.dtype)
    branch = pair_ref[:, :, cols:].reshape(-1, cols)
    products = jnp.concatenate(
        [matmul_tn(ref[...].reshape(-1, cols), branch).astype(bf16) for ref in att_refs], axis=0
    )
    for sums_ref, mats in ((away_ref, away_mats), (own_ref, own_mats)):
        weight_sums(
            sums_ref, 3 * cols, *mats, logits_ref, grad_qkv, products, gain_one, gain_two_ref[...]
        )


def sum_kernel(groups, sums_ref, mats_ref, rest_ref):
    rows = rest_ref.shape[0]
    cols = mats_ref.shape[2] // groups
    rest = None
    for head in range(groups):
        total = sums_ref[head].astype(f32)
        for place in range(head + groups, sums_ref.shape[0], groups):
            total = total + sums_ref[place].astype(f32)
        total = total[:rows]
        for mat in range(4):
            mats_ref[mat, :, head * cols : (head + 1) * cols] = total[
                :, mat * cols : (mat + 1) * cols
            ]
        extra = total[:, 4 * cols :]
        rest = extra if rest is None else rest + extra
    rest_ref[...] = rest


def body(
    inputs,
    gain_attn,
    w_query,
    w_key,
    w_value,
    w_output,
    gain_ffn,
    router,
    expert_in,
    expert_out,
    expert_index,
    slot_index,
    segment_ids,
    cotangent,
):
    tok_rows, width = inputs.shape
    head_dim = width // HEADS
    factor = head_dim ** (-0.5)
    cols = width // GROUPS
    heads_here = HEADS // GROUPS
    experts_all = router.shape[1]
    rows_held = w_query.shape[0]
    local_experts = expert_in.shape[0]
    hidden = expert_in.shape[2]
    block_rows = GROUPS * tok_rows

    core = lax.axis_index("core")
    head_place = lax.axis_index("x")
    query_place = lax.axis_index("y")
    ring = jnp.arange(GROUPS, dtype=jnp.int32)

    def core_swap(values):
        return lax.ppermute(values, "core", [(0, 1), (1, 0)])

    def gathered(values, axis):
        return [values] + [shifted(values, axis, step) for step in range(1, GROUPS)]

    input_parts = gathered(inputs, "x")

    wide = 896
    (packed,) = call_kernel(
        functools.partial(pack_kernel, GROUPS),
        (jax.ShapeDtypeStruct((64, 8, wide), bf16),),
        1,
        4,
        w_query,
        w_key,
        w_value,
        w_output,
        gain_attn[None, :],
        gain_ffn[None, :],
        router,
        segment_ids[None, :],
    )
    held = swap_rows(packed, ("z", "y", "x"))
    held_other = core_swap(held)
    feature = jnp.arange(width, dtype=jnp.int32)

    def spread_slot(feature):
        owner = feature // rows_held
        return (owner // 32 * 16 + owner % 16) * 8 + feature % rows_held

    spread_row = jnp.where(feature // rows_held // 16 % 2 == core, 0, 512) + spread_slot(feature)
    place_row = jnp.arange(1024, dtype=jnp.int32)
    halves = (place_row[:512], place_row[512:])
    spread = [(rows[:, None] == spread_row[None, :]).astype(bf16) for rows in halves]
    pick = (spread_row[:, None] == place_row[None, :]).astype(bf16)
    segs = held.reshape(4, 16, 8, wide)[:, :, rows_held, :tok_rows]
    segs = lax.dynamic_index_in_dim(segs, lax.axis_index("z"), axis=0, keepdims=False)
    segs = segs.reshape(GROUPS, GROUPS, tok_rows)
    key_segs = jnp.take(segs, (query_place - ring) % GROUPS, axis=0)
    query_seg = key_segs[0].reshape(block_rows)
    key_segs = key_segs.reshape(GROUPS * block_rows)

    places = head_place.astype(jnp.int32)[None]
    qkv_mat, out_cols, extra, gains, block_inputs, normed_one, queries, kv_own = call_kernel(
        functools.partial(front_kernel, cols),
        (
            shape(width, 3 * cols, bf16),
            shape(width, cols, bf16),
            shape(width, 64, bf16),
            shape(8, width),
            shape(block_rows, width, bf16),
            shape(block_rows, width, bf16),
            shape(block_rows, cols, bf16),
            shape(block_rows, 2 * cols, bf16),
        ),
        4,
        12,
        pick,
        held,
        held_other,
        *input_parts,
        scalars=places,
    )
    kv_blocks = gathered(kv_own, "y")
    out_parts = gathered(out_cols, "x")
    documents = jnp.arange(head_dim, dtype=bf16)[None, :]
    query_mask = (query_seg[:, None] == documents).astype(bf16)
    key_masks = jnp.where((key_segs[:, None] == documents) | (documents > 2), 0.0, MASKED)
    key_masks = key_masks.astype(bf16).reshape(GROUPS, block_rows, head_dim)
    key_masks = [key_masks[i] for i in range(GROUPS)]
    sizes = (heads_here, head_dim, factor)
    state = call_kernel(
        functools.partial(attend_kernel, True, False, 1, *sizes),
        (shape(cols, block_rows), shape(8, block_rows), shape(8, block_rows)),
        2,
        8,
        queries,
        query_mask,
        kv_own,
        key_masks[0],
    )
    attended, att_low, log_total = call_kernel(
        functools.partial(attend_kernel, False, True, GROUPS - 1, *sizes),
        (
            shape(cols, block_rows),
            jax.ShapeDtypeStruct((GROUPS, tok_rows, cols), bf16),
            shape(8, block_rows),
        ),
        6,
        8,
        queries,
        query_mask,
        *kv_blocks[1:],
        *key_masks[1:],
        *state,
    )
    mixed_parts = swap_rows(att_low, "x")
    att_parts = gathered(att_low, "x")
    expert_col = expert_index[:, None]
    slot_row = expert_index // local_experts * 16 + expert_index % local_experts * 8 + slot_index
    keys = slot_row[None, :]
    slots = 16 * 16
    sent, hidden_one, normed_two, router_probs = call_kernel(
        functools.partial(route_kernel, experts_all),
        (
            shape(slots, 2 * width, bf16),
            shape(tok_rows, width),
            shape(tok_rows, width, bf16),
            shape(tok_rows, 64),
        ),
        3,
        6,
        mixed_parts,
        *out_parts,
        inputs,
        cotangent,
        gains,
        extra,
        expert_col,
        keys,
        scalars=places,
    )

    dev_rows = 16 * CAPACITY
    dense = jnp.arange(dev_rows, dtype=jnp.int32)
    squeeze = [
        (
            (dense // CAPACITY * 16 + expert * 8 + dense % CAPACITY)[:, None]
            == jnp.arange(slots, dtype=jnp.int32)[None, :]
        ).astype(bf16)
        for expert in range(local_experts)
    ]

    def seq_swap(values):
        values = values.reshape(16, slots // 16, 2 * width)
        return swap_rows(values, ("y", "x")).reshape(slots, 2 * width)

    half_block = shape(4 * dev_rows, 2 * width, bf16)
    all_rows = 8 * dev_rows
    act_shape = shape(all_rows, hidden, bf16)
    arrived = seq_swap(sent)
    arrived = [matmul(mat, arrived).astype(bf16) for mat in squeeze]
    kept, home = [], []
    for expert in range(local_experts):
        z_rows = gathered(arrived[expert], "z")
        if expert + 1 < local_experts:
            *z_rows, arrived[expert + 1] = lax.optimization_barrier(
                (*z_rows, arrived[expert + 1])
            )
        row_blocks = z_rows + [core_swap(rows) for rows in z_rows]
        own_parts, away_parts, rows_all, activated, grad_pre = call_kernel(
            functools.partial(expert_kernel, expert, 8, dev_rows, width),
            (half_block, half_block, shape(all_rows, 2 * width, bf16), act_shape, act_shape),
            5,
            8,
            *row_blocks,
            expert_in,
            expert_out,
        )
        kept += [rows_all, activated, grad_pre]
        chip_sums = own_parts.astype(f32) + core_swap(away_parts).astype(f32)
        total = chip_sums[:dev_rows]
        for step in range(1, 4):
            far = chip_sums[step * dev_rows : (step + 1) * dev_rows].astype(bf16)
            total = total + shifted(far, "z", 4 - step).astype(f32)
        home.append(total.astype(bf16))
    d_expert_in, d_expert_out = call_kernel(
        functools.partial(expert_grad_kernel, local_experts, width),
        (
            jax.ShapeDtypeStruct(expert_in.shape, f32),
            jax.ShapeDtypeStruct(expert_out.shape, f32),
        ),
        4,
        8,
        *kept,
    )
    home, d_expert_in, d_expert_out = lax.optimization_barrier((home, d_expert_in, d_expert_out))
    back = seq_swap(
        sum(matmul_tn(mat, rows) for mat, rows in zip(squeeze, home)).astype(bf16)
    )

    outputs, grad_hidden, pair, grad_logits, d_gain_ffn = call_kernel(
        functools.partial(return_kernel, experts_all),
        (
            shape(tok_rows, width, bf16),
            shape(tok_rows, width),
            jax.ShapeDtypeStruct((GROUPS, tok_rows, 2 * cols), bf16),
            shape(tok_rows, 64, bf16),
            shape(1, width),
        ),
        3,
        6,
        back,
        *out_parts,
        hidden_one,
        cotangent,
        router_probs,
        gains,
        extra,
        expert_col,
        keys,
        scalars=places,
    )

    pair = swap_rows(pair, "x")
    dq_parts, kv_parts = [], []
    for step in (2, 1, 3, 0):
        dq, kv_part = call_kernel(
            functools.partial(attend_back_kernel, 1, *sizes),
            (shape(block_rows, cols), shape(block_rows, 2 * cols, bf16 if step else f32)),
            3,
            8,
            queries,
            query_mask,
            pair,
            attended,
            log_total,
            kv_blocks[step],
            key_masks[step],
        )
        dq_parts.append(dq)
        kv_parts.append(shifted(kv_part, "y", GROUPS - step) if step else kv_part)
    kv_parts = kv_parts[::-1]

    turned_feature = (head_place - feature // cols) % GROUPS * cols + feature % cols
    turned_row = jnp.where(turned_feature // rows_held // 16 % 2 == core, 0, 512)
    turned_row = turned_row + spread_slot(turned_feature)
    shared = [
        (
            matmul_t(spread_half, normed_one).astype(bf16),
            (rows[:, None] == turned_row[None, :]).astype(bf16),
            matmul_t(spread_half, normed_two).astype(bf16),
            spread_half,
        )
        for spread_half, rows in zip(spread, halves)
    ]
    sums_shape = shape(512, wide, bf16)
    part_shape = shape(tok_rows, width, bf16)
    away_sums, own_sums, *normed_parts = call_kernel(
        functools.partial(tail_kernel, GROUPS),
        (sums_shape, sums_shape) + (part_shape,) * GROUPS,
        5,
        12,
        *dq_parts,
        *kv_parts,
        *att_parts,
        qkv_mat,
        block_inputs,
        pair,
        d_gain_ffn,
        grad_logits,
        *shared[0],
        *shared[1],
        scalars=places,
    )
    chip_sums = own_sums.astype(f32) + core_swap(away_sums).astype(f32)
    sums = swap_rows(chip_sums.astype(bf16).reshape(64, 8, wide), ("z", "y", "x"))
    grad_normed_one = normed_parts[0].astype(f32)
    for step in range(1, GROUPS):
        grad_normed_one = grad_normed_one + shifted(normed_parts[step], "x", step).astype(f32)
    mats, rest = call_kernel(
        functools.partial(sum_kernel, GROUPS),
        (
            jax.ShapeDtypeStruct((4, rows_held, width), f32),
            shape(rows_held, 896 - 4 * cols),
        ),
        1,
        4,
        sums,
    )

    inputs_f = inputs.astype(f32)
    d_inputs = grad_hidden + norm_back(
        inputs_f, inverse_rms(inputs_f), grad_normed_one, gains[0:1]
    )
    return (
        outputs,
        d_inputs,
        rest[:, 0],
        mats[0],
        mats[1],
        mats[2],
        mats[3],
        rest[:, 1],
        rest[:, 2 : 2 + experts_all],
        d_expert_in,
        d_expert_out,
    )


def solution(mesh):
    mesh = Mesh(mesh.devices.reshape(SIZES), ALL)
    dp = ("z", "core")
    seq = ("y", "x")
    rows = P(ALL, None)
    in_specs = (
        rows,
        P(ALL),
        rows,
        rows,
        rows,
        rows,
        P(ALL),
        rows,
        P(seq, None, dp),
        P(seq, dp, None),
        P(ALL),
        P(ALL),
        P(ALL),
        rows,
    )
    out_specs = (
        rows,
        rows,
        P(ALL),
        rows,
        rows,
        rows,
        rows,
        P(ALL),
        rows,
        P(seq, None, dp),
        P(seq, dp, None),
    )
    return jax.shard_map(body, mesh=mesh, in_specs=in_specs, out_specs=out_specs, check_vma=False)
```

```python
import functools

import jax
import jax.numpy as jnp
from jax import lax
from jax.experimental import pallas as pl
from jax.experimental.pallas import tpu as pltpu
from jax.sharding import Mesh
from jax.sharding import PartitionSpec as P

HEADS = 12
GROUPS = 4
CAPACITY = 5
EPSILON = 1e-06
ALL = ("z", "core", "y", "x")
SIZES = (4, 2, 4, 4)

f32 = jnp.float32
bf16 = jnp.bfloat16


def shifted(values, axis, step):
    return lax.ppermute(values, axis, [(i, (i + step) % 4) for i in range(4)])


def swap_rows(values, axes):
    return lax.all_to_all(values, axes, split_axis=0, concat_axis=0, tiled=True)


def matmul(a, b):
    return jnp.dot(a, b, preferred_element_type=f32)


def matmul_t(a, b):
    return lax.dot_general(a, b, (((1,), (1,)), ((), ())), preferred_element_type=f32)


def matmul_tn(a, b):
    return lax.dot_general(a, b, (((0,), (0,)), ((), ())), preferred_element_type=f32)


def inverse_rms(values):
    return lax.rsqrt(jnp.mean(values * values, axis=-1, keepdims=True) + EPSILON)


def norm_back(values, scale, grad, gain_vec):
    u = grad * gain_vec
    return scale * u - values * (scale * scale * scale) * jnp.mean(
        u * values, axis=-1, keepdims=True
    )

MASKED = -1e30
MIB = 1024 * 1024


def call_kernel(kernel, out_shapes, micros, scratch_mib, *operands, scalars=None, whole=False):
    moved = sum(v.size * v.dtype.itemsize for v in operands)
    moved += sum(v.size * v.dtype.itemsize for v in out_shapes)
    in_specs = [pl.BlockSpec(memory_space=pltpu.VMEM)] * len(operands)
    if scalars is not None:
        in_specs = [pl.BlockSpec(memory_space=pltpu.SMEM)] + in_specs
        operands = (scalars,) + operands
    return pl.pallas_call(
        kernel,
        out_shape=out_shapes,
        in_specs=in_specs,
        out_specs=[pl.BlockSpec(memory_space=pltpu.VMEM)] * len(out_shapes),
        compiler_params=pltpu.CompilerParams(
            vmem_limit_bytes=(58 if whole else moved * 4 // 3 // MIB + 2 + scratch_mib) * MIB
        ),
        cost_estimate=pl.CostEstimate(
            flops=int(micros * 1.1e9), bytes_accessed=moved, transcendentals=0
        ),
    )(*operands)


def shape(rows, columns, dtype=f32):
    return jax.ShapeDtypeStruct((rows, columns), dtype)


def transposed_scores(k_ref, kmask_ref, q_ref, qmask_ref, lanes, factor):
    key_side = jnp.concatenate((k_ref[:, lanes], kmask_ref[...]), axis=1)
    query_side = jnp.concatenate((q_ref[:, lanes] * factor, qmask_ref[...]), axis=1)
    return matmul_t(key_side, query_side)


def attend_kernel(first, last, blocks, heads, head_dim, factor, *refs):
    q_ref, qmask_ref = refs[:2]
    kv_refs = refs[2 : 2 + blocks]
    mask_refs = refs[2 + blocks : 2 + 2 * blocks]
    rest = refs[2 + 2 * blocks :]
    if not first:
        old_sum, old_top, old_total = rest[:3]
        rest = rest[3:]
    cols = heads * head_dim
    for head in range(heads):
        lanes = slice(head * head_dim, (head + 1) * head_dim)
        value_lanes = slice(cols + head * head_dim, cols + (head + 1) * head_dim)
        if first:
            top = total = accum = None
        else:
            top = old_top[head : head + 1, :]
            total = old_total[head : head + 1, :]
            accum = old_sum[lanes, :]
        for kv_ref, mask_ref in zip(kv_refs, mask_refs):
            scores = transposed_scores(kv_ref, mask_ref, q_ref, qmask_ref, lanes, factor)
            newest = jnp.max(scores, axis=0, keepdims=True)
            if top is not None:
                newest = jnp.maximum(top, newest)
            terms = jnp.exp(scores - newest)
            term_sum = jnp.sum(terms, axis=0, keepdims=True)
            product = matmul_tn(kv_ref[:, value_lanes], terms.astype(bf16))
            if top is None:
                total, accum = term_sum, product
            else:
                shrink = jnp.exp(top - newest)
                total = total * shrink + term_sum
                accum = accum * shrink + product
            top = newest
        if last:
            att_ref, low_ref, log_ref = rest
            accum = accum / total
            att_ref[lanes, :] = accum
            low_ref[:, :, lanes] = accum.T.astype(bf16).reshape(low_ref.shape[:2] + (head_dim,))
            log_ref[head : head + 1, :] = top + jnp.log(total)
        else:
            sum_ref, top_ref, total_ref = rest
            sum_ref[lanes, :] = accum
            top_ref[head : head + 1, :] = top
            total_ref[head : head + 1, :] = total


def attend_back_kernel(blocks, heads, head_dim, factor, *refs):
    q_ref, qmask_ref, grad_ref, att_ref, log_ref = refs[:5]
    kv_refs = refs[5 : 5 + blocks]
    mask_refs = refs[5 + blocks : 5 + 2 * blocks]
    dq_ref = refs[5 + 2 * blocks]
    out_refs = refs[6 + 2 * blocks :]
    cols = heads * head_dim
    for head in range(heads):
        lanes = slice(head * head_dim, (head + 1) * head_dim)
        value_lanes = slice(cols + head * head_dim, cols + (head + 1) * head_dim)
        grad = grad_ref[:, :, lanes].reshape(-1, head_dim)
        query = q_ref[:, lanes] * factor
        delta = jnp.sum(grad.astype(f32).T * att_ref[lanes, :], axis=0, keepdims=True)
        log_total = log_ref[head : head + 1, :]
        dq = None
        for kv_ref, mask_ref, out_ref in zip(kv_refs, mask_refs, out_refs):
            scores = transposed_scores(kv_ref, mask_ref, q_ref, qmask_ref, lanes, factor)
            probs = jnp.exp(scores - log_total)
            grad_probs = matmul_t(kv_ref[:, value_lanes], grad)
            grad_scores = (probs * (grad_probs - delta)).astype(bf16)
            out_ref[:, value_lanes] = matmul(probs.astype(bf16), grad).astype(out_ref.dtype)
            out_ref[:, lanes] = matmul(grad_scores, query).astype(out_ref.dtype)
            product = matmul_tn(kv_ref[:, lanes], grad_scores)
            dq = product if dq is None else dq + product
        dq_ref[:, lanes] = dq.T * factor


def pack_kernel(
    groups,
    query_ref,
    key_ref,
    value_ref,
    output_ref,
    gain_one_ref,
    gain_two_ref,
    router_ref,
    seg_ref,
    packed_ref,
):
    rows = query_ref.shape[0]
    cols = query_ref.shape[1] // groups
    wide = packed_ref.shape[2]
    across = lax.broadcasted_iota(jnp.int32, (rows, rows), 1)
    same = across == lax.broadcasted_iota(jnp.int32, (rows, rows), 0)

    def column(ref):
        return jnp.sum(jnp.where(same, ref[...].astype(f32), 0.0), axis=1, keepdims=True)

    extra = (column(gain_one_ref), column(gain_two_ref), router_ref[...].astype(f32))
    used = 4 * cols + 2 + router_ref.shape[1]
    numbers = seg_ref[...].astype(f32)
    numbers = jnp.concatenate((numbers, jnp.zeros((1, wide - numbers.shape[1]), f32)), axis=1)
    for head in range(groups):
        lanes = slice(head * cols, (head + 1) * cols)
        mats = tuple(
            ref[:, lanes].astype(f32) for ref in (query_ref, key_ref, value_ref, output_ref)
        )
        block = jnp.concatenate(mats + extra + (jnp.zeros((rows, wide - used), f32),), axis=1)
        block = jnp.concatenate((block, numbers, jnp.zeros((7 - rows, wide), f32)), axis=0)
        block = block.astype(bf16)
        for place in range(head, packed_ref.shape[0], groups):
            packed_ref[place] = block


def front_kernel(
    cols,
    place_ref,
    pick_ref,
    held_ref,
    other_ref,
    r0_ref,
    r1_ref,
    r2_ref,
    r3_ref,
    mat_ref,
    out_ref,
    extra_ref,
    gain_ref,
    rows_ref,
    normed_ref,
    q_ref,
    kv_ref,
):
    head_place = place_ref[0]
    held = jnp.concatenate((held_ref[...], other_ref[...]), axis=0)
    weights = matmul(pick_ref[...], held.reshape(-1, held.shape[2])).astype(bf16)
    mat = weights[:, : 3 * cols]
    mat_ref[...] = mat
    out_ref[...] = weights[:, 3 * cols : 4 * cols]
    extra = weights[:, 4 * cols : 4 * cols + 64]
    extra_ref[...] = extra
    gains = extra.astype(f32).T[:8]
    gain_ref[...] = gains
    part = r0_ref.shape[0]
    for step, ref in enumerate((r0_ref, r1_ref, r2_ref, r3_ref)):
        start = (head_place + GROUPS - step) % GROUPS * part
        rows_ref[pl.ds(pl.multiple_of(start, part), part), :] = ref[...]
    rows = rows_ref[...].astype(f32)
    normed = (rows * inverse_rms(rows) * gains[0:1]).astype(bf16)
    normed_ref[...] = normed
    qkv = matmul(normed, mat).astype(bf16)
    q_ref[...] = qkv[:, :cols]
    kv_ref[...] = qkv[:, cols:]


def chosen_lane(expert_ref, lanes):
    lane = lax.broadcasted_iota(jnp.int32, (expert_ref.shape[0], lanes), 1)
    return (lane == expert_ref[...] + 2).astype(f32)


def slot_matrix(keys_ref, slots):
    slot = lax.broadcasted_iota(jnp.int32, (slots, keys_ref.shape[1]), 0)
    return (slot == keys_ref[...]).astype(bf16)


def route_kernel(
    experts,
    place_ref,
    att_ref,
    w0_ref,
    w1_ref,
    w2_ref,
    w3_ref,
    in_ref,
    cot_ref,
    gain_ref,
    extra_ref,
    expert_ref,
    keys_ref,
    sent_ref,
    hidden_ref,
    normed_ref,
    probs_ref,
):
    head_place = place_ref[0]
    mixed = jnp.concatenate([att_ref[i] for i in range(GROUPS)], axis=1)
    pieces = [matmul(mixed, ref[...]) for ref in (w0_ref, w1_ref, w2_ref, w3_ref)]
    columns = []
    for spot in range(GROUPS):
        value = pieces[0]
        for step in range(1, GROUPS):
            value = jnp.where((head_place + GROUPS - step) % GROUPS == spot, pieces[step], value)
        columns.append(value)
    hidden = in_ref[...].astype(f32) + jnp.concatenate(columns, axis=1)
    hidden_ref[...] = hidden
    normed = (hidden * inverse_rms(hidden) * gain_ref[1:2]).astype(bf16)
    normed_ref[...] = normed
    logits = matmul(normed, extra_ref[...])
    lane = lax.broadcasted_iota(jnp.int32, logits.shape, 1)
    logits = jnp.where((lane >= 2) & (lane < 2 + experts), logits, MASKED)
    terms = jnp.exp(logits - jnp.max(logits, axis=1, keepdims=True))
    probs = terms / jnp.sum(terms, axis=1, keepdims=True)
    probs_ref[...] = probs
    gate = jnp.sum(probs * chosen_lane(expert_ref, probs.shape[1]), axis=1, keepdims=True)
    grad_expert = (gate * cot_ref[...].astype(f32)).astype(bf16)
    width = normed.shape[1]
    slots = slot_matrix(keys_ref, sent_ref.shape[0])
    sent_ref[:, :width] = matmul(slots, normed).astype(bf16)
    sent_ref[:, width:] = matmul(slots, grad_expert).astype(bf16)


def return_kernel(
    experts,
    place_ref,
    back_ref,
    w0_ref,
    w1_ref,
    w2_ref,
    w3_ref,
    hidden_ref,
    cot_ref,
    probs_ref,
    gain_ref,
    extra_ref,
    expert_ref,
    keys_ref,
    outputs_ref,
    grad_ref,
    pair_ref,
    logits_ref,
    gain_sum_ref,
):
    head_place = place_ref[0]
    width = hidden_ref.shape[1]
    cols = width // GROUPS
    back = matmul_tn(slot_matrix(keys_ref, back_ref.shape[0]), back_ref[...])
    expert_tok, grad_routed = back[:, :width], back[:, width:]
    hidden = hidden_ref[...]
    grad_out = cot_ref[...].astype(f32)
    probs = probs_ref[...]
    chosen = chosen_lane(expert_ref, probs.shape[1])
    gate = jnp.sum(probs * chosen, axis=1, keepdims=True)
    outputs_ref[...] = (hidden + gate * expert_tok).astype(bf16)
    grad_gate = jnp.sum(grad_out * expert_tok, axis=1, keepdims=True)
    grad_logits = (probs * (chosen - gate) * grad_gate).astype(bf16)
    logits_ref[...] = grad_logits
    grad_normed = grad_routed + matmul_t(grad_logits, extra_ref[...])
    scale = inverse_rms(hidden)
    gain_sum_ref[...] = jnp.sum(grad_normed * hidden * scale, axis=0, keepdims=True)
    grad_hidden = grad_out + norm_back(hidden, scale, grad_normed, gain_ref[1:2])
    grad_ref[...] = grad_hidden
    branch = grad_hidden.astype(bf16)
    grad_mixed = None
    for step, ref in enumerate((w0_ref, w1_ref, w2_ref, w3_ref)):
        block = branch[:, :cols]
        for spot in range(1, GROUPS):
            block = jnp.where(
                (head_place + GROUPS - step) % GROUPS == spot,
                branch[:, spot * cols : (spot + 1) * cols],
                block,
            )
        product = matmul_t(block, ref[...])
        grad_mixed = product if grad_mixed is None else grad_mixed + product
    for spot in range(GROUPS):
        lanes = slice(spot * cols, (spot + 1) * cols)
        pair_ref[spot, :, :cols] = grad_mixed[:, lanes].astype(bf16)
        pair_ref[spot, :, cols:] = branch[:, lanes]


def expert_kernel(expert, blocks, part, width, *refs):
    row_refs = refs[:blocks]
    in_ref, out_ref = refs[blocks : blocks + 2]
    own_ref, away_ref, rows_ref, act_ref, pre_ref = refs[blocks + 2 :]
    for place, row_ref in enumerate(row_refs):
        rows_ref[pl.ds(place * part, part), :] = row_ref[...]
    before_act = matmul(rows_ref[:, :width], in_ref[expert])
    grad_act = matmul_t(rows_ref[:, width:], out_ref[expert])
    square = before_act * before_act
    inner = jnp.tanh(0.7978845608028654 * (before_act + 0.044715 * square * before_act))
    half = 0.5 * (1.0 + inner)
    act_ref[...] = (before_act * half).astype(bf16)
    slope = half + (0.5 * 0.7978845608028654) * before_act * (1.0 - inner * inner) * (
        1.0 + (3 * 0.044715) * square
    )
    pre_ref[...] = (grad_act * slope).astype(bf16)
    part_out = matmul(act_ref[...], out_ref[expert])
    part_back = matmul_t(pre_ref[...], in_ref[expert])
    half = own_ref.shape[0]
    for rows, part_ref in ((slice(half, None), away_ref), (slice(0, half), own_ref)):
        part_ref[:, :width] = part_out[rows].astype(bf16)
        part_ref[:, width:] = part_back[rows].astype(bf16)


def expert_grad_kernel(experts, width, *refs):
    in_ref, out_ref = refs[3 * experts :]
    for expert in range(experts):
        rows_ref, act_ref, pre_ref = refs[3 * expert : 3 * expert + 3]
        out_ref[expert] = matmul_tn(act_ref[...], rows_ref[:, width:])
        in_ref[expert] = matmul_tn(rows_ref[:, :width], pre_ref[...])


def weight_sums(sums_ref, three, one_ref, turned_ref, two_ref, spread_ref, logits_ref, *given):
    grad_qkv, products, gain_one, gain_two = given
    four = three + products.shape[1]
    sums_ref[:, :three] = matmul(one_ref[...], grad_qkv).astype(bf16)
    sums_ref[:, three:four] = matmul(turned_ref[...], products).astype(bf16)
    rest = matmul(two_ref[...], logits_ref[...])
    lane = lax.broadcasted_iota(jnp.int32, rest.shape, 1)
    spread = spread_ref[...].astype(f32)
    for index, gain in ((0, gain_one), (1, gain_two)):
        gain = jnp.sum(spread * gain, axis=1, keepdims=True)
        rest = jnp.where(lane == index, gain, rest)
    rest = jnp.concatenate((rest, jnp.zeros_like(rest)), axis=1)
    sums_ref[:, four:] = rest.astype(bf16)


def tail_kernel(blocks, place_ref, *refs):
    dq_refs, kv_refs = refs[:blocks], refs[blocks : 2 * blocks]
    att_refs = refs[2 * blocks : 3 * blocks]
    mat_ref, rows_ref, pair_ref, gain_two_ref, logits_ref = refs[3 * blocks : 3 * blocks + 5]
    own_mats, away_mats = refs[3 * blocks + 5 : 3 * blocks + 9], refs[3 * blocks + 9 : 3 * blocks + 13]
    away_ref, own_ref = refs[3 * blocks + 13 : 3 * blocks + 15]
    part_refs = refs[3 * blocks + 15 :]
    head_place = place_ref[0]
    cols = dq_refs[0].shape[1]
    grad_q = dq_refs[0][...]
    for ref in dq_refs[1:]:
        grad_q = grad_q + ref[...]
    grad_kv = kv_refs[0][...]
    for ref in kv_refs[1:]:
        grad_kv = grad_kv + ref[...].astype(f32)
    grad_qkv = jnp.concatenate((grad_q.astype(bf16), grad_kv.astype(bf16)), axis=1)
    part = matmul_t(grad_qkv, mat_ref[...])
    rows = rows_ref[...].astype(f32)
    gain_one = jnp.sum(part * rows * inverse_rms(rows), axis=0, keepdims=True)
    part = part.astype(bf16).astype(f32).reshape(blocks, -1, part.shape[1])
    for step, part_ref in enumerate(part_refs):
        value = part[0]
        for spot in range(1, blocks):
            value = jnp.where((head_place + step) % blocks == spot, part[spot], value)
        part_ref[...] = value.astype(part_ref.dtype)
    branch = pair_ref[:, :, cols:].reshape(-1, cols)
    products = jnp.concatenate(
        [matmul_tn(ref[...].reshape(-1, cols), branch).astype(bf16) for ref in att_refs], axis=0
    )
    for sums_ref, mats in ((away_ref, away_mats), (own_ref, own_mats)):
        weight_sums(
            sums_ref, 3 * cols, *mats, logits_ref, grad_qkv, products, gain_one, gain_two_ref[...]
        )


def sum_kernel(groups, sums_ref, mats_ref, rest_ref):
    rows = rest_ref.shape[0]
    cols = mats_ref.shape[2] // groups
    rest = None
    for head in range(groups):
        total = sums_ref[head].astype(f32)
        for place in range(head + groups, sums_ref.shape[0], groups):
            total = total + sums_ref[place].astype(f32)
        total = total[:rows]
        for mat in range(4):
            mats_ref[mat, :, head * cols : (head + 1) * cols] = total[
                :, mat * cols : (mat + 1) * cols
            ]
        extra = total[:, 4 * cols :]
        rest = extra if rest is None else rest + extra
    rest_ref[...] = rest


def body(
    inputs,
    gain_attn,
    w_query,
    w_key,
    w_value,
    w_output,
    gain_ffn,
    router,
    expert_in,
    expert_out,
    expert_index,
    slot_index,
    segment_ids,
    cotangent,
):
    tok_rows, width = inputs.shape
    head_dim = width // HEADS
    factor = head_dim ** (-0.5)
    cols = width // GROUPS
    heads_here = HEADS // GROUPS
    experts_all = router.shape[1]
    rows_held = w_query.shape[0]
    local_experts = expert_in.shape[0]
    hidden = expert_in.shape[2]
    block_rows = GROUPS * tok_rows

    core = lax.axis_index("core")
    head_place = lax.axis_index("x")
    query_place = lax.axis_index("y")
    ring = jnp.arange(GROUPS, dtype=jnp.int32)

    def core_swap(values):
        return lax.ppermute(values, "core", [(0, 1), (1, 0)])

    def gathered(values, axis):
        return [values] + [shifted(values, axis, step) for step in range(1, GROUPS)]

    input_parts = gathered(inputs, "x")

    wide = 896
    (packed,) = call_kernel(
        functools.partial(pack_kernel, GROUPS),
        (jax.ShapeDtypeStruct((64, 8, wide), bf16),),
        1,
        4,
        w_query,
        w_key,
        w_value,
        w_output,
        gain_attn[None, :],
        gain_ffn[None, :],
        router,
        segment_ids[None, :],
        whole=True,
    )
    held = swap_rows(packed, ("z", "y", "x"))
    held_other = core_swap(held)
    feature = jnp.arange(width, dtype=jnp.int32)

    def spread_slot(feature):
        owner = feature // rows_held
        return (owner // 32 * 16 + owner % 16) * 8 + feature % rows_held

    spread_row = jnp.where(feature // rows_held // 16 % 2 == core, 0, 512) + spread_slot(feature)
    place_row = jnp.arange(1024, dtype=jnp.int32)
    halves = (place_row[:512], place_row[512:])
    spread = [(rows[:, None] == spread_row[None, :]).astype(bf16) for rows in halves]
    pick = (spread_row[:, None] == place_row[None, :]).astype(bf16)
    segs = held.reshape(4, 16, 8, wide)[:, :, rows_held, :tok_rows]
    segs = lax.dynamic_index_in_dim(segs, lax.axis_index("z"), axis=0, keepdims=False)
    segs = segs.reshape(GROUPS, GROUPS, tok_rows)
    key_segs = jnp.take(segs, (query_place - ring) % GROUPS, axis=0)
    query_seg = key_segs[0].reshape(block_rows)
    key_segs = key_segs.reshape(GROUPS * block_rows)

    places = head_place.astype(jnp.int32)[None]
    qkv_mat, out_cols, extra, gains, block_inputs, normed_one, queries, kv_own = call_kernel(
        functools.partial(front_kernel, cols),
        (
            shape(width, 3 * cols, bf16),
            shape(width, cols, bf16),
            shape(width, 64, bf16),
            shape(8, width),
            shape(block_rows, width, bf16),
            shape(block_rows, width, bf16),
            shape(block_rows, cols, bf16),
            shape(block_rows, 2 * cols, bf16),
        ),
        4,
        12,
        pick,
        held,
        held_other,
        *input_parts,
        scalars=places,
    )
    kv_blocks = gathered(kv_own, "y")
    out_parts = gathered(out_cols, "x")
    documents = jnp.arange(head_dim, dtype=bf16)[None, :]
    query_mask = (query_seg[:, None] == documents).astype(bf16)
    key_masks = jnp.where((key_segs[:, None] == documents) | (documents > 2), 0.0, MASKED)
    key_masks = key_masks.astype(bf16).reshape(GROUPS, block_rows, head_dim)
    key_masks = [key_masks[i] for i in range(GROUPS)]
    sizes = (heads_here, head_dim, factor)
    state = call_kernel(
        functools.partial(attend_kernel, True, False, 1, *sizes),
        (shape(cols, block_rows), shape(8, block_rows), shape(8, block_rows)),
        2,
        8,
        queries,
        query_mask,
        kv_own,
        key_masks[0],
    )
    state = call_kernel(
        functools.partial(attend_kernel, False, False, 2, *sizes),
        (shape(cols, block_rows), shape(8, block_rows), shape(8, block_rows)),
        4,
        8,
        queries,
        query_mask,
        kv_blocks[1],
        kv_blocks[3],
        key_masks[1],
        key_masks[3],
        *state,
    )
    attended, att_low, log_total = call_kernel(
        functools.partial(attend_kernel, False, True, 1, *sizes),
        (
            shape(cols, block_rows),
            jax.ShapeDtypeStruct((GROUPS, tok_rows, cols), bf16),
            shape(8, block_rows),
        ),
        2,
        8,
        queries,
        query_mask,
        kv_blocks[2],
        key_masks[2],
        *state,
    )
    mixed_parts = swap_rows(att_low, "x")
    expert_col = expert_index[:, None]
    slot_row = expert_index // local_experts * 16 + expert_index % local_experts * 8 + slot_index
    keys = slot_row[None, :]
    slots = 16 * 16
    sent, hidden_one, normed_two, router_probs = call_kernel(
        functools.partial(route_kernel, experts_all),
        (
            shape(slots, 2 * width, bf16),
            shape(tok_rows, width),
            shape(tok_rows, width, bf16),
            shape(tok_rows, 64),
        ),
        3,
        6,
        mixed_parts,
        *out_parts,
        inputs,
        cotangent,
        gains,
        extra,
        expert_col,
        keys,
        scalars=places,
    )

    turned_feature = (head_place - feature // cols) % GROUPS * cols + feature % cols
    turned_row = jnp.where(turned_feature // rows_held // 16 % 2 == core, 0, 512)
    turned_row = turned_row + spread_slot(turned_feature)
    shared = [
        (
            matmul_t(spread_half, normed_one).astype(bf16),
            (rows[:, None] == turned_row[None, :]).astype(bf16),
            matmul_t(spread_half, normed_two).astype(bf16),
            spread_half,
        )
        for spread_half, rows in zip(spread, halves)
    ]

    dev_rows = 16 * CAPACITY
    dense = jnp.arange(dev_rows, dtype=jnp.int32)
    squeeze = [
        (
            (dense // CAPACITY * 16 + expert * 8 + dense % CAPACITY)[:, None]
            == jnp.arange(slots, dtype=jnp.int32)[None, :]
        ).astype(bf16)
        for expert in range(local_experts)
    ]

    def seq_swap(values):
        values = values.reshape(16, slots // 16, 2 * width)
        return swap_rows(values, ("y", "x")).reshape(slots, 2 * width)

    half_block = shape(4 * dev_rows, 2 * width, bf16)
    all_rows = 8 * dev_rows
    act_shape = shape(all_rows, hidden, bf16)
    arrived = seq_swap(sent)
    arrived, att_low = lax.optimization_barrier((arrived, att_low))
    att_parts = gathered(att_low, "x")
    arrived = [matmul(mat, arrived).astype(bf16) for mat in squeeze]
    z_rows = [gathered(arrived[0], "z")]

    z_rows.append(gathered(arrived[1], "z"))

    kept, totals = [], []
    for expert in range(local_experts):
        row_blocks = z_rows[expert] + [core_swap(rows) for rows in z_rows[expert]]
        own_parts, away_parts, *held_back = call_kernel(
            functools.partial(expert_kernel, expert, 8, dev_rows, width),
            (half_block, half_block, shape(all_rows, 2 * width, bf16), act_shape, act_shape),
            5,
            8,
            *row_blocks,
            expert_in,
            expert_out,
        )
        kept += held_back
        totals.append(own_parts.astype(f32) + core_swap(away_parts).astype(f32))
    kept, totals, shared, att_parts = lax.optimization_barrier((kept, totals, shared, att_parts))
    home = []
    for sums in totals:
        total = sums[:dev_rows]
        for step in range(1, 4):
            away = sums[step * dev_rows : (step + 1) * dev_rows].astype(bf16)
            total = total + shifted(away, "z", 4 - step).astype(f32)
        home.append(total.astype(bf16))
    d_expert_in, d_expert_out = call_kernel(
        functools.partial(expert_grad_kernel, local_experts, width),
        (
            jax.ShapeDtypeStruct(expert_in.shape, f32),
            jax.ShapeDtypeStruct(expert_out.shape, f32),
        ),
        4,
        8,
        *kept,
    )
    home, d_expert_in, d_expert_out = lax.optimization_barrier((home, d_expert_in, d_expert_out))
    back = seq_swap(
        sum(matmul_tn(mat, rows) for mat, rows in zip(squeeze, home)).astype(bf16)
    )

    outputs, grad_hidden, pair, grad_logits, d_gain_ffn = call_kernel(
        functools.partial(return_kernel, experts_all),
        (
            shape(tok_rows, width, bf16),
            shape(tok_rows, width),
            jax.ShapeDtypeStruct((GROUPS, tok_rows, 2 * cols), bf16),
            shape(tok_rows, 64, bf16),
            shape(1, width),
        ),
        3,
        6,
        back,
        *out_parts,
        hidden_one,
        cotangent,
        router_probs,
        gains,
        extra,
        expert_col,
        keys,
        scalars=places,
    )

    pair = swap_rows(pair, "x")
    dq_parts, kv_parts = [], []
    for step in (2, 1, 3, 0):
        dq, kv_part = call_kernel(
            functools.partial(attend_back_kernel, 1, *sizes),
            (shape(block_rows, cols), shape(block_rows, 2 * cols, bf16 if step else f32)),
            3,
            8,
            queries,
            query_mask,
            pair,
            attended,
            log_total,
            kv_blocks[step],
            key_masks[step],
        )
        dq_parts.append(dq)
        kv_parts.append(shifted(kv_part, "y", GROUPS - step) if step else kv_part)
    kv_parts = kv_parts[::-1]

    sums_shape = shape(512, wide, bf16)
    part_shape = shape(tok_rows, width, bf16)
    away_sums, own_sums, *normed_parts = call_kernel(
        functools.partial(tail_kernel, GROUPS),
        (sums_shape, sums_shape) + (part_shape,) * GROUPS,
        5,
        12,
        *dq_parts,
        *kv_parts,
        *att_parts,
        qkv_mat,
        block_inputs,
        pair,
        d_gain_ffn,
        grad_logits,
        *shared[0],
        *shared[1],
        scalars=places,
    )
    chip_sums = own_sums.astype(f32) + core_swap(away_sums).astype(f32)
    sums = swap_rows(chip_sums.astype(bf16).reshape(64, 8, wide), ("z", "y", "x"))
    grad_normed_one = normed_parts[0].astype(f32)
    for step in range(1, GROUPS):
        grad_normed_one = grad_normed_one + shifted(normed_parts[step], "x", step).astype(f32)
    mats, rest = call_kernel(
        functools.partial(sum_kernel, GROUPS),
        (
            jax.ShapeDtypeStruct((4, rows_held, width), f32),
            shape(rows_held, 896 - 4 * cols),
        ),
        1,
        4,
        sums,
    )

    inputs_f = inputs.astype(f32)
    d_inputs = grad_hidden + norm_back(
        inputs_f, inverse_rms(inputs_f), grad_normed_one, gains[0:1]
    )
    return (
        outputs,
        d_inputs,
        rest[:, 0],
        mats[0],
        mats[1],
        mats[2],
        mats[3],
        rest[:, 1],
        rest[:, 2 : 2 + experts_all],
        d_expert_in,
        d_expert_out,
    )


def solution(mesh):
    mesh = Mesh(mesh.devices.reshape(SIZES), ALL)
    dp = ("z", "core")
    seq = ("y", "x")
    rows = P(ALL, None)
    in_specs = (
        rows,
        P(ALL),
        rows,
        rows,
        rows,
        rows,
        P(ALL),
        rows,
        P(seq, None, dp),
        P(seq, dp, None),
        P(ALL),
        P(ALL),
        P(ALL),
        rows,
    )
    out_specs = (
        rows,
        rows,
        P(ALL),
        rows,
        rows,
        rows,
        rows,
        P(ALL),
        rows,
        P(seq, None, dp),
        P(seq, dp, None),
    )
    return jax.shard_map(body, mesh=mesh, in_specs=in_specs, out_specs=out_specs, check_vma=False)
```

```python
import functools

import jax
import jax.numpy as jnp
from jax import lax
from jax.experimental import pallas as pl
from jax.experimental.pallas import tpu as pltpu
from jax.sharding import Mesh
from jax.sharding import PartitionSpec as P

HEADS = 12
GROUPS = 4
CAPACITY = 5
EPSILON = 1e-06
ALL = ("z", "core", "y", "x")
SIZES = (4, 2, 4, 4)

f32 = jnp.float32
bf16 = jnp.bfloat16


def shifted(values, axis, step):
    return lax.ppermute(values, axis, [(i, (i + step) % 4) for i in range(4)])


def swap_rows(values, axes):
    return lax.all_to_all(values, axes, split_axis=0, concat_axis=0, tiled=True)


def matmul(a, b):
    return jnp.dot(a, b, preferred_element_type=f32)


def matmul_t(a, b):
    return lax.dot_general(a, b, (((1,), (1,)), ((), ())), preferred_element_type=f32)


def matmul_tn(a, b):
    return lax.dot_general(a, b, (((0,), (0,)), ((), ())), preferred_element_type=f32)


def inverse_rms(values):
    return lax.rsqrt(jnp.mean(values * values, axis=-1, keepdims=True) + EPSILON)


def norm_back(values, scale, grad, gain_vec):
    u = grad * gain_vec
    return scale * u - values * (scale * scale * scale) * jnp.mean(
        u * values, axis=-1, keepdims=True
    )

MASKED = -1e30
MIB = 1024 * 1024


def call_kernel(kernel, out_shapes, micros, scratch_mib, *operands, scalars=None, whole=False):
    moved = sum(v.size * v.dtype.itemsize for v in operands)
    moved += sum(v.size * v.dtype.itemsize for v in out_shapes)
    in_specs = [pl.BlockSpec(memory_space=pltpu.VMEM)] * len(operands)
    if scalars is not None:
        in_specs = [pl.BlockSpec(memory_space=pltpu.SMEM)] + in_specs
        operands = (scalars,) + operands
    return pl.pallas_call(
        kernel,
        out_shape=out_shapes,
        in_specs=in_specs,
        out_specs=[pl.BlockSpec(memory_space=pltpu.VMEM)] * len(out_shapes),
        compiler_params=pltpu.CompilerParams(
            vmem_limit_bytes=(58 if whole else moved * 4 // 3 // MIB + 2 + scratch_mib) * MIB
        ),
        cost_estimate=pl.CostEstimate(
            flops=int(micros * 1.1e9), bytes_accessed=moved, transcendentals=0
        ),
    )(*operands)


def shape(rows, columns, dtype=f32):
    return jax.ShapeDtypeStruct((rows, columns), dtype)


def transposed_scores(k_ref, kmask_ref, q_ref, qmask_ref, lanes, factor):
    key_side = jnp.concatenate((k_ref[:, lanes], kmask_ref[...]), axis=1)
    query_side = jnp.concatenate((q_ref[:, lanes] * factor, qmask_ref[...]), axis=1)
    return matmul_t(key_side, query_side)


def attend_kernel(first, last, blocks, heads, head_dim, factor, *refs):
    q_ref, qmask_ref = refs[:2]
    kv_refs = refs[2 : 2 + blocks]
    mask_refs = refs[2 + blocks : 2 + 2 * blocks]
    rest = refs[2 + 2 * blocks :]
    if not first:
        old_sum, old_top, old_total = rest[:3]
        rest = rest[3:]
    cols = heads * head_dim
    for head in range(heads):
        lanes = slice(head * head_dim, (head + 1) * head_dim)
        value_lanes = slice(cols + head * head_dim, cols + (head + 1) * head_dim)
        if first:
            top = total = accum = None
        else:
            top = old_top[head : head + 1, :]
            total = old_total[head : head + 1, :]
            accum = old_sum[lanes, :]
        for kv_ref, mask_ref in zip(kv_refs, mask_refs):
            scores = transposed_scores(kv_ref, mask_ref, q_ref, qmask_ref, lanes, factor)
            newest = jnp.max(scores, axis=0, keepdims=True)
            if top is not None:
                newest = jnp.maximum(top, newest)
            terms = jnp.exp(scores - newest)
            term_sum = jnp.sum(terms, axis=0, keepdims=True)
            product = matmul_tn(kv_ref[:, value_lanes], terms.astype(bf16))
            if top is None:
                total, accum = term_sum, product
            else:
                shrink = jnp.exp(top - newest)
                total = total * shrink + term_sum
                accum = accum * shrink + product
            top = newest
        if last:
            att_ref, low_ref, log_ref = rest
            accum = accum / total
            att_ref[lanes, :] = accum
            low_ref[:, :, lanes] = accum.T.astype(bf16).reshape(low_ref.shape[:2] + (head_dim,))
            log_ref[head : head + 1, :] = top + jnp.log(total)
        else:
            sum_ref, top_ref, total_ref = rest
            sum_ref[lanes, :] = accum
            top_ref[head : head + 1, :] = top
            total_ref[head : head + 1, :] = total


def attend_back_kernel(blocks, heads, head_dim, factor, *refs):
    q_ref, qmask_ref, grad_ref, att_ref, log_ref = refs[:5]
    kv_refs = refs[5 : 5 + blocks]
    mask_refs = refs[5 + blocks : 5 + 2 * blocks]
    dq_ref = refs[5 + 2 * blocks]
    out_refs = refs[6 + 2 * blocks :]
    cols = heads * head_dim
    for head in range(heads):
        lanes = slice(head * head_dim, (head + 1) * head_dim)
        value_lanes = slice(cols + head * head_dim, cols + (head + 1) * head_dim)
        grad = grad_ref[:, :, lanes].reshape(-1, head_dim)
        query = q_ref[:, lanes] * factor
        delta = jnp.sum(grad.astype(f32).T * att_ref[lanes, :], axis=0, keepdims=True)
        log_total = log_ref[head : head + 1, :]
        dq = None
        for kv_ref, mask_ref, out_ref in zip(kv_refs, mask_refs, out_refs):
            scores = transposed_scores(kv_ref, mask_ref, q_ref, qmask_ref, lanes, factor)
            probs = jnp.exp(scores - log_total)
            grad_probs = matmul_t(kv_ref[:, value_lanes], grad)
            grad_scores = (probs * (grad_probs - delta)).astype(bf16)
            out_ref[:, value_lanes] = matmul(probs.astype(bf16), grad).astype(out_ref.dtype)
            out_ref[:, lanes] = matmul(grad_scores, query).astype(out_ref.dtype)
            product = matmul_tn(kv_ref[:, lanes], grad_scores)
            dq = product if dq is None else dq + product
        dq_ref[:, lanes] = dq.T * factor


def pack_kernel(
    groups,
    query_ref,
    key_ref,
    value_ref,
    output_ref,
    gain_one_ref,
    gain_two_ref,
    router_ref,
    seg_ref,
    packed_ref,
):
    rows = query_ref.shape[0]
    cols = query_ref.shape[1] // groups
    wide = packed_ref.shape[2]
    across = lax.broadcasted_iota(jnp.int32, (rows, rows), 1)
    same = across == lax.broadcasted_iota(jnp.int32, (rows, rows), 0)

    def column(ref):
        return jnp.sum(jnp.where(same, ref[...].astype(f32), 0.0), axis=1, keepdims=True)

    extra = (column(gain_one_ref), column(gain_two_ref), router_ref[...].astype(f32))
    used = 2 + router_ref.shape[1]
    extra = jnp.concatenate(extra + (jnp.zeros((rows, 128 - used), f32),), axis=1)
    extra = jnp.concatenate([extra[row : row + 1] for row in range(rows)], axis=1)
    numbers = seg_ref[...].astype(f32)
    numbers = jnp.concatenate((numbers, jnp.zeros((1, wide - numbers.shape[1]), f32)), axis=1)
    for head in range(groups):
        lanes = slice(head * cols, (head + 1) * cols)
        mats = tuple(
            ref[:, lanes].astype(f32) for ref in (query_ref, key_ref, value_ref, output_ref)
        )
        block = jnp.concatenate((jnp.concatenate(mats, axis=1), numbers, extra), axis=0)
        block = block.astype(bf16)
        for place in range(head, packed_ref.shape[0], groups):
            packed_ref[place] = block


def front_kernel(
    cols,
    place_ref,
    pick_ref,
    held_ref,
    other_ref,
    r0_ref,
    r1_ref,
    r2_ref,
    r3_ref,
    mat_ref,
    out_ref,
    extra_ref,
    gain_ref,
    rows_ref,
    normed_ref,
    q_ref,
    kv_ref,
):
    head_place = place_ref[0]
    held = jnp.concatenate((held_ref[...], other_ref[...]), axis=0)
    held = held.reshape(-1, held.shape[2])
    weights = matmul(pick_ref[...], held).astype(bf16)
    mat = weights[:, : 3 * cols]
    mat_ref[...] = mat
    out_ref[...] = weights[:, 3 * cols :]
    count = held.shape[0]
    spot = lax.broadcasted_iota(jnp.int32, (count, 128), 0) % 8
    spare = jnp.zeros((count, 128), f32)
    for row in range(held.shape[1] // 128):
        piece = held[:, row * 128 : row * 128 + 128].astype(f32)
        spare = jnp.where(spot == row, pltpu.roll(piece, count + row - 7, 0), spare)
    extra = matmul(pick_ref[...], spare.astype(bf16)).astype(bf16)[:, :64]
    extra_ref[...] = extra
    gains = extra.astype(f32).T[:8]
    gain_ref[...] = gains
    part = r0_ref.shape[0]
    for step, ref in enumerate((r0_ref, r1_ref, r2_ref, r3_ref)):
        start = (head_place + GROUPS - step) % GROUPS * part
        rows_ref[pl.ds(pl.multiple_of(start, part), part), :] = ref[...]
    rows = rows_ref[...].astype(f32)
    normed = (rows * inverse_rms(rows) * gains[0:1]).astype(bf16)
    normed_ref[...] = normed
    qkv = matmul(normed, mat).astype(bf16)
    q_ref[...] = qkv[:, :cols]
    kv_ref[...] = qkv[:, cols:]


def chosen_lane(expert_ref, lanes):
    lane = lax.broadcasted_iota(jnp.int32, (expert_ref.shape[0], lanes), 1)
    return (lane == expert_ref[...] + 2).astype(f32)


def slot_matrix(keys_ref, slots):
    slot = lax.broadcasted_iota(jnp.int32, (slots, keys_ref.shape[1]), 0)
    return (slot == keys_ref[...]).astype(bf16)


def route_kernel(
    experts,
    place_ref,
    att_ref,
    w0_ref,
    w1_ref,
    w2_ref,
    w3_ref,
    in_ref,
    cot_ref,
    gain_ref,
    extra_ref,
    expert_ref,
    keys_ref,
    sent_ref,
    hidden_ref,
    normed_ref,
    probs_ref,
):
    head_place = place_ref[0]
    mixed = jnp.concatenate([att_ref[i] for i in range(GROUPS)], axis=1)
    pieces = [matmul(mixed, ref[...]) for ref in (w0_ref, w1_ref, w2_ref, w3_ref)]
    columns = []
    for spot in range(GROUPS):
        value = pieces[0]
        for step in range(1, GROUPS):
            value = jnp.where((head_place + GROUPS - step) % GROUPS == spot, pieces[step], value)
        columns.append(value)
    hidden = in_ref[...].astype(f32) + jnp.concatenate(columns, axis=1)
    hidden_ref[...] = hidden
    normed = (hidden * inverse_rms(hidden) * gain_ref[1:2]).astype(bf16)
    normed_ref[...] = normed
    logits = matmul(normed, extra_ref[...])
    lane = lax.broadcasted_iota(jnp.int32, logits.shape, 1)
    logits = jnp.where((lane >= 2) & (lane < 2 + experts), logits, MASKED)
    terms = jnp.exp(logits - jnp.max(logits, axis=1, keepdims=True))
    probs = terms / jnp.sum(terms, axis=1, keepdims=True)
    probs_ref[...] = probs
    gate = jnp.sum(probs * chosen_lane(expert_ref, probs.shape[1]), axis=1, keepdims=True)
    grad_expert = (gate * cot_ref[...].astype(f32)).astype(bf16)
    width = normed.shape[1]
    slots = slot_matrix(keys_ref, sent_ref.shape[0])
    sent_ref[:, :width] = matmul(slots, normed).astype(bf16)
    sent_ref[:, width:] = matmul(slots, grad_expert).astype(bf16)


def return_kernel(
    experts,
    place_ref,
    back_ref,
    w0_ref,
    w1_ref,
    w2_ref,
    w3_ref,
    hidden_ref,
    cot_ref,
    probs_ref,
    gain_ref,
    extra_ref,
    expert_ref,
    keys_ref,
    outputs_ref,
    grad_ref,
    pair_ref,
    logits_ref,
    gain_sum_ref,
):
    head_place = place_ref[0]
    width = hidden_ref.shape[1]
    cols = width // GROUPS
    back = matmul_tn(slot_matrix(keys_ref, back_ref.shape[0]), back_ref[...])
    expert_tok, grad_routed = back[:, :width], back[:, width:]
    hidden = hidden_ref[...]
    grad_out = cot_ref[...].astype(f32)
    probs = probs_ref[...]
    chosen = chosen_lane(expert_ref, probs.shape[1])
    gate = jnp.sum(probs * chosen, axis=1, keepdims=True)
    outputs_ref[...] = (hidden + gate * expert_tok).astype(bf16)
    grad_gate = jnp.sum(grad_out * expert_tok, axis=1, keepdims=True)
    grad_logits = (probs * (chosen - gate) * grad_gate).astype(bf16)
    logits_ref[...] = grad_logits
    grad_normed = grad_routed + matmul_t(grad_logits, extra_ref[...])
    scale = inverse_rms(hidden)
    gain_sum_ref[...] = jnp.sum(grad_normed * hidden * scale, axis=0, keepdims=True)
    grad_hidden = grad_out + norm_back(hidden, scale, grad_normed, gain_ref[1:2])
    grad_ref[...] = grad_hidden
    branch = grad_hidden.astype(bf16)
    grad_mixed = None
    for step, ref in enumerate((w0_ref, w1_ref, w2_ref, w3_ref)):
        block = branch[:, :cols]
        for spot in range(1, GROUPS):
            block = jnp.where(
                (head_place + GROUPS - step) % GROUPS == spot,
                branch[:, spot * cols : (spot + 1) * cols],
                block,
            )
        product = matmul_t(block, ref[...])
        grad_mixed = product if grad_mixed is None else grad_mixed + product
    for spot in range(GROUPS):
        lanes = slice(spot * cols, (spot + 1) * cols)
        pair_ref[spot, :, :cols] = grad_mixed[:, lanes].astype(bf16)
        pair_ref[spot, :, cols:] = branch[:, lanes]


def expert_kernel(expert, blocks, part, width, *refs):
    row_refs = refs[:blocks]
    in_ref, out_ref = refs[blocks : blocks + 2]
    own_ref, away_ref, rows_ref, act_ref, pre_ref = refs[blocks + 2 :]
    for place, row_ref in enumerate(row_refs):
        rows_ref[pl.ds(place * part, part), :] = row_ref[...]
    before_act = matmul(rows_ref[:, :width], in_ref[expert])
    grad_act = matmul_t(rows_ref[:, width:], out_ref[expert])
    square = before_act * before_act
    inner = jnp.tanh(0.7978845608028654 * (before_act + 0.044715 * square * before_act))
    half = 0.5 * (1.0 + inner)
    act_ref[...] = (before_act * half).astype(bf16)
    slope = half + (0.5 * 0.7978845608028654) * before_act * (1.0 - inner * inner) * (
        1.0 + (3 * 0.044715) * square
    )
    pre_ref[...] = (grad_act * slope).astype(bf16)
    part_out = matmul(act_ref[...], out_ref[expert])
    part_back = matmul_t(pre_ref[...], in_ref[expert])
    half = own_ref.shape[0]
    for rows, part_ref in ((slice(half, None), away_ref), (slice(0, half), own_ref)):
        part_ref[:, :width] = part_out[rows].astype(bf16)
        part_ref[:, width:] = part_back[rows].astype(bf16)


def expert_grad_kernel(experts, width, *refs):
    in_ref, out_ref = refs[3 * experts :]
    for expert in range(experts):
        rows_ref, act_ref, pre_ref = refs[3 * expert : 3 * expert + 3]
        out_ref[expert] = matmul_tn(act_ref[...], rows_ref[:, width:])
        in_ref[expert] = matmul_tn(rows_ref[:, :width], pre_ref[...])


def weight_sums(sums_ref, one_ref, turned_ref, two_ref, spread_ref, logits_ref, *given):
    grad_qkv, products, gain_one, gain_two = given
    sums = jnp.concatenate(
        (matmul(one_ref[...], grad_qkv), matmul(turned_ref[...], products)), axis=1
    )
    rest = matmul(two_ref[...], logits_ref[...])
    lane = lax.broadcasted_iota(jnp.int32, rest.shape, 1)
    spread = spread_ref[...].astype(f32)
    for index, gain in ((0, gain_one), (1, gain_two)):
        gain = jnp.sum(spread * gain, axis=1, keepdims=True)
        rest = jnp.where(lane == index, gain, rest)
    rest = jnp.concatenate((rest, jnp.zeros_like(rest)), axis=1)
    rest = jnp.concatenate(
        [pltpu.roll(rest, 7 - row, 0) for row in range(sums.shape[1] // 128)], axis=1
    )
    spot = lax.broadcasted_iota(jnp.int32, sums.shape, 0) % 8
    sums_ref[...] = jnp.where(spot == 7, rest, sums).astype(bf16)


def tail_kernel(blocks, place_ref, *refs):
    dq_refs, kv_refs = refs[:blocks], refs[blocks : 2 * blocks]
    att_refs = refs[2 * blocks : 3 * blocks]
    mat_ref, rows_ref, pair_ref, gain_two_ref, logits_ref = refs[3 * blocks : 3 * blocks + 5]
    own_mats, away_mats = refs[3 * blocks + 5 : 3 * blocks + 9], refs[3 * blocks + 9 : 3 * blocks + 13]
    away_ref, own_ref = refs[3 * blocks + 13 : 3 * blocks + 15]
    part_refs = refs[3 * blocks + 15 :]
    head_place = place_ref[0]
    cols = dq_refs[0].shape[1]
    grad_q = dq_refs[0][...]
    for ref in dq_refs[1:]:
        grad_q = grad_q + ref[...]
    grad_kv = kv_refs[0][...]
    for ref in kv_refs[1:]:
        grad_kv = grad_kv + ref[...].astype(f32)
    grad_qkv = jnp.concatenate((grad_q.astype(bf16), grad_kv.astype(bf16)), axis=1)
    part = matmul_t(grad_qkv, mat_ref[...])
    rows = rows_ref[...].astype(f32)
    gain_one = jnp.sum(part * rows * inverse_rms(rows), axis=0, keepdims=True)
    part = part.astype(bf16).astype(f32).reshape(blocks, -1, part.shape[1])
    for step, part_ref in enumerate(part_refs):
        value = part[0]
        for spot in range(1, blocks):
            value = jnp.where((head_place + step) % blocks == spot, part[spot], value)
        part_ref[...] = value.astype(part_ref.dtype)
    branch = pair_ref[:, :, cols:].reshape(-1, cols)
    products = jnp.concatenate(
        [matmul_tn(ref[...].reshape(-1, cols), branch).astype(bf16) for ref in att_refs], axis=0
    )
    for sums_ref, mats in ((away_ref, away_mats), (own_ref, own_mats)):
        weight_sums(
            sums_ref, *mats, logits_ref, grad_qkv, products, gain_one, gain_two_ref[...]
        )


def sum_kernel(groups, sums_ref, mats_ref, rest_ref):
    rows = mats_ref.shape[1]
    cols = mats_ref.shape[2] // groups
    rest = None
    for head in range(groups):
        total = sums_ref[head].astype(f32)
        for place in range(head + groups, sums_ref.shape[0], groups):
            total = total + sums_ref[place].astype(f32)
        for mat in range(4):
            mats_ref[mat, :, head * cols : (head + 1) * cols] = total[
                :rows, mat * cols : (mat + 1) * cols
            ]
        rest = total[7:8] if rest is None else rest + total[7:8]
    rest_ref[...] = rest


def body(
    inputs,
    gain_attn,
    w_query,
    w_key,
    w_value,
    w_output,
    gain_ffn,
    router,
    expert_in,
    expert_out,
    expert_index,
    slot_index,
    segment_ids,
    cotangent,
):
    tok_rows, width = inputs.shape
    head_dim = width // HEADS
    factor = head_dim ** (-0.5)
    cols = width // GROUPS
    heads_here = HEADS // GROUPS
    experts_all = router.shape[1]
    rows_held = w_query.shape[0]
    local_experts = expert_in.shape[0]
    hidden = expert_in.shape[2]
    block_rows = GROUPS * tok_rows

    core = lax.axis_index("core")
    head_place = lax.axis_index("x")
    query_place = lax.axis_index("y")
    ring = jnp.arange(GROUPS, dtype=jnp.int32)

    def core_swap(values):
        return lax.ppermute(values, "core", [(0, 1), (1, 0)])

    def gathered(values, axis):
        return [values] + [shifted(values, axis, step) for step in range(1, GROUPS)]

    input_parts = gathered(inputs, "x")

    wide = width
    (packed,) = call_kernel(
        functools.partial(pack_kernel, GROUPS),
        (jax.ShapeDtypeStruct((64, 8, wide), bf16),),
        1,
        4,
        w_query,
        w_key,
        w_value,
        w_output,
        gain_attn[None, :],
        gain_ffn[None, :],
        router,
        segment_ids[None, :],
        whole=True,
    )
    held = swap_rows(packed, ("z", "y", "x"))
    held_other = core_swap(held)
    feature = jnp.arange(width, dtype=jnp.int32)

    def spread_slot(feature):
        owner = feature // rows_held
        return (owner // 32 * 16 + owner % 16) * 8 + feature % rows_held

    spread_row = jnp.where(feature // rows_held // 16 % 2 == core, 0, 512) + spread_slot(feature)
    place_row = jnp.arange(1024, dtype=jnp.int32)
    halves = (place_row[:512], place_row[512:])
    spread = [(rows[:, None] == spread_row[None, :]).astype(bf16) for rows in halves]
    pick = (spread_row[:, None] == place_row[None, :]).astype(bf16)
    segs = held.reshape(4, 16, 8, wide)[:, :, rows_held, :tok_rows]
    segs = lax.dynamic_index_in_dim(segs, lax.axis_index("z"), axis=0, keepdims=False)
    segs = segs.reshape(GROUPS, GROUPS, tok_rows)
    key_segs = jnp.take(segs, (query_place - ring) % GROUPS, axis=0)
    query_seg = key_segs[0].reshape(block_rows)
    key_segs = key_segs.reshape(GROUPS * block_rows)

    places = head_place.astype(jnp.int32)[None]
    qkv_mat, out_cols, extra, gains, block_inputs, normed_one, queries, kv_own = call_kernel(
        functools.partial(front_kernel, cols),
        (
            shape(width, 3 * cols, bf16),
            shape(width, cols, bf16),
            shape(width, 64, bf16),
            shape(8, width),
            shape(block_rows, width, bf16),
            shape(block_rows, width, bf16),
            shape(block_rows, cols, bf16),
            shape(block_rows, 2 * cols, bf16),
        ),
        4,
        12,
        pick,
        held,
        held_other,
        *input_parts,
        scalars=places,
        whole=True,
    )
    kv_blocks = gathered(kv_own, "y")
    out_parts = gathered(out_cols, "x")
    documents = jnp.arange(head_dim, dtype=bf16)[None, :]
    query_mask = (query_seg[:, None] == documents).astype(bf16)
    key_masks = jnp.where((key_segs[:, None] == documents) | (documents > 2), 0.0, MASKED)
    key_masks = key_masks.astype(bf16).reshape(GROUPS, block_rows, head_dim)
    key_masks = [key_masks[i] for i in range(GROUPS)]
    sizes = (heads_here, head_dim, factor)
    state = call_kernel(
        functools.partial(attend_kernel, True, False, 1, *sizes),
        (shape(cols, block_rows), shape(8, block_rows), shape(8, block_rows)),
        2,
        8,
        queries,
        query_mask,
        kv_own,
        key_masks[0],
    )
    state = call_kernel(
        functools.partial(attend_kernel, False, False, 2, *sizes),
        (shape(cols, block_rows), shape(8, block_rows), shape(8, block_rows)),
        4,
        8,
        queries,
        query_mask,
        kv_blocks[1],
        kv_blocks[3],
        key_masks[1],
        key_masks[3],
        *state,
    )
    attended, att_low, log_total = call_kernel(
        functools.partial(attend_kernel, False, True, 1, *sizes),
        (
            shape(cols, block_rows),
            jax.ShapeDtypeStruct((GROUPS, tok_rows, cols), bf16),
            shape(8, block_rows),
        ),
        2,
        8,
        queries,
        query_mask,
        kv_blocks[2],
        key_masks[2],
        *state,
    )
    mixed_parts = swap_rows(att_low, "x")
    expert_col = expert_index[:, None]
    slot_row = expert_index // local_experts * 16 + expert_index % local_experts * 8 + slot_index
    keys = slot_row[None, :]
    slots = 16 * 16
    sent, hidden_one, normed_two, router_probs = call_kernel(
        functools.partial(route_kernel, experts_all),
        (
            shape(slots, 2 * width, bf16),
            shape(tok_rows, width),
            shape(tok_rows, width, bf16),
            shape(tok_rows, 64),
        ),
        3,
        6,
        mixed_parts,
        *out_parts,
        inputs,
        cotangent,
        gains,
        extra,
        expert_col,
        keys,
        scalars=places,
    )

    turned_feature = (head_place - feature // cols) % GROUPS * cols + feature % cols
    turned_row = jnp.where(turned_feature // rows_held // 16 % 2 == core, 0, 512)
    turned_row = turned_row + spread_slot(turned_feature)
    shared = [
        (
            matmul_t(spread_half, normed_one).astype(bf16),
            (rows[:, None] == turned_row[None, :]).astype(bf16),
            matmul_t(spread_half, normed_two).astype(bf16),
            spread_half,
        )
        for spread_half, rows in zip(spread, halves)
    ]

    dev_rows = 16 * CAPACITY
    dense = jnp.arange(dev_rows, dtype=jnp.int32)
    squeeze = [
        (
            (dense // CAPACITY * 16 + expert * 8 + dense % CAPACITY)[:, None]
            == jnp.arange(slots, dtype=jnp.int32)[None, :]
        ).astype(bf16)
        for expert in range(local_experts)
    ]

    def seq_swap(values):
        values = values.reshape(16, slots // 16, 2 * width)
        return swap_rows(values, ("y", "x")).reshape(slots, 2 * width)

    half_block = shape(4 * dev_rows, 2 * width, bf16)
    all_rows = 8 * dev_rows
    act_shape = shape(all_rows, hidden, bf16)
    arrived = seq_swap(sent)
    arrived, att_low = lax.optimization_barrier((arrived, att_low))
    att_parts = gathered(att_low, "x")
    arrived = [matmul(mat, arrived).astype(bf16) for mat in squeeze]
    z_rows = [gathered(arrived[0], "z")]

    z_rows.append(gathered(arrived[1], "z"))
    z_rows[0], att_parts, shared = lax.optimization_barrier((z_rows[0], att_parts, shared))

    kept, totals = [], []
    for expert in range(local_experts):
        row_blocks = z_rows[expert] + [core_swap(rows) for rows in z_rows[expert]]
        own_parts, away_parts, *held_back = call_kernel(
            functools.partial(expert_kernel, expert, 8, dev_rows, width),
            (half_block, half_block, shape(all_rows, 2 * width, bf16), act_shape, act_shape),
            5,
            8,
            *row_blocks,
            expert_in,
            expert_out,
        )
        kept += held_back
        totals.append(own_parts.astype(f32) + core_swap(away_parts).astype(f32))
    kept, totals = lax.optimization_barrier((kept, totals))
    home = []
    for sums in totals:
        total = sums[:dev_rows]
        for step in range(1, 4):
            away = sums[step * dev_rows : (step + 1) * dev_rows].astype(bf16)
            total = total + shifted(away, "z", 4 - step).astype(f32)
        home.append(total.astype(bf16))
    d_expert_in, d_expert_out = call_kernel(
        functools.partial(expert_grad_kernel, local_experts, width),
        (
            jax.ShapeDtypeStruct(expert_in.shape, f32),
            jax.ShapeDtypeStruct(expert_out.shape, f32),
        ),
        4,
        8,
        *kept,
    )
    home, d_expert_in, d_expert_out = lax.optimization_barrier((home, d_expert_in, d_expert_out))
    back = seq_swap(
        sum(matmul_tn(mat, rows) for mat, rows in zip(squeeze, home)).astype(bf16)
    )

    outputs, grad_hidden, pair, grad_logits, d_gain_ffn = call_kernel(
        functools.partial(return_kernel, experts_all),
        (
            shape(tok_rows, width, bf16),
            shape(tok_rows, width),
            jax.ShapeDtypeStruct((GROUPS, tok_rows, 2 * cols), bf16),
            shape(tok_rows, 64, bf16),
            shape(1, width),
        ),
        3,
        6,
        back,
        *out_parts,
        hidden_one,
        cotangent,
        router_probs,
        gains,
        extra,
        expert_col,
        keys,
        scalars=places,
    )

    pair = swap_rows(pair, "x")
    dq_parts, kv_parts = [], []
    for step in (2, 1, 3, 0):
        dq, kv_part = call_kernel(
            functools.partial(attend_back_kernel, 1, *sizes),
            (shape(block_rows, cols), shape(block_rows, 2 * cols, bf16 if step else f32)),
            3,
            8,
            queries,
            query_mask,
            pair,
            attended,
            log_total,
            kv_blocks[step],
            key_masks[step],
        )
        dq_parts.append(dq)
        kv_parts.append(shifted(kv_part, "y", GROUPS - step) if step else kv_part)
    kv_parts = kv_parts[::-1]

    sums_shape = shape(512, wide, bf16)
    part_shape = shape(tok_rows, width, bf16)
    away_sums, own_sums, *normed_parts = call_kernel(
        functools.partial(tail_kernel, GROUPS),
        (sums_shape, sums_shape) + (part_shape,) * GROUPS,
        5,
        12,
        *dq_parts,
        *kv_parts,
        *att_parts,
        qkv_mat,
        block_inputs,
        pair,
        d_gain_ffn,
        grad_logits,
        *shared[0],
        *shared[1],
        scalars=places,
    )
    chip_sums = own_sums.astype(f32) + core_swap(away_sums).astype(f32)
    sums = swap_rows(chip_sums.astype(bf16).reshape(64, 8, wide), ("z", "y", "x"))
    grad_normed_one = normed_parts[0].astype(f32)
    for step in range(1, GROUPS):
        grad_normed_one = grad_normed_one + shifted(normed_parts[step], "x", step).astype(f32)
    mats, rest = call_kernel(
        functools.partial(sum_kernel, GROUPS),
        (
            jax.ShapeDtypeStruct((4, rows_held, width), f32),
            shape(1, wide),
        ),
        1,
        4,
        sums,
    )

    rest = rest.reshape(rows_held, wide // rows_held)
    inputs_f = inputs.astype(f32)
    d_inputs = grad_hidden + norm_back(
        inputs_f, inverse_rms(inputs_f), grad_normed_one, gains[0:1]
    )
    return (
        outputs,
        d_inputs,
        rest[:, 0],
        mats[0],
        mats[1],
        mats[2],
        mats[3],
        rest[:, 1],
        rest[:, 2 : 2 + experts_all],
        d_expert_in,
        d_expert_out,
    )


def solution(mesh):
    mesh = Mesh(mesh.devices.reshape(SIZES), ALL)
    dp = ("z", "core")
    seq = ("y", "x")
    rows = P(ALL, None)
    in_specs = (
        rows,
        P(ALL),
        rows,
        rows,
        rows,
        rows,
        P(ALL),
        rows,
        P(seq, None, dp),
        P(seq, dp, None),
        P(ALL),
        P(ALL),
        P(ALL),
        rows,
    )
    out_specs = (
        rows,
        rows,
        P(ALL),
        rows,
        rows,
        rows,
        rows,
        P(ALL),
        rows,
        P(seq, None, dp),
        P(seq, dp, None),
    )
    return jax.shard_map(body, mesh=mesh, in_specs=in_specs, out_specs=out_specs, check_vma=False)
```

```python
import functools

import jax
import jax.numpy as jnp
from jax import lax
from jax.experimental import pallas as pl
from jax.experimental.pallas import tpu as pltpu
from jax.sharding import Mesh
from jax.sharding import PartitionSpec as P

HEADS = 12
GROUPS = 4
CAPACITY = 5
EPSILON = 1e-06
ALL = ("z", "core", "y", "x")
SIZES = (4, 2, 4, 4)

f32 = jnp.float32
bf16 = jnp.bfloat16


def shifted(values, axis, step):
    return lax.ppermute(values, axis, [(i, (i + step) % 4) for i in range(4)])


def swap_rows(values, axes):
    return lax.all_to_all(values, axes, split_axis=0, concat_axis=0, tiled=True)


def matmul(a, b):
    return jnp.dot(a, b, preferred_element_type=f32)


def matmul_t(a, b):
    return lax.dot_general(a, b, (((1,), (1,)), ((), ())), preferred_element_type=f32)


def matmul_tn(a, b):
    return lax.dot_general(a, b, (((0,), (0,)), ((), ())), preferred_element_type=f32)


def inverse_rms(values):
    return lax.rsqrt(jnp.mean(values * values, axis=-1, keepdims=True) + EPSILON)


def norm_back(values, scale, grad, gain_vec):
    u = grad * gain_vec
    return scale * u - values * (scale * scale * scale) * jnp.mean(
        u * values, axis=-1, keepdims=True
    )

MASKED = -1e30
MIB = 1024 * 1024


def call_kernel(kernel, out_shapes, micros, scratch_mib, *operands, scalars=None, whole=False):
    moved = sum(v.size * v.dtype.itemsize for v in operands)
    moved += sum(v.size * v.dtype.itemsize for v in out_shapes)
    in_specs = [pl.BlockSpec(memory_space=pltpu.VMEM)] * len(operands)
    if scalars is not None:
        in_specs = [pl.BlockSpec(memory_space=pltpu.SMEM)] + in_specs
        operands = (scalars,) + operands
    return pl.pallas_call(
        kernel,
        out_shape=out_shapes,
        in_specs=in_specs,
        out_specs=[pl.BlockSpec(memory_space=pltpu.VMEM)] * len(out_shapes),
        compiler_params=pltpu.CompilerParams(
            vmem_limit_bytes=(58 if whole else moved * 4 // 3 // MIB + 2 + scratch_mib) * MIB
        ),
        cost_estimate=pl.CostEstimate(
            flops=int(micros * 1.1e9), bytes_accessed=moved, transcendentals=0
        ),
    )(*operands)


def shape(rows, columns, dtype=f32):
    return jax.ShapeDtypeStruct((rows, columns), dtype)


def transposed_scores(k_ref, kmask_ref, q_ref, qmask_ref, lanes, factor):
    key_side = jnp.concatenate((k_ref[:, lanes], kmask_ref[...]), axis=1)
    query_side = jnp.concatenate((q_ref[:, lanes] * factor, qmask_ref[...]), axis=1)
    return matmul_t(key_side, query_side)


def attend_kernel(first, last, blocks, heads, head_dim, factor, *refs):
    q_ref, qmask_ref = refs[:2]
    kv_refs = refs[2 : 2 + blocks]
    mask_refs = refs[2 + blocks : 2 + 2 * blocks]
    rest = refs[2 + 2 * blocks :]
    if not first:
        old_sum, old_top, old_total = rest[:3]
        rest = rest[3:]
    cols = heads * head_dim
    for head in range(heads):
        lanes = slice(head * head_dim, (head + 1) * head_dim)
        value_lanes = slice(cols + head * head_dim, cols + (head + 1) * head_dim)
        if first:
            top = total = accum = None
        else:
            top = old_top[head : head + 1, :]
            total = old_total[head : head + 1, :]
            accum = old_sum[lanes, :]
        for kv_ref, mask_ref in zip(kv_refs, mask_refs):
            scores = transposed_scores(kv_ref, mask_ref, q_ref, qmask_ref, lanes, factor)
            newest = jnp.max(scores, axis=0, keepdims=True)
            if top is not None:
                newest = jnp.maximum(top, newest)
            terms = jnp.exp(scores - newest)
            term_sum = jnp.sum(terms, axis=0, keepdims=True)
            product = matmul_tn(kv_ref[:, value_lanes], terms.astype(bf16))
            if top is None:
                total, accum = term_sum, product
            else:
                shrink = jnp.exp(top - newest)
                total = total * shrink + term_sum
                accum = accum * shrink + product
            top = newest
        if last:
            att_ref, low_ref, log_ref = rest
            accum = accum / total
            att_ref[lanes, :] = accum
            low_ref[:, :, lanes] = accum.T.astype(bf16).reshape(low_ref.shape[:2] + (head_dim,))
            log_ref[head : head + 1, :] = top + jnp.log(total)
        else:
            sum_ref, top_ref, total_ref = rest
            sum_ref[lanes, :] = accum
            top_ref[head : head + 1, :] = top
            total_ref[head : head + 1, :] = total


def attend_back_kernel(blocks, heads, head_dim, factor, *refs):
    q_ref, qmask_ref, grad_ref, att_ref, log_ref = refs[:5]
    kv_refs = refs[5 : 5 + blocks]
    mask_refs = refs[5 + blocks : 5 + 2 * blocks]
    dq_ref = refs[5 + 2 * blocks]
    out_refs = refs[6 + 2 * blocks :]
    cols = heads * head_dim
    for head in range(heads):
        lanes = slice(head * head_dim, (head + 1) * head_dim)
        value_lanes = slice(cols + head * head_dim, cols + (head + 1) * head_dim)
        grad = grad_ref[:, :, lanes].reshape(-1, head_dim)
        query = q_ref[:, lanes] * factor
        delta = jnp.sum(grad.astype(f32).T * att_ref[lanes, :], axis=0, keepdims=True)
        log_total = log_ref[head : head + 1, :]
        dq = None
        for kv_ref, mask_ref, out_ref in zip(kv_refs, mask_refs, out_refs):
            scores = transposed_scores(kv_ref, mask_ref, q_ref, qmask_ref, lanes, factor)
            probs = jnp.exp(scores - log_total)
            grad_probs = matmul_t(kv_ref[:, value_lanes], grad)
            grad_scores = (probs * (grad_probs - delta)).astype(bf16)
            out_ref[:, value_lanes] = matmul(probs.astype(bf16), grad).astype(out_ref.dtype)
            out_ref[:, lanes] = matmul(grad_scores, query).astype(out_ref.dtype)
            product = matmul_tn(kv_ref[:, lanes], grad_scores)
            dq = product if dq is None else dq + product
        dq_ref[:, lanes] = dq.T * factor


def pack_kernel(
    groups,
    query_ref,
    key_ref,
    value_ref,
    output_ref,
    gain_one_ref,
    gain_two_ref,
    router_ref,
    seg_ref,
    packed_ref,
):
    rows = query_ref.shape[0]
    cols = query_ref.shape[1] // groups
    wide = packed_ref.shape[2]
    across = lax.broadcasted_iota(jnp.int32, (rows, rows), 1)
    same = across == lax.broadcasted_iota(jnp.int32, (rows, rows), 0)

    def column(ref):
        return jnp.sum(jnp.where(same, ref[...].astype(f32), 0.0), axis=1, keepdims=True)

    extra = (column(gain_one_ref), column(gain_two_ref), router_ref[...].astype(f32))
    used = 2 + router_ref.shape[1]
    extra = jnp.concatenate(extra + (jnp.zeros((rows, 128 - used), f32),), axis=1)
    extra = jnp.concatenate([extra[row : row + 1] for row in range(rows)], axis=1)
    numbers = seg_ref[...].astype(f32)
    numbers = jnp.concatenate((numbers, jnp.zeros((1, wide - numbers.shape[1]), f32)), axis=1)
    for head in range(groups):
        lanes = slice(head * cols, (head + 1) * cols)
        mats = tuple(
            ref[:, lanes].astype(f32) for ref in (query_ref, key_ref, value_ref, output_ref)
        )
        block = jnp.concatenate((jnp.concatenate(mats, axis=1), numbers, extra), axis=0)
        block = block.astype(bf16)
        for place in range(head, packed_ref.shape[0], groups):
            packed_ref[place] = block


def front_kernel(
    cols,
    place_ref,
    pick_ref,
    held_ref,
    other_ref,
    r0_ref,
    r1_ref,
    r2_ref,
    r3_ref,
    mat_ref,
    out_ref,
    extra_ref,
    gain_ref,
    rows_ref,
    normed_ref,
    q_ref,
    kv_ref,
):
    head_place = place_ref[0]
    held = jnp.concatenate((held_ref[...], other_ref[...]), axis=0)
    held = held.reshape(-1, held.shape[2])
    weights = matmul(pick_ref[...], held).astype(bf16)
    mat = weights[:, : 3 * cols]
    mat_ref[...] = mat
    out_ref[...] = weights[:, 3 * cols :]
    count = held.shape[0]
    spot = lax.broadcasted_iota(jnp.int32, (count, 128), 0) % 8
    spare = jnp.zeros((count, 128), f32)
    for row in range(held.shape[1] // 128):
        piece = held[:, row * 128 : row * 128 + 128].astype(f32)
        spare = jnp.where(spot == row, pltpu.roll(piece, count + row - 7, 0), spare)
    extra = matmul(pick_ref[...], spare.astype(bf16)).astype(bf16)[:, :64]
    extra_ref[...] = extra
    gains = extra.astype(f32).T[:8]
    gain_ref[...] = gains
    part = r0_ref.shape[0]
    for step, ref in enumerate((r0_ref, r1_ref, r2_ref, r3_ref)):
        start = (head_place + GROUPS - step) % GROUPS * part
        rows_ref[pl.ds(pl.multiple_of(start, part), part), :] = ref[...]
    rows = rows_ref[...].astype(f32)
    normed = (rows * inverse_rms(rows) * gains[0:1]).astype(bf16)
    normed_ref[...] = normed
    qkv = matmul(normed, mat).astype(bf16)
    q_ref[...] = qkv[:, :cols]
    kv_ref[...] = qkv[:, cols:]


def chosen_lane(expert_ref, lanes):
    lane = lax.broadcasted_iota(jnp.int32, (expert_ref.shape[0], lanes), 1)
    return (lane == expert_ref[...] + 2).astype(f32)


def slot_matrix(keys_ref, slots):
    slot = lax.broadcasted_iota(jnp.int32, (slots, keys_ref.shape[1]), 0)
    return (slot == keys_ref[...]).astype(bf16)


def route_kernel(
    experts,
    place_ref,
    att_ref,
    w0_ref,
    w1_ref,
    w2_ref,
    w3_ref,
    in_ref,
    cot_ref,
    gain_ref,
    extra_ref,
    expert_ref,
    keys_ref,
    sent_ref,
    hidden_ref,
    normed_ref,
    probs_ref,
):
    head_place = place_ref[0]
    mixed = jnp.concatenate([att_ref[i] for i in range(GROUPS)], axis=1)
    pieces = [matmul(mixed, ref[...]) for ref in (w0_ref, w1_ref, w2_ref, w3_ref)]
    columns = []
    for spot in range(GROUPS):
        value = pieces[0]
        for step in range(1, GROUPS):
            value = jnp.where((head_place + GROUPS - step) % GROUPS == spot, pieces[step], value)
        columns.append(value)
    hidden = in_ref[...].astype(f32) + jnp.concatenate(columns, axis=1)
    hidden_ref[...] = hidden
    normed = (hidden * inverse_rms(hidden) * gain_ref[1:2]).astype(bf16)
    normed_ref[...] = normed
    logits = matmul(normed, extra_ref[...])
    lane = lax.broadcasted_iota(jnp.int32, logits.shape, 1)
    logits = jnp.where((lane >= 2) & (lane < 2 + experts), logits, MASKED)
    terms = jnp.exp(logits - jnp.max(logits, axis=1, keepdims=True))
    probs = terms / jnp.sum(terms, axis=1, keepdims=True)
    probs_ref[...] = probs
    gate = jnp.sum(probs * chosen_lane(expert_ref, probs.shape[1]), axis=1, keepdims=True)
    grad_expert = (gate * cot_ref[...].astype(f32)).astype(bf16)
    width = normed.shape[1]
    slots = slot_matrix(keys_ref, sent_ref.shape[0])
    sent_ref[:, :width] = matmul(slots, normed).astype(bf16)
    sent_ref[:, width:] = matmul(slots, grad_expert).astype(bf16)


def return_kernel(
    experts,
    place_ref,
    back_ref,
    w0_ref,
    w1_ref,
    w2_ref,
    w3_ref,
    hidden_ref,
    cot_ref,
    probs_ref,
    gain_ref,
    extra_ref,
    expert_ref,
    keys_ref,
    outputs_ref,
    grad_ref,
    pair_ref,
    logits_ref,
    gain_sum_ref,
):
    head_place = place_ref[0]
    width = hidden_ref.shape[1]
    cols = width // GROUPS
    back = matmul_tn(slot_matrix(keys_ref, back_ref.shape[0]), back_ref[...])
    expert_tok, grad_routed = back[:, :width], back[:, width:]
    hidden = hidden_ref[...]
    grad_out = cot_ref[...].astype(f32)
    probs = probs_ref[...]
    chosen = chosen_lane(expert_ref, probs.shape[1])
    gate = jnp.sum(probs * chosen, axis=1, keepdims=True)
    outputs_ref[...] = (hidden + gate * expert_tok).astype(bf16)
    grad_gate = jnp.sum(grad_out * expert_tok, axis=1, keepdims=True)
    grad_logits = (probs * (chosen - gate) * grad_gate).astype(bf16)
    logits_ref[...] = grad_logits
    grad_normed = grad_routed + matmul_t(grad_logits, extra_ref[...])
    scale = inverse_rms(hidden)
    gain_sum_ref[...] = jnp.sum(grad_normed * hidden * scale, axis=0, keepdims=True)
    grad_hidden = grad_out + norm_back(hidden, scale, grad_normed, gain_ref[1:2])
    grad_ref[...] = grad_hidden
    branch = grad_hidden.astype(bf16)
    grad_mixed = None
    for step, ref in enumerate((w0_ref, w1_ref, w2_ref, w3_ref)):
        block = branch[:, :cols]
        for spot in range(1, GROUPS):
            block = jnp.where(
                (head_place + GROUPS - step) % GROUPS == spot,
                branch[:, spot * cols : (spot + 1) * cols],
                block,
            )
        product = matmul_t(block, ref[...])
        grad_mixed = product if grad_mixed is None else grad_mixed + product
    for spot in range(GROUPS):
        lanes = slice(spot * cols, (spot + 1) * cols)
        pair_ref[spot, :, :cols] = grad_mixed[:, lanes].astype(bf16)
        pair_ref[spot, :, cols:] = branch[:, lanes]


def squeeze_kernel(rows_ref, mat0_ref, mat1_ref, first_ref, second_ref):
    rows = rows_ref[...]
    first_ref[...] = matmul(mat0_ref[...], rows).astype(bf16)
    second_ref[...] = matmul(mat1_ref[...], rows).astype(bf16)


def home_kernel(*refs):
    back_ref = refs[10]
    back = None
    for expert in range(2):
        own_ref, *others = refs[5 * expert : 5 * expert + 4]
        total = own_ref[...]
        for ref in others:
            total = total + ref[...].astype(f32)
        product = matmul_tn(refs[5 * expert + 4][...], total.astype(bf16))
        back = product if back is None else back + product
    back_ref[...] = back.astype(bf16)


def chip_kernel(part, own_ref, other_ref, *out_refs):
    for place, out_ref in enumerate(out_refs):
        rows = slice(place * part, (place + 1) * part)
        total = own_ref[rows].astype(f32) + other_ref[rows].astype(f32)
        out_ref[...] = total.astype(out_ref.dtype)


def expert_kernel(expert, blocks, part, width, *refs):
    row_refs = refs[:blocks]
    in_ref, out_ref = refs[blocks : blocks + 2]
    own_ref, away_ref, rows_ref, act_ref, pre_ref = refs[blocks + 2 :]
    for place, row_ref in enumerate(row_refs):
        rows_ref[pl.ds(place * part, part), :] = row_ref[...]
    before_act = matmul(rows_ref[:, :width], in_ref[expert])
    grad_act = matmul_t(rows_ref[:, width:], out_ref[expert])
    square = before_act * before_act
    inner = jnp.tanh(0.7978845608028654 * (before_act + 0.044715 * square * before_act))
    half = 0.5 * (1.0 + inner)
    act_ref[...] = (before_act * half).astype(bf16)
    slope = half + (0.5 * 0.7978845608028654) * before_act * (1.0 - inner * inner) * (
        1.0 + (3 * 0.044715) * square
    )
    pre_ref[...] = (grad_act * slope).astype(bf16)
    part_out = matmul(act_ref[...], out_ref[expert])
    part_back = matmul_t(pre_ref[...], in_ref[expert])
    half = own_ref.shape[0]
    for rows, part_ref in ((slice(half, None), away_ref), (slice(0, half), own_ref)):
        part_ref[:, :width] = part_out[rows].astype(bf16)
        part_ref[:, width:] = part_back[rows].astype(bf16)


def expert_grad_kernel(experts, width, *refs):
    in_ref, out_ref = refs[3 * experts :]
    for expert in range(experts):
        rows_ref, act_ref, pre_ref = refs[3 * expert : 3 * expert + 3]
        out_ref[expert] = matmul_tn(act_ref[...], rows_ref[:, width:])
        in_ref[expert] = matmul_tn(rows_ref[:, :width], pre_ref[...])


def weight_sums(sums_ref, one_ref, turned_ref, two_ref, spread_ref, logits_ref, *given):
    grad_qkv, products, gain_one, gain_two = given
    sums = jnp.concatenate(
        (matmul(one_ref[...], grad_qkv), matmul(turned_ref[...], products)), axis=1
    )
    rest = matmul(two_ref[...], logits_ref[...])
    lane = lax.broadcasted_iota(jnp.int32, rest.shape, 1)
    spread = spread_ref[...].astype(f32)
    for index, gain in ((0, gain_one), (1, gain_two)):
        gain = jnp.sum(spread * gain, axis=1, keepdims=True)
        rest = jnp.where(lane == index, gain, rest)
    rest = jnp.concatenate((rest, jnp.zeros_like(rest)), axis=1)
    rest = jnp.concatenate(
        [pltpu.roll(rest, 7 - row, 0) for row in range(sums.shape[1] // 128)], axis=1
    )
    spot = lax.broadcasted_iota(jnp.int32, sums.shape, 0) % 8
    sums_ref[...] = jnp.where(spot == 7, rest, sums).astype(bf16)


def tail_kernel(blocks, place_ref, *refs):
    dq_refs, kv_refs = refs[:blocks], refs[blocks : 2 * blocks]
    att_refs = refs[2 * blocks : 3 * blocks]
    mat_ref, rows_ref, pair_ref, gain_two_ref, logits_ref = refs[3 * blocks : 3 * blocks + 5]
    own_mats, away_mats = refs[3 * blocks + 5 : 3 * blocks + 9], refs[3 * blocks + 9 : 3 * blocks + 13]
    away_ref, own_ref = refs[3 * blocks + 13 : 3 * blocks + 15]
    part_refs = refs[3 * blocks + 15 :]
    head_place = place_ref[0]
    cols = dq_refs[0].shape[1]
    grad_q = dq_refs[0][...]
    for ref in dq_refs[1:]:
        grad_q = grad_q + ref[...]
    grad_kv = kv_refs[0][...]
    for ref in kv_refs[1:]:
        grad_kv = grad_kv + ref[...].astype(f32)
    grad_qkv = jnp.concatenate((grad_q.astype(bf16), grad_kv.astype(bf16)), axis=1)
    part = matmul_t(grad_qkv, mat_ref[...])
    rows = rows_ref[...].astype(f32)
    gain_one = jnp.sum(part * rows * inverse_rms(rows), axis=0, keepdims=True)
    part = part.astype(bf16).astype(f32).reshape(blocks, -1, part.shape[1])
    for step, part_ref in enumerate(part_refs):
        value = part[0]
        for spot in range(1, blocks):
            value = jnp.where((head_place + step) % blocks == spot, part[spot], value)
        part_ref[...] = value.astype(part_ref.dtype)
    branch = pair_ref[:, :, cols:].reshape(-1, cols)
    products = jnp.concatenate(
        [matmul_tn(ref[...].reshape(-1, cols), branch).astype(bf16) for ref in att_refs], axis=0
    )
    for sums_ref, mats in ((away_ref, away_mats), (own_ref, own_mats)):
        weight_sums(
            sums_ref, *mats, logits_ref, grad_qkv, products, gain_one, gain_two_ref[...]
        )


def sum_kernel(groups, sums_ref, mats_ref, rest_ref):
    rows = mats_ref.shape[1]
    cols = mats_ref.shape[2] // groups
    rest = None
    for head in range(groups):
        total = sums_ref[head].astype(f32)
        for place in range(head + groups, sums_ref.shape[0], groups):
            total = total + sums_ref[place].astype(f32)
        for mat in range(4):
            mats_ref[mat, :, head * cols : (head + 1) * cols] = total[
                :rows, mat * cols : (mat + 1) * cols
            ]
        rest = total[7:8] if rest is None else rest + total[7:8]
    rest_ref[...] = rest


def body(
    inputs,
    gain_attn,
    w_query,
    w_key,
    w_value,
    w_output,
    gain_ffn,
    router,
    expert_in,
    expert_out,
    expert_index,
    slot_index,
    segment_ids,
    cotangent,
):
    tok_rows, width = inputs.shape
    head_dim = width // HEADS
    factor = head_dim ** (-0.5)
    cols = width // GROUPS
    heads_here = HEADS // GROUPS
    experts_all = router.shape[1]
    rows_held = w_query.shape[0]
    local_experts = expert_in.shape[0]
    hidden = expert_in.shape[2]
    block_rows = GROUPS * tok_rows

    core = lax.axis_index("core")
    head_place = lax.axis_index("x")
    query_place = lax.axis_index("y")
    ring = jnp.arange(GROUPS, dtype=jnp.int32)

    def core_swap(values):
        return lax.ppermute(values, "core", [(0, 1), (1, 0)])

    def gathered(values, axis):
        return [values] + [shifted(values, axis, step) for step in range(1, GROUPS)]

    input_parts = gathered(inputs, "x")

    wide = width
    (packed,) = call_kernel(
        functools.partial(pack_kernel, GROUPS),
        (jax.ShapeDtypeStruct((64, 8, wide), bf16),),
        1,
        4,
        w_query,
        w_key,
        w_value,
        w_output,
        gain_attn[None, :],
        gain_ffn[None, :],
        router,
        segment_ids[None, :],
        whole=True,
    )
    held = swap_rows(packed, ("z", "y", "x"))
    held_other = core_swap(held)
    feature = jnp.arange(width, dtype=jnp.int32)

    def spread_slot(feature):
        owner = feature // rows_held
        return (owner // 32 * 16 + owner % 16) * 8 + feature % rows_held

    spread_row = jnp.where(feature // rows_held // 16 % 2 == core, 0, 512) + spread_slot(feature)
    place_row = jnp.arange(1024, dtype=jnp.int32)
    halves = (place_row[:512], place_row[512:])
    spread = [(rows[:, None] == spread_row[None, :]).astype(bf16) for rows in halves]
    pick = (spread_row[:, None] == place_row[None, :]).astype(bf16)
    segs = held.reshape(4, 16, 8, wide)[:, :, rows_held, :tok_rows]
    segs = lax.dynamic_index_in_dim(segs, lax.axis_index("z"), axis=0, keepdims=False)
    segs = segs.reshape(GROUPS, GROUPS, tok_rows)
    key_segs = jnp.take(segs, (query_place - ring) % GROUPS, axis=0)
    query_seg = key_segs[0].reshape(block_rows)
    key_segs = key_segs.reshape(GROUPS * block_rows)

    places = head_place.astype(jnp.int32)[None]
    qkv_mat, out_cols, extra, gains, block_inputs, normed_one, queries, kv_own = call_kernel(
        functools.partial(front_kernel, cols),
        (
            shape(width, 3 * cols, bf16),
            shape(width, cols, bf16),
            shape(width, 64, bf16),
            shape(8, width),
            shape(block_rows, width, bf16),
            shape(block_rows, width, bf16),
            shape(block_rows, cols, bf16),
            shape(block_rows, 2 * cols, bf16),
        ),
        4,
        12,
        pick,
        held,
        held_other,
        *input_parts,
        scalars=places,
        whole=True,
    )
    kv_blocks = gathered(kv_own, "y")
    out_parts = gathered(out_cols, "x")
    documents = jnp.arange(head_dim, dtype=bf16)[None, :]
    query_mask = (query_seg[:, None] == documents).astype(bf16)
    key_masks = jnp.where((key_segs[:, None] == documents) | (documents > 2), 0.0, MASKED)
    key_masks = key_masks.astype(bf16).reshape(GROUPS, block_rows, head_dim)
    key_masks = [key_masks[i] for i in range(GROUPS)]
    sizes = (heads_here, head_dim, factor)
    state = call_kernel(
        functools.partial(attend_kernel, True, False, 1, *sizes),
        (shape(cols, block_rows), shape(8, block_rows), shape(8, block_rows)),
        2,
        8,
        queries,
        query_mask,
        kv_own,
        key_masks[0],
    )
    state = call_kernel(
        functools.partial(attend_kernel, False, False, 2, *sizes),
        (shape(cols, block_rows), shape(8, block_rows), shape(8, block_rows)),
        4,
        8,
        queries,
        query_mask,
        kv_blocks[1],
        kv_blocks[3],
        key_masks[1],
        key_masks[3],
        *state,
    )
    attended, att_low, log_total = call_kernel(
        functools.partial(attend_kernel, False, True, 1, *sizes),
        (
            shape(cols, block_rows),
            jax.ShapeDtypeStruct((GROUPS, tok_rows, cols), bf16),
            shape(8, block_rows),
        ),
        2,
        8,
        queries,
        query_mask,
        kv_blocks[2],
        key_masks[2],
        *state,
    )
    mixed_parts = swap_rows(att_low, "x")
    expert_col = expert_index[:, None]
    slot_row = expert_index // local_experts * 16 + expert_index % local_experts * 8 + slot_index
    keys = slot_row[None, :]
    slots = 16 * 16
    sent, hidden_one, normed_two, router_probs = call_kernel(
        functools.partial(route_kernel, experts_all),
        (
            shape(slots, 2 * width, bf16),
            shape(tok_rows, width),
            shape(tok_rows, width, bf16),
            shape(tok_rows, 64),
        ),
        3,
        6,
        mixed_parts,
        *out_parts,
        inputs,
        cotangent,
        gains,
        extra,
        expert_col,
        keys,
        scalars=places,
    )

    turned_feature = (head_place - feature // cols) % GROUPS * cols + feature % cols
    turned_row = jnp.where(turned_feature // rows_held // 16 % 2 == core, 0, 512)
    turned_row = turned_row + spread_slot(turned_feature)
    shared = [
        (
            matmul_t(spread_half, normed_one).astype(bf16),
            (rows[:, None] == turned_row[None, :]).astype(bf16),
            matmul_t(spread_half, normed_two).astype(bf16),
            spread_half,
        )
        for spread_half, rows in zip(spread, halves)
    ]

    dev_rows = 16 * CAPACITY
    dense = jnp.arange(dev_rows, dtype=jnp.int32)
    squeeze = [
        (
            (dense // CAPACITY * 16 + expert * 8 + dense % CAPACITY)[:, None]
            == jnp.arange(slots, dtype=jnp.int32)[None, :]
        ).astype(bf16)
        for expert in range(local_experts)
    ]

    def seq_swap(values):
        values = values.reshape(16, slots // 16, 2 * width)
        return swap_rows(values, ("y", "x")).reshape(slots, 2 * width)

    half_block = shape(4 * dev_rows, 2 * width, bf16)
    all_rows = 8 * dev_rows
    act_shape = shape(all_rows, hidden, bf16)
    arrived = seq_swap(sent)
    arrived, att_low = lax.optimization_barrier((arrived, att_low))
    att_parts = gathered(att_low, "x")
    arrived = list(
        call_kernel(
            squeeze_kernel,
            (shape(dev_rows, 2 * width, bf16),) * local_experts,
            1,
            4,
            arrived,
            *squeeze,
        )
    )
    z_rows = [gathered(arrived[0], "z")]

    z_rows.append(gathered(arrived[1], "z"))
    z_rows[0], att_parts, shared = lax.optimization_barrier((z_rows[0], att_parts, shared))

    kept, totals = [], []
    for expert in range(local_experts):
        row_blocks = z_rows[expert] + [core_swap(rows) for rows in z_rows[expert]]
        own_parts, away_parts, *held_back = call_kernel(
            functools.partial(expert_kernel, expert, 8, dev_rows, width),
            (half_block, half_block, shape(all_rows, 2 * width, bf16), act_shape, act_shape),
            5,
            8,
            *row_blocks,
            expert_in,
            expert_out,
        )
        kept += held_back
        totals.append(
            call_kernel(
                functools.partial(chip_kernel, dev_rows),
                tuple(shape(dev_rows, 2 * width, bf16 if step else f32) for step in range(4)),
                1,
                4,
                own_parts,
                core_swap(away_parts),
            )
        )
    kept, totals = lax.optimization_barrier((kept, totals))
    home = []
    for sums, mat in zip(totals, squeeze):
        home.append(sums[0])
        for step in range(1, 4):
            home.append(shifted(sums[step], "z", 4 - step))
        home.append(mat)
    d_expert_in, d_expert_out = call_kernel(
        functools.partial(expert_grad_kernel, local_experts, width),
        (
            jax.ShapeDtypeStruct(expert_in.shape, f32),
            jax.ShapeDtypeStruct(expert_out.shape, f32),
        ),
        4,
        8,
        *kept,
    )
    (home,) = call_kernel(
        home_kernel,
        (shape(slots, 2 * width, bf16),),
        1,
        6,
        *home,
    )
    home, d_expert_in, d_expert_out = lax.optimization_barrier((home, d_expert_in, d_expert_out))
    back = seq_swap(home)

    outputs, grad_hidden, pair, grad_logits, d_gain_ffn = call_kernel(
        functools.partial(return_kernel, experts_all),
        (
            shape(tok_rows, width, bf16),
            shape(tok_rows, width),
            jax.ShapeDtypeStruct((GROUPS, tok_rows, 2 * cols), bf16),
            shape(tok_rows, 64, bf16),
            shape(1, width),
        ),
        3,
        6,
        back,
        *out_parts,
        hidden_one,
        cotangent,
        router_probs,
        gains,
        extra,
        expert_col,
        keys,
        scalars=places,
    )

    pair = swap_rows(pair, "x")
    dq_parts, kv_parts = [], []
    for step in (2, 1, 3, 0):
        dq, kv_part = call_kernel(
            functools.partial(attend_back_kernel, 1, *sizes),
            (shape(block_rows, cols), shape(block_rows, 2 * cols, bf16 if step else f32)),
            3,
            8,
            queries,
            query_mask,
            pair,
            attended,
            log_total,
            kv_blocks[step],
            key_masks[step],
        )
        dq_parts.append(dq)
        kv_parts.append(shifted(kv_part, "y", GROUPS - step) if step else kv_part)
    kv_parts = kv_parts[::-1]

    sums_shape = shape(512, wide, bf16)
    part_shape = shape(tok_rows, width, bf16)
    away_sums, own_sums, *normed_parts = call_kernel(
        functools.partial(tail_kernel, GROUPS),
        (sums_shape, sums_shape) + (part_shape,) * GROUPS,
        5,
        12,
        *dq_parts,
        *kv_parts,
        *att_parts,
        qkv_mat,
        block_inputs,
        pair,
        d_gain_ffn,
        grad_logits,
        *shared[0],
        *shared[1],
        scalars=places,
    )
    chip_sums = own_sums.astype(f32) + core_swap(away_sums).astype(f32)
    sums = swap_rows(chip_sums.astype(bf16).reshape(64, 8, wide), ("z", "y", "x"))
    grad_normed_one = normed_parts[0].astype(f32)
    for step in range(1, GROUPS):
        grad_normed_one = grad_normed_one + shifted(normed_parts[step], "x", step).astype(f32)
    mats, rest = call_kernel(
        functools.partial(sum_kernel, GROUPS),
        (
            jax.ShapeDtypeStruct((4, rows_held, width), f32),
            shape(1, wide),
        ),
        1,
        4,
        sums,
    )

    rest = rest.reshape(rows_held, wide // rows_held)
    inputs_f = inputs.astype(f32)
    d_inputs = grad_hidden + norm_back(
        inputs_f, inverse_rms(inputs_f), grad_normed_one, gains[0:1]
    )
    return (
        outputs,
        d_inputs,
        rest[:, 0],
        mats[0],
        mats[1],
        mats[2],
        mats[3],
        rest[:, 1],
        rest[:, 2 : 2 + experts_all],
        d_expert_in,
        d_expert_out,
    )


def solution(mesh):
    mesh = Mesh(mesh.devices.reshape(SIZES), ALL)
    dp = ("z", "core")
    seq = ("y", "x")
    rows = P(ALL, None)
    in_specs = (
        rows,
        P(ALL),
        rows,
        rows,
        rows,
        rows,
        P(ALL),
        rows,
        P(seq, None, dp),
        P(seq, dp, None),
        P(ALL),
        P(ALL),
        P(ALL),
        rows,
    )
    out_specs = (
        rows,
        rows,
        P(ALL),
        rows,
        rows,
        rows,
        rows,
        P(ALL),
        rows,
        P(seq, None, dp),
        P(seq, dp, None),
    )
    return jax.shard_map(body, mesh=mesh, in_specs=in_specs, out_specs=out_specs, check_vma=False)
```

```python
import functools

import jax
import jax.numpy as jnp
from jax import lax
from jax.experimental import pallas as pl
from jax.experimental.pallas import tpu as pltpu
from jax.sharding import Mesh
from jax.sharding import PartitionSpec as P

HEADS = 12
GROUPS = 4
CAPACITY = 5
EPSILON = 1e-06
ALL = ("z", "core", "y", "x")
SIZES = (4, 2, 4, 4)

f32 = jnp.float32
bf16 = jnp.bfloat16


def shifted(values, axis, step):
    return lax.ppermute(values, axis, [(i, (i + step) % 4) for i in range(4)])


def swap_rows(values, axes):
    return lax.all_to_all(values, axes, split_axis=0, concat_axis=0, tiled=True)


def matmul(a, b):
    return jnp.dot(a, b, preferred_element_type=f32)


def matmul_t(a, b):
    return lax.dot_general(a, b, (((1,), (1,)), ((), ())), preferred_element_type=f32)


def matmul_tn(a, b):
    return lax.dot_general(a, b, (((0,), (0,)), ((), ())), preferred_element_type=f32)


def inverse_rms(values):
    return lax.rsqrt(jnp.mean(values * values, axis=-1, keepdims=True) + EPSILON)


def norm_back(values, scale, grad, gain_vec):
    u = grad * gain_vec
    return scale * u - values * (scale * scale * scale) * jnp.mean(
        u * values, axis=-1, keepdims=True
    )

MASKED = -1e30
MIB = 1024 * 1024


def call_kernel(kernel, out_shapes, micros, scratch_mib, *operands, scalars=None, whole=False):
    moved = sum(v.size * v.dtype.itemsize for v in operands)
    moved += sum(v.size * v.dtype.itemsize for v in out_shapes)
    in_specs = [pl.BlockSpec(memory_space=pltpu.VMEM)] * len(operands)
    if scalars is not None:
        in_specs = [pl.BlockSpec(memory_space=pltpu.SMEM)] + in_specs
        operands = (scalars,) + operands
    return pl.pallas_call(
        kernel,
        out_shape=out_shapes,
        in_specs=in_specs,
        out_specs=[pl.BlockSpec(memory_space=pltpu.VMEM)] * len(out_shapes),
        compiler_params=pltpu.CompilerParams(
            vmem_limit_bytes=(58 if whole else moved * 4 // 3 // MIB + 2 + scratch_mib) * MIB
        ),
        cost_estimate=pl.CostEstimate(
            flops=int(micros * 1.1e9), bytes_accessed=moved, transcendentals=0
        ),
    )(*operands)


def shape(rows, columns, dtype=f32):
    return jax.ShapeDtypeStruct((rows, columns), dtype)


def transposed_scores(k_ref, kmask_ref, q_ref, qmask_ref, lanes, factor):
    key_side = jnp.concatenate((k_ref[:, lanes], kmask_ref[...]), axis=1)
    query_side = jnp.concatenate((q_ref[:, lanes] * factor, qmask_ref[...]), axis=1)
    return matmul_t(key_side, query_side)


def attend_kernel(first, last, blocks, heads, head_dim, factor, *refs):
    q_ref, qmask_ref = refs[:2]
    kv_refs = refs[2 : 2 + blocks]
    mask_refs = refs[2 + blocks : 2 + 2 * blocks]
    rest = refs[2 + 2 * blocks :]
    if not first:
        old_sum, old_top, old_total = rest[:3]
        rest = rest[3:]
    cols = heads * head_dim
    for head in range(heads):
        lanes = slice(head * head_dim, (head + 1) * head_dim)
        value_lanes = slice(cols + head * head_dim, cols + (head + 1) * head_dim)
        if first:
            top = total = accum = None
        else:
            top = old_top[head : head + 1, :]
            total = old_total[head : head + 1, :]
            accum = old_sum[lanes, :]
        for kv_ref, mask_ref in zip(kv_refs, mask_refs):
            scores = transposed_scores(kv_ref, mask_ref, q_ref, qmask_ref, lanes, factor)
            newest = jnp.max(scores, axis=0, keepdims=True)
            if top is not None:
                newest = jnp.maximum(top, newest)
            terms = jnp.exp(scores - newest)
            term_sum = jnp.sum(terms, axis=0, keepdims=True)
            product = matmul_tn(kv_ref[:, value_lanes], terms.astype(bf16))
            if top is None:
                total, accum = term_sum, product
            else:
                shrink = jnp.exp(top - newest)
                total = total * shrink + term_sum
                accum = accum * shrink + product
            top = newest
        if last:
            att_ref, low_ref, log_ref = rest
            accum = accum / total
            att_ref[lanes, :] = accum
            low_ref[:, :, lanes] = accum.T.astype(bf16).reshape(low_ref.shape[:2] + (head_dim,))
            log_ref[head : head + 1, :] = top + jnp.log(total)
        else:
            sum_ref, top_ref, total_ref = rest
            sum_ref[lanes, :] = accum
            top_ref[head : head + 1, :] = top
            total_ref[head : head + 1, :] = total


def attend_back_kernel(blocks, heads, head_dim, factor, *refs):
    q_ref, qmask_ref, grad_ref, att_ref, log_ref = refs[:5]
    kv_refs = refs[5 : 5 + blocks]
    mask_refs = refs[5 + blocks : 5 + 2 * blocks]
    dq_ref = refs[5 + 2 * blocks]
    out_refs = refs[6 + 2 * blocks :]
    cols = heads * head_dim
    for head in range(heads):
        lanes = slice(head * head_dim, (head + 1) * head_dim)
        value_lanes = slice(cols + head * head_dim, cols + (head + 1) * head_dim)
        grad = grad_ref[:, :, lanes].reshape(-1, head_dim)
        query = q_ref[:, lanes] * factor
        delta = jnp.sum(grad.astype(f32).T * att_ref[lanes, :], axis=0, keepdims=True)
        log_total = log_ref[head : head + 1, :]
        dq = None
        for kv_ref, mask_ref, out_ref in zip(kv_refs, mask_refs, out_refs):
            scores = transposed_scores(kv_ref, mask_ref, q_ref, qmask_ref, lanes, factor)
            probs = jnp.exp(scores - log_total)
            grad_probs = matmul_t(kv_ref[:, value_lanes], grad)
            grad_scores = (probs * (grad_probs - delta)).astype(bf16)
            out_ref[:, value_lanes] = matmul(probs.astype(bf16), grad).astype(out_ref.dtype)
            out_ref[:, lanes] = matmul(grad_scores, query).astype(out_ref.dtype)
            product = matmul_tn(kv_ref[:, lanes], grad_scores)
            dq = product if dq is None else dq + product
        dq_ref[:, lanes] = dq.T * factor


def pack_kernel(
    groups,
    query_ref,
    key_ref,
    value_ref,
    output_ref,
    gain_one_ref,
    gain_two_ref,
    router_ref,
    seg_ref,
    packed_ref,
):
    rows = query_ref.shape[0]
    cols = query_ref.shape[1] // groups
    wide = packed_ref.shape[2]
    across = lax.broadcasted_iota(jnp.int32, (rows, rows), 1)
    same = across == lax.broadcasted_iota(jnp.int32, (rows, rows), 0)

    def column(ref):
        return jnp.sum(jnp.where(same, ref[...].astype(f32), 0.0), axis=1, keepdims=True)

    extra = (column(gain_one_ref), column(gain_two_ref), router_ref[...].astype(f32))
    used = 2 + router_ref.shape[1]
    extra = jnp.concatenate(extra + (jnp.zeros((rows, 128 - used), f32),), axis=1)
    extra = jnp.concatenate([extra[row : row + 1] for row in range(rows)], axis=1)
    numbers = seg_ref[...].astype(f32)
    numbers = jnp.concatenate((numbers, jnp.zeros((1, wide - numbers.shape[1]), f32)), axis=1)
    for head in range(groups):
        lanes = slice(head * cols, (head + 1) * cols)
        mats = tuple(
            ref[:, lanes].astype(f32) for ref in (query_ref, key_ref, value_ref, output_ref)
        )
        block = jnp.concatenate((jnp.concatenate(mats, axis=1), numbers, extra), axis=0)
        block = block.astype(bf16)
        for place in range(head, packed_ref.shape[0], groups):
            packed_ref[place] = block


def front_kernel(
    cols,
    place_ref,
    pick_ref,
    held_ref,
    other_ref,
    r0_ref,
    r1_ref,
    r2_ref,
    r3_ref,
    mat_ref,
    out_ref,
    extra_ref,
    gain_ref,
    rows_ref,
    normed_ref,
    q_ref,
    kv_ref,
):
    head_place = place_ref[0]
    held = jnp.concatenate((held_ref[...], other_ref[...]), axis=0)
    held = held.reshape(-1, held.shape[2])
    weights = matmul(pick_ref[...], held).astype(bf16)
    mat = weights[:, : 3 * cols]
    mat_ref[...] = mat
    out_ref[...] = weights[:, 3 * cols :]
    count = held.shape[0]
    spot = lax.broadcasted_iota(jnp.int32, (count, 128), 0) % 8
    spare = jnp.zeros((count, 128), f32)
    for row in range(held.shape[1] // 128):
        piece = held[:, row * 128 : row * 128 + 128].astype(f32)
        spare = jnp.where(spot == row, pltpu.roll(piece, count + row - 7, 0), spare)
    extra = matmul(pick_ref[...], spare.astype(bf16)).astype(bf16)[:, :64]
    extra_ref[...] = extra
    gains = extra.astype(f32).T[:8]
    gain_ref[...] = gains
    part = r0_ref.shape[0]
    for step, ref in enumerate((r0_ref, r1_ref, r2_ref, r3_ref)):
        start = (head_place + GROUPS - step) % GROUPS * part
        rows_ref[pl.ds(pl.multiple_of(start, part), part), :] = ref[...]
    rows = rows_ref[...].astype(f32)
    normed = (rows * inverse_rms(rows) * gains[0:1]).astype(bf16)
    normed_ref[...] = normed
    qkv = matmul(normed, mat).astype(bf16)
    q_ref[...] = qkv[:, :cols]
    kv_ref[...] = qkv[:, cols:]


def chosen_lane(expert_ref, lanes):
    lane = lax.broadcasted_iota(jnp.int32, (expert_ref.shape[0], lanes), 1)
    return (lane == expert_ref[...] + 2).astype(f32)


def slot_matrix(keys_ref, slots):
    slot = lax.broadcasted_iota(jnp.int32, (slots, keys_ref.shape[1]), 0)
    return (slot == keys_ref[...]).astype(bf16)


def route_kernel(
    experts,
    place_ref,
    att_ref,
    w0_ref,
    w1_ref,
    w2_ref,
    w3_ref,
    in_ref,
    cot_ref,
    gain_ref,
    extra_ref,
    expert_ref,
    keys_ref,
    sent_ref,
    hidden_ref,
    normed_ref,
    probs_ref,
):
    head_place = place_ref[0]
    mixed = jnp.concatenate([att_ref[i] for i in range(GROUPS)], axis=1)
    pieces = [matmul(mixed, ref[...]) for ref in (w0_ref, w1_ref, w2_ref, w3_ref)]
    columns = []
    for spot in range(GROUPS):
        value = pieces[0]
        for step in range(1, GROUPS):
            value = jnp.where((head_place + GROUPS - step) % GROUPS == spot, pieces[step], value)
        columns.append(value)
    hidden = in_ref[...].astype(f32) + jnp.concatenate(columns, axis=1)
    hidden_ref[...] = hidden
    normed = (hidden * inverse_rms(hidden) * gain_ref[1:2]).astype(bf16)
    normed_ref[...] = normed
    logits = matmul(normed, extra_ref[...])
    lane = lax.broadcasted_iota(jnp.int32, logits.shape, 1)
    logits = jnp.where((lane >= 2) & (lane < 2 + experts), logits, MASKED)
    terms = jnp.exp(logits - jnp.max(logits, axis=1, keepdims=True))
    probs = terms / jnp.sum(terms, axis=1, keepdims=True)
    probs_ref[...] = probs
    gate = jnp.sum(probs * chosen_lane(expert_ref, probs.shape[1]), axis=1, keepdims=True)
    grad_expert = (gate * cot_ref[...].astype(f32)).astype(bf16)
    width = normed.shape[1]
    slots = slot_matrix(keys_ref, sent_ref.shape[0])
    sent_ref[:, :width] = matmul(slots, normed).astype(bf16)
    sent_ref[:, width:] = matmul(slots, grad_expert).astype(bf16)


def return_kernel(
    experts,
    place_ref,
    back_ref,
    w0_ref,
    w1_ref,
    w2_ref,
    w3_ref,
    hidden_ref,
    cot_ref,
    probs_ref,
    gain_ref,
    extra_ref,
    expert_ref,
    keys_ref,
    outputs_ref,
    grad_ref,
    pair_ref,
    logits_ref,
    gain_sum_ref,
):
    head_place = place_ref[0]
    width = hidden_ref.shape[1]
    cols = width // GROUPS
    back = matmul_tn(slot_matrix(keys_ref, back_ref.shape[0]), back_ref[...])
    expert_tok, grad_routed = back[:, :width], back[:, width:]
    hidden = hidden_ref[...]
    grad_out = cot_ref[...].astype(f32)
    probs = probs_ref[...]
    chosen = chosen_lane(expert_ref, probs.shape[1])
    gate = jnp.sum(probs * chosen, axis=1, keepdims=True)
    outputs_ref[...] = (hidden + gate * expert_tok).astype(bf16)
    grad_gate = jnp.sum(grad_out * expert_tok, axis=1, keepdims=True)
    grad_logits = (probs * (chosen - gate) * grad_gate).astype(bf16)
    logits_ref[...] = grad_logits
    grad_normed = grad_routed + matmul_t(grad_logits, extra_ref[...])
    scale = inverse_rms(hidden)
    gain_sum_ref[...] = jnp.sum(grad_normed * hidden * scale, axis=0, keepdims=True)
    grad_hidden = grad_out + norm_back(hidden, scale, grad_normed, gain_ref[1:2])
    grad_ref[...] = grad_hidden
    branch = grad_hidden.astype(bf16)
    grad_mixed = None
    for step, ref in enumerate((w0_ref, w1_ref, w2_ref, w3_ref)):
        block = branch[:, :cols]
        for spot in range(1, GROUPS):
            block = jnp.where(
                (head_place + GROUPS - step) % GROUPS == spot,
                branch[:, spot * cols : (spot + 1) * cols],
                block,
            )
        product = matmul_t(block, ref[...])
        grad_mixed = product if grad_mixed is None else grad_mixed + product
    for spot in range(GROUPS):
        lanes = slice(spot * cols, (spot + 1) * cols)
        pair_ref[spot, :, :cols] = grad_mixed[:, lanes].astype(bf16)
        pair_ref[spot, :, cols:] = branch[:, lanes]


def squeeze_kernel(rows_ref, mat0_ref, mat1_ref, first_ref, second_ref):
    rows = rows_ref[...]
    first_ref[...] = matmul(mat0_ref[...], rows).astype(bf16)
    second_ref[...] = matmul(mat1_ref[...], rows).astype(bf16)


def home_kernel(*refs):
    back_ref = refs[10]
    back = None
    for expert in range(2):
        own_ref, *others = refs[5 * expert : 5 * expert + 4]
        total = own_ref[...]
        for ref in others:
            total = total + ref[...].astype(f32)
        product = matmul_tn(refs[5 * expert + 4][...], total.astype(bf16))
        back = product if back is None else back + product
    back_ref[...] = back.astype(bf16)


def chip_kernel(part, own_ref, other_ref, *out_refs):
    for place, out_ref in enumerate(out_refs):
        rows = slice(place * part, (place + 1) * part)
        total = own_ref[rows].astype(f32) + other_ref[rows].astype(f32)
        out_ref[...] = total.astype(out_ref.dtype)


def expert_kernel(expert, blocks, part, width, *refs):
    row_refs = refs[:blocks]
    in_ref, out_ref = refs[blocks : blocks + 2]
    own_ref, away_ref, rows_ref, act_ref, pre_ref = refs[blocks + 2 :]
    for place, row_ref in enumerate(row_refs):
        rows_ref[pl.ds(place * part, part), :] = row_ref[...]
    before_act = matmul(rows_ref[:, :width], in_ref[expert])
    grad_act = matmul_t(rows_ref[:, width:], out_ref[expert])
    square = before_act * before_act
    inner = jnp.tanh(0.7978845608028654 * (before_act + 0.044715 * square * before_act))
    half = 0.5 * (1.0 + inner)
    act_ref[...] = (before_act * half).astype(bf16)
    slope = half + (0.5 * 0.7978845608028654) * before_act * (1.0 - inner * inner) * (
        1.0 + (3 * 0.044715) * square
    )
    pre_ref[...] = (grad_act * slope).astype(bf16)
    part_out = matmul(act_ref[...], out_ref[expert])
    part_back = matmul_t(pre_ref[...], in_ref[expert])
    half = own_ref.shape[0]
    for rows, part_ref in ((slice(half, None), away_ref), (slice(0, half), own_ref)):
        part_ref[:, :width] = part_out[rows].astype(bf16)
        part_ref[:, width:] = part_back[rows].astype(bf16)


def expert_grad_kernel(experts, width, *refs):
    in_ref, out_ref = refs[3 * experts :]
    for expert in range(experts):
        rows_ref, act_ref, pre_ref = refs[3 * expert : 3 * expert + 3]
        out_ref[expert] = matmul_tn(act_ref[...], rows_ref[:, width:])
        in_ref[expert] = matmul_tn(rows_ref[:, :width], pre_ref[...])


def weight_sums(sums_ref, one_ref, turned_ref, two_ref, spread_ref, logits_ref, *given):
    grad_qkv, products, gain_one, gain_two = given
    sums = jnp.concatenate(
        (matmul(one_ref[...], grad_qkv), matmul(turned_ref[...], products)), axis=1
    )
    rest = matmul(two_ref[...], logits_ref[...])
    lane = lax.broadcasted_iota(jnp.int32, rest.shape, 1)
    spread = spread_ref[...].astype(f32)
    for index, gain in ((0, gain_one), (1, gain_two)):
        gain = jnp.sum(spread * gain, axis=1, keepdims=True)
        rest = jnp.where(lane == index, gain, rest)
    rest = jnp.concatenate((rest, jnp.zeros_like(rest)), axis=1)
    rest = jnp.concatenate(
        [pltpu.roll(rest, 7 - row, 0) for row in range(sums.shape[1] // 128)], axis=1
    )
    spot = lax.broadcasted_iota(jnp.int32, sums.shape, 0) % 8
    sums_ref[...] = jnp.where(spot == 7, rest, sums).astype(bf16)


def tail_kernel(blocks, place_ref, *refs):
    dq_refs, kv_refs = refs[:blocks], refs[blocks : 2 * blocks]
    att_refs = refs[2 * blocks : 3 * blocks]
    mat_ref, rows_ref, pair_ref, gain_two_ref, logits_ref = refs[3 * blocks : 3 * blocks + 5]
    own_mats, away_mats = refs[3 * blocks + 5 : 3 * blocks + 9], refs[3 * blocks + 9 : 3 * blocks + 13]
    away_ref, own_ref = refs[3 * blocks + 13 : 3 * blocks + 15]
    part_refs = refs[3 * blocks + 15 :]
    head_place = place_ref[0]
    cols = dq_refs[0].shape[1]
    grad_q = dq_refs[0][...]
    for ref in dq_refs[1:]:
        grad_q = grad_q + ref[...]
    grad_kv = kv_refs[0][...]
    for ref in kv_refs[1:]:
        grad_kv = grad_kv + ref[...].astype(f32)
    grad_qkv = jnp.concatenate((grad_q.astype(bf16), grad_kv.astype(bf16)), axis=1)
    part = matmul_t(grad_qkv, mat_ref[...])
    rows = rows_ref[...].astype(f32)
    gain_one = jnp.sum(part * rows * inverse_rms(rows), axis=0, keepdims=True)
    part = part.astype(bf16).astype(f32).reshape(blocks, -1, part.shape[1])
    for step, part_ref in enumerate(part_refs):
        value = part[0]
        for spot in range(1, blocks):
            value = jnp.where((head_place + step) % blocks == spot, part[spot], value)
        part_ref[...] = value.astype(part_ref.dtype)
    branch = pair_ref[:, :, cols:].reshape(-1, cols)
    products = jnp.concatenate(
        [matmul_tn(ref[...].reshape(-1, cols), branch).astype(bf16) for ref in att_refs], axis=0
    )
    for sums_ref, mats in ((away_ref, away_mats), (own_ref, own_mats)):
        weight_sums(
            sums_ref, *mats, logits_ref, grad_qkv, products, gain_one, gain_two_ref[...]
        )


def sum_kernel(groups, sums_ref, mats_ref, rest_ref):
    rows = mats_ref.shape[1]
    cols = mats_ref.shape[2] // groups
    rest = None
    for head in range(groups):
        total = sums_ref[head].astype(f32)
        for place in range(head + groups, sums_ref.shape[0], groups):
            total = total + sums_ref[place].astype(f32)
        for mat in range(4):
            mats_ref[mat, :, head * cols : (head + 1) * cols] = total[
                :rows, mat * cols : (mat + 1) * cols
            ]
        rest = total[7:8] if rest is None else rest + total[7:8]
    rest_ref[...] = rest


def body(
    inputs,
    gain_attn,
    w_query,
    w_key,
    w_value,
    w_output,
    gain_ffn,
    router,
    expert_in,
    expert_out,
    expert_index,
    slot_index,
    segment_ids,
    cotangent,
):
    tok_rows, width = inputs.shape
    head_dim = width // HEADS
    factor = head_dim ** (-0.5)
    cols = width // GROUPS
    heads_here = HEADS // GROUPS
    experts_all = router.shape[1]
    rows_held = w_query.shape[0]
    local_experts = expert_in.shape[0]
    hidden = expert_in.shape[2]
    block_rows = GROUPS * tok_rows

    core = lax.axis_index("core")
    head_place = lax.axis_index("x")
    query_place = lax.axis_index("y")
    ring = jnp.arange(GROUPS, dtype=jnp.int32)

    def core_swap(values):
        return lax.ppermute(values, "core", [(0, 1), (1, 0)])

    def gathered(values, axis):
        return [values] + [shifted(values, axis, step) for step in range(1, GROUPS)]

    input_parts = gathered(inputs, "x")

    wide = width
    (packed,) = call_kernel(
        functools.partial(pack_kernel, GROUPS),
        (jax.ShapeDtypeStruct((64, 8, wide), bf16),),
        1,
        4,
        w_query,
        w_key,
        w_value,
        w_output,
        gain_attn[None, :],
        gain_ffn[None, :],
        router,
        segment_ids[None, :],
        whole=True,
    )
    held = swap_rows(packed, ("z", "y", "x"))
    held_other = core_swap(held)
    feature = jnp.arange(width, dtype=jnp.int32)

    def spread_slot(feature):
        owner = feature // rows_held
        return (owner // 32 * 16 + owner % 16) * 8 + feature % rows_held

    spread_row = jnp.where(feature // rows_held // 16 % 2 == core, 0, 512) + spread_slot(feature)
    place_row = jnp.arange(1024, dtype=jnp.int32)
    halves = (place_row[:512], place_row[512:])
    spread = [(rows[:, None] == spread_row[None, :]).astype(bf16) for rows in halves]
    pick = (spread_row[:, None] == place_row[None, :]).astype(bf16)
    segs = held.reshape(4, 16, 8, wide)[:, :, rows_held, :tok_rows]
    segs = lax.dynamic_index_in_dim(segs, lax.axis_index("z"), axis=0, keepdims=False)
    segs = segs.reshape(GROUPS, GROUPS, tok_rows)
    key_segs = jnp.take(segs, (query_place - ring) % GROUPS, axis=0)
    query_seg = key_segs[0].reshape(block_rows)
    key_segs = key_segs.reshape(GROUPS * block_rows)

    places = head_place.astype(jnp.int32)[None]
    qkv_mat, out_cols, extra, gains, block_inputs, normed_one, queries, kv_own = call_kernel(
        functools.partial(front_kernel, cols),
        (
            shape(width, 3 * cols, bf16),
            shape(width, cols, bf16),
            shape(width, 64, bf16),
            shape(8, width),
            shape(block_rows, width, bf16),
            shape(block_rows, width, bf16),
            shape(block_rows, cols, bf16),
            shape(block_rows, 2 * cols, bf16),
        ),
        4,
        12,
        pick,
        held,
        held_other,
        *input_parts,
        scalars=places,
        whole=True,
    )
    kv_blocks = gathered(kv_own, "y")
    out_parts = gathered(out_cols, "x")
    documents = jnp.arange(head_dim, dtype=bf16)[None, :]
    query_mask = (query_seg[:, None] == documents).astype(bf16)
    key_masks = jnp.where((key_segs[:, None] == documents) | (documents > 2), 0.0, MASKED)
    key_masks = key_masks.astype(bf16).reshape(GROUPS, block_rows, head_dim)
    key_masks = [key_masks[i] for i in range(GROUPS)]
    sizes = (heads_here, head_dim, factor)
    state = call_kernel(
        functools.partial(attend_kernel, True, False, 1, *sizes),
        (shape(cols, block_rows), shape(8, block_rows), shape(8, block_rows)),
        2,
        8,
        queries,
        query_mask,
        kv_own,
        key_masks[0],
    )
    state = call_kernel(
        functools.partial(attend_kernel, False, False, 2, *sizes),
        (shape(cols, block_rows), shape(8, block_rows), shape(8, block_rows)),
        4,
        8,
        queries,
        query_mask,
        kv_blocks[1],
        kv_blocks[3],
        key_masks[1],
        key_masks[3],
        *state,
    )
    attended, att_low, log_total = call_kernel(
        functools.partial(attend_kernel, False, True, 1, *sizes),
        (
            shape(cols, block_rows),
            jax.ShapeDtypeStruct((GROUPS, tok_rows, cols), bf16),
            shape(8, block_rows),
        ),
        2,
        8,
        queries,
        query_mask,
        kv_blocks[2],
        key_masks[2],
        *state,
    )
    mixed_parts = swap_rows(att_low, "x")
    expert_col = expert_index[:, None]
    slot_row = expert_index // local_experts * 16 + expert_index % local_experts * 8 + slot_index
    keys = slot_row[None, :]
    slots = 16 * 16
    sent, hidden_one, normed_two, router_probs = call_kernel(
        functools.partial(route_kernel, experts_all),
        (
            shape(slots, 2 * width, bf16),
            shape(tok_rows, width),
            shape(tok_rows, width, bf16),
            shape(tok_rows, 64),
        ),
        3,
        6,
        mixed_parts,
        *out_parts,
        inputs,
        cotangent,
        gains,
        extra,
        expert_col,
        keys,
        scalars=places,
    )

    turned_feature = (head_place - feature // cols) % GROUPS * cols + feature % cols
    turned_row = jnp.where(turned_feature // rows_held // 16 % 2 == core, 0, 512)
    turned_row = turned_row + spread_slot(turned_feature)
    shared = [
        (
            matmul_t(spread_half, normed_one).astype(bf16),
            (rows[:, None] == turned_row[None, :]).astype(bf16),
            matmul_t(spread_half, normed_two).astype(bf16),
            spread_half,
        )
        for spread_half, rows in zip(spread, halves)
    ]

    dev_rows = 16 * CAPACITY
    dense = jnp.arange(dev_rows, dtype=jnp.int32)
    squeeze = [
        (
            (dense // CAPACITY * 16 + expert * 8 + dense % CAPACITY)[:, None]
            == jnp.arange(slots, dtype=jnp.int32)[None, :]
        ).astype(bf16)
        for expert in range(local_experts)
    ]

    def seq_swap(values):
        values = values.reshape(16, slots // 16, 2 * width)
        return swap_rows(values, ("y", "x")).reshape(slots, 2 * width)

    half_block = shape(4 * dev_rows, 2 * width, bf16)
    all_rows = 8 * dev_rows
    act_shape = shape(all_rows, hidden, bf16)
    arrived = seq_swap(sent)
    arrived, att_low = lax.optimization_barrier((arrived, att_low))
    att_parts = gathered(att_low, "x")
    arrived = list(
        call_kernel(
            squeeze_kernel,
            (shape(dev_rows, 2 * width, bf16),) * local_experts,
            1,
            4,
            arrived,
            *squeeze,
        )
    )
    z_rows = [gathered(arrived[0], "z")]

    z_rows.append(gathered(arrived[1], "z"))
    z_rows[0], att_parts, shared = lax.optimization_barrier((z_rows[0], att_parts, shared))

    kept, totals = [], []
    for expert in range(local_experts):
        row_blocks = z_rows[expert] + [core_swap(rows) for rows in z_rows[expert]]
        own_parts, away_parts, *held_back = call_kernel(
            functools.partial(expert_kernel, expert, 8, dev_rows, width),
            (half_block, half_block, shape(all_rows, 2 * width, bf16), act_shape, act_shape),
            5,
            8,
            *row_blocks,
            expert_in,
            expert_out,
        )
        kept += held_back
        totals.append(
            call_kernel(
                functools.partial(chip_kernel, dev_rows),
                tuple(shape(dev_rows, 2 * width, bf16 if step else f32) for step in range(4)),
                1,
                4,
                own_parts,
                core_swap(away_parts),
            )
        )
    kept, totals = lax.optimization_barrier((kept, totals))
    home = []
    for sums, mat in zip(totals, squeeze):
        home.append(sums[0])
        for step in range(1, 4):
            home.append(shifted(sums[step], "z", 4 - step))
        home.append(mat)
    d_expert_in, d_expert_out = call_kernel(
        functools.partial(expert_grad_kernel, local_experts, width),
        (
            jax.ShapeDtypeStruct(expert_in.shape, f32),
            jax.ShapeDtypeStruct(expert_out.shape, f32),
        ),
        4,
        8,
        *kept,
    )
    (home,) = call_kernel(
        home_kernel,
        (shape(slots, 2 * width, bf16),),
        1,
        6,
        *home,
    )
    home, d_expert_in, d_expert_out = lax.optimization_barrier((home, d_expert_in, d_expert_out))
    back = seq_swap(home)

    outputs, grad_hidden, pair, grad_logits, d_gain_ffn = call_kernel(
        functools.partial(return_kernel, experts_all),
        (
            shape(tok_rows, width, bf16),
            shape(tok_rows, width),
            jax.ShapeDtypeStruct((GROUPS, tok_rows, 2 * cols), bf16),
            shape(tok_rows, 64, bf16),
            shape(1, width),
        ),
        3,
        6,
        back,
        *out_parts,
        hidden_one,
        cotangent,
        router_probs,
        gains,
        extra,
        expert_col,
        keys,
        scalars=places,
    )

    pair = swap_rows(pair, "x")
    dq_parts, kv_parts = [], []
    for step in (2, 1, 3, 0):
        dq, kv_part = call_kernel(
            functools.partial(attend_back_kernel, 1, *sizes),
            (shape(block_rows, cols), shape(block_rows, 2 * cols, bf16 if step else f32)),
            3,
            8,
            queries,
            query_mask,
            pair,
            attended,
            log_total,
            kv_blocks[step],
            key_masks[step],
        )
        dq_parts.append(dq)
        kv_parts.append(shifted(kv_part, "y", GROUPS - step) if step else kv_part)
    kv_parts = kv_parts[::-1]

    sums_shape = shape(512, wide, bf16)
    part_shape = shape(tok_rows, width, bf16)
    away_sums, own_sums, *normed_parts = call_kernel(
        functools.partial(tail_kernel, GROUPS),
        (sums_shape, sums_shape) + (part_shape,) * GROUPS,
        5,
        12,
        *dq_parts,
        *kv_parts,
        *att_parts,
        qkv_mat,
        block_inputs,
        pair,
        d_gain_ffn,
        grad_logits,
        *shared[0],
        *shared[1],
        scalars=places,
    )
    (chip_sums,) = call_kernel(
        functools.partial(chip_kernel, own_sums.shape[0]),
        (sums_shape,),
        1,
        4,
        own_sums,
        core_swap(away_sums),
    )
    sums = swap_rows(chip_sums.reshape(64, 8, wide), ("z", "y", "x"))
    grad_normed_one = normed_parts[0].astype(f32)
    for step in range(1, GROUPS):
        grad_normed_one = grad_normed_one + shifted(normed_parts[step], "x", step).astype(f32)
    mats, rest = call_kernel(
        functools.partial(sum_kernel, GROUPS),
        (
            jax.ShapeDtypeStruct((4, rows_held, width), f32),
            shape(1, wide),
        ),
        1,
        4,
        sums,
    )

    rest = rest.reshape(rows_held, wide // rows_held)
    inputs_f = inputs.astype(f32)
    d_inputs = grad_hidden + norm_back(
        inputs_f, inverse_rms(inputs_f), grad_normed_one, gains[0:1]
    )
    return (
        outputs,
        d_inputs,
        rest[:, 0],
        mats[0],
        mats[1],
        mats[2],
        mats[3],
        rest[:, 1],
        rest[:, 2 : 2 + experts_all],
        d_expert_in,
        d_expert_out,
    )


def solution(mesh):
    mesh = Mesh(mesh.devices.reshape(SIZES), ALL)
    dp = ("z", "core")
    seq = ("y", "x")
    rows = P(ALL, None)
    in_specs = (
        rows,
        P(ALL),
        rows,
        rows,
        rows,
        rows,
        P(ALL),
        rows,
        P(seq, None, dp),
        P(seq, dp, None),
        P(ALL),
        P(ALL),
        P(ALL),
        rows,
    )
    out_specs = (
        rows,
        rows,
        P(ALL),
        rows,
        rows,
        rows,
        rows,
        P(ALL),
        rows,
        P(seq, None, dp),
        P(seq, dp, None),
    )
    return jax.shard_map(body, mesh=mesh, in_specs=in_specs, out_specs=out_specs, check_vma=False)
```
